32 devices in a mesh: pipe: 2 (over x), expert: 16 (over z, y, core).
Axes of the slice: x: 2, y: 2, z: 4, core: 2. Of those that a mesh axis runs over, the one named last changes fastest.
Arguments:
- tokens: bfloat16 [2, 128, 3584], P(None, ('pipe', 'expert')), may hold values from -6 to 6
- cotangent: bfloat16 [2, 128, 3584], P(None, ('pipe', 'expert')), may hold values from -6 to 6
- expert_ids: int32 [2, 128, 2], P(None, ('pipe', 'expert')), may hold values from 0 to 3, all different within a row; in each aligned block of 4 rows (0 to 3, 4 to 7, ..., all dimensions but the last counted through in order) at most 3 rows name the same one
- gate_values: bfloat16 [2, 128, 2], P(None, ('pipe', 'expert')), may hold values from 0.19921875 to 1.5
- w_gate: bfloat16 [3584, 8192], P('pipe', 'expert'), may hold values from -0.09375 to 0.09375
- w_up: bfloat16 [3584, 8192], P('pipe', 'expert'), may hold values from -0.09375 to 0.09375
- w_down_t: bfloat16 [3584, 8192], P('pipe', 'expert'), may hold values from -0.125 to 0.125
Outputs:
- d_tokens: bfloat16 [2, 128, 3584], P(None, ('pipe', 'expert'))
- gate_weight_gradient: float32 [2, 128, 2], P(None, ('pipe', 'expert'))
- dw_gate: bfloat16 [3584, 8192], P('pipe', 'expert')
- dw_up: bfloat16 [3584, 8192], P('pipe', 'expert')
- dw_down_t: bfloat16 [3584, 8192], P('pipe', 'expert')
The draws below stay inside these ranges and needn't reach their ends.
Inputs may be any that keep to these rules, and one draw needn't show every extreme that they name: `expert_ids`: within each micro-batch, the 4 tokens of one device route to one expert at most 3 times; a token's 2 experts differ.
All inputs are finite; a program needn't handle non-finite values.
Results may differ from the reference program's by a relative error of at most 0.014.
Values may be sent and summed in bfloat16 or wider, within the bound.
No kernel may reach another device: no remote copies, remote signals or barrier semaphores. Data moves between devices by JAX's collectives and lax.ppermute only.
A program may use at most 64 MiB of HBM per device.

```python
import math
import jax
import jax.numpy as jnp
import numpy as np
from jax import lax

D = 3584
F = 2048
EXPERTS = 4
TOP = 2
MB = 2
TOK_MB = 4
CAP = 3
TOKENS = 128
N_PIPE = 2
N_EXPERT = 16


def shard_levels(key, extent, pieces, low, top_value):
    level, own = 1.0, jax.random.fold_in(key, 6)
    for axis_at, shards_of in pieces:
        draws = jnp.exp(jax.random.uniform(jax.random.fold_in(own, axis_at), (shards_of,), jnp.float32, low / len(pieces), top_value / len(pieces)))
        level = level * jnp.repeat(draws, extent[axis_at] // shards_of).reshape([-1 if axis == axis_at else 1 for axis in range(len(extent))])
    return level


def assign_block(key, own, number, rows, count, top, reach, lean):
    ranking = jax.random.permutation(key, count)
    heavy_load, ordinary = shares(count, rows * top, reach, lean, True), shares(count, rows * top, reach, lean, False)
    places = jnp.arange(count)

    def named(sizes, turn):
        used = int((sizes > 0).sum())
        fixed = max(1, used // 4)
        passed = fixed + (places - fixed + turn * (used - fixed)) % max(1, count - fixed)
        return jnp.zeros((count,), jnp.int32).at[ranking[jnp.where(places < fixed, places, passed)]].set(jnp.asarray(sizes, jnp.int32))

    sizes = jnp.where(number % 4 == 0, named(heavy_load, number // 4), named(ordinary, number - number // 4 - 1))
    mixed = jax.random.permutation(jax.random.fold_in(own, 3), count)
    donor, sink = mixed[0:count // 2 * 2:2], mixed[1:count // 2 * 2:2]
    room = jnp.minimum(sizes[donor] - 1, reach - sizes[sink]) // 2
    room = jnp.where((donor == ranking[0]) | (sink == ranking[0]) | (sizes[sink] == 0), 0, jnp.maximum(room, 0))
    passed = jax.random.randint(jax.random.fold_in(own, 4), (count // 2,), 0, 1 << 20) % (room + 1)
    sizes = sizes.at[donor].add(-passed).at[sink].add(passed)
    items = jnp.searchsorted(jnp.cumsum(sizes), jnp.arange(rows * top), side="right").astype(jnp.int32)
    listing = items.reshape(top, rows).T
    listing = listing[jax.random.permutation(jax.random.fold_in(own, 1), rows)]
    turn = jax.random.randint(jax.random.fold_in(own, 2), (rows, 1), 0, top)
    return jnp.take_along_axis(listing, (jnp.arange(top)[None, :] + turn) % top, axis=1)


def shares(number_of, total, reach, lean, full):
    loads = [(1 << 20) // math.isqrt(rank ** lean) + 1 for rank in range(1, number_of + 1)]
    largest = reach if full else min(reach, max(-(-total // number_of), total * loads[0] // sum(loads)))
    least = 1 if total - largest >= number_of - 1 else 0
    holding, rest = [largest] + [least] * (number_of - 1), total - largest - least * (number_of - 1)
    while rest > 0:
        candidates = [i for i in range(1, number_of) if holding[i] < largest] or [i for i in range(1, number_of) if holding[i] < reach]
        pool, left = sum([loads[i] for i in candidates]), rest
        for i in candidates:
            addition = min(reach - holding[i], max(1, left * loads[i] // pool), rest)
            holding[i] = holding[i] + addition
            rest = rest - addition
    return np.array(holding)


def gaussian(key, dims, width, most, cuts=(), kind=jnp.bfloat16):
    drawn = width * jax.random.normal(key, dims, jnp.float32)
    if cuts:
        drawn = drawn * shard_levels(key, dims, cuts, -0.22, 0.18)
    return jnp.clip(drawn, -most, most).astype(kind)


def setup_inputs(seed: int = 0) -> dict:
    keys = jax.random.split(jax.random.key(seed), 8)
    tokens = gaussian(keys[0], (MB, TOKENS, D), 1.0, 6.0, ((1, 32),))
    cotangent = gaussian(keys[1], (MB, TOKENS, D), 1.0, 6.0, ((1, 32),))
    expert_ids_keys = jax.random.split(jax.random.fold_in(keys[2], 1), MB * TOKENS // TOK_MB)
    expert_ids_turns = jax.random.permutation(jax.random.fold_in(keys[2], 3), MB * TOKENS // TOK_MB)
    expert_ids = jax.vmap(lambda own, number: assign_block(jax.random.fold_in(keys[2], 2), own, number, TOK_MB, EXPERTS, TOP, CAP, 2))(expert_ids_keys, expert_ids_turns).reshape((MB, TOKENS, TOP))
    gate_values = jnp.clip(0.19921875 + 1.3007812 * jax.random.uniform(keys[3], (MB, TOKENS, TOP), jnp.float32) ** shard_levels(keys[3], (MB, TOKENS, TOP), ((1, 32),), -0.2, 0.2), 0.19921875, 1.5).astype(jnp.bfloat16)
    w_gate = gaussian(keys[4], (D, EXPERTS * F), D ** -0.5, 0.09375, ((0, 2), (1, 16)))
    w_up = gaussian(keys[5], (D, EXPERTS * F), D ** -0.5, 0.09375, ((0, 2), (1, 16)))
    w_down_t = gaussian(keys[6], (D, EXPERTS * F), F ** -0.5, 0.125, ((0, 2), (1, 16)))
    return {"tokens": tokens, "cotangent": cotangent, "expert_ids": expert_ids, "gate_values": gate_values, "w_gate": w_gate, "w_up": w_up, "w_down_t": w_down_t}


def reference(tokens, cotangent, expert_ids, gate_values, w_gate, w_up, w_down_t):
    devices = N_PIPE * N_EXPERT
    routes = TOK_MB * TOP
    ids = expert_ids.reshape(MB, devices, routes).astype(jnp.int32)
    onehot = (ids[..., None] == jnp.arange(EXPERTS, dtype=jnp.int32)).astype(jnp.int32)
    earlier = jnp.cumsum(onehot, axis=2) - onehot
    position = lax.optimization_barrier(jnp.sum(earlier * onehot, axis=3)).astype(jnp.int32)
    micro_index = jnp.broadcast_to(jnp.arange(MB, dtype=jnp.int32)[:, None, None], ids.shape)
    device_index = jnp.broadcast_to(jnp.arange(devices, dtype=jnp.int32)[None, :, None], ids.shape)
    route_index = jnp.broadcast_to(jnp.arange(routes, dtype=jnp.int32)[None, None, :], ids.shape)
    token_flat = micro_index * TOKENS + device_index * TOK_MB + route_index // TOP
    route_flat = token_flat * TOP + route_index % TOP
    empty_slots = jnp.full((MB, devices, EXPERTS, CAP), -1, jnp.int32)
    token_slot = empty_slots.at[micro_index, device_index, ids, position].set(token_flat)
    route_slot = empty_slots.at[micro_index, device_index, ids, position].set(route_flat)
    tok_flat = tokens.reshape(MB * TOKENS, D)
    cot_flat = cotangent.reshape(MB * TOKENS, D)
    flattened_gate = gate_values.reshape(MB * TOKENS * TOP)
    scale = 1.0 / math.sqrt(MB * TOKENS * TOP / EXPERTS)
    highest_precision = lax.Precision.HIGHEST

    def pipe_sum(left_rows, right_rows):
        left_part = left_rows.reshape(MB, N_PIPE, N_EXPERT * CAP, D).astype(jnp.float32)
        right_part = right_rows.reshape(MB, N_PIPE, N_EXPERT * CAP, F).astype(jnp.float32)
        term = jnp.einsum('mprd,mprf->pdf', left_part, right_part, precision=highest_precision) * scale
        return lax.optimization_barrier(jnp.sum(term.astype(jnp.bfloat16).astype(jnp.float32), axis=0)).astype(jnp.bfloat16)

    def one_expert(carry, expert):
        dx_acc, gate_acc = carry
        tok_slot_e = jnp.take(token_slot, expert, axis=2).reshape(-1)
        route_slot_e = jnp.take(route_slot, expert, axis=2).reshape(-1)
        live = tok_slot_e >= 0
        safe_tok = jnp.where(live, tok_slot_e, 0).astype(jnp.int32)
        safe_route = jnp.where(live, route_slot_e, 0).astype(jnp.int32)
        live_bf = live.astype(jnp.bfloat16)[:, None]
        tok_rows = tok_flat[safe_tok] * live_bf
        cot_rows = cot_flat[safe_tok] * live_bf
        gate_rows = (flattened_gate[safe_route] * live_bf[:, 0]).astype(jnp.float32)[:, None]
        start = (expert * F).astype(jnp.int32)
        gate_cols = lax.dynamic_slice_in_dim(w_gate, start, F, 1)
        up_cols = lax.dynamic_slice_in_dim(w_up, start, F, 1)
        down_cols = lax.dynamic_slice_in_dim(w_down_t, start, F, 1)
        pre_gate = jnp.dot(tok_rows, gate_cols, preferred_element_type=jnp.float32)
        pre_up = jnp.dot(tok_rows, up_cols, preferred_element_type=jnp.float32)
        back_proj = jnp.dot(cot_rows, down_cols, preferred_element_type=jnp.float32)
        sigmoid_gate = jax.nn.sigmoid(pre_gate)
        activated = pre_gate * sigmoid_gate
        hidden = activated * pre_up
        gate_part = lax.optimization_barrier(jnp.sum(back_proj * hidden, axis=1))
        scaled_hidden = (gate_rows * hidden).astype(jnp.bfloat16)
        d_hidden = gate_rows * back_proj
        d_pre_gate = (d_hidden * pre_up * sigmoid_gate * (1.0 + pre_gate * (1.0 - sigmoid_gate))).astype(jnp.bfloat16)
        d_pre_up = (d_hidden * activated).astype(jnp.bfloat16)
        input_grad = jnp.dot(d_pre_gate, gate_cols.T, preferred_element_type=jnp.float32)
        input_grad = input_grad + jnp.dot(d_pre_up, up_cols.T, preferred_element_type=jnp.float32)
        dx_acc = dx_acc.at[safe_tok].add(input_grad)
        gate_acc = gate_acc.at[safe_route].add(gate_part)
        grad_gate = pipe_sum(tok_rows, d_pre_gate)
        grad_up = pipe_sum(tok_rows, d_pre_up)
        grad_down = pipe_sum(cot_rows, scaled_hidden)
        return ((dx_acc, gate_acc), (grad_gate, grad_up, grad_down))
    init = (jnp.zeros((MB * TOKENS, D), jnp.float32), jnp.zeros((MB * TOKENS * TOP,), jnp.float32))
    (dx_acc, gate_acc), grads = lax.scan(one_expert, init, jnp.arange(EXPERTS, dtype=jnp.int32))

    def columns(stacked):
        return jnp.transpose(stacked, (1, 0, 2)).reshape(D, EXPERTS * F)
    d_tokens = dx_acc.reshape(MB, TOKENS, D).astype(jnp.bfloat16)
    gate_weight_gradient = gate_acc.reshape(MB, TOKENS, TOP)
    return (d_tokens, gate_weight_gradient, columns(grads[0]), columns(grads[1]), columns(grads[2]))
```

```python
import functools
import math

import jax
import jax.numpy as jnp
from jax import lax
from jax.experimental import pallas as pl
from jax.experimental.pallas import tpu as pltpu
from jax.sharding import PartitionSpec as P

EXPERTS = 4
CAP = 3
LANES = 128
VMEM_LIMIT = 48 * 1024 * 1024
f32, bf16 = jnp.float32, jnp.bfloat16


def swap(x, axis, bit):
    return lax.ppermute(x, axis, [(i, i ^ bit) for i in range(lax.axis_size(axis))])


def compact_kernel(tok_count, me_ref, rows_ref, slots_ref, place_ref):
    row_count = rows_ref.shape[0]
    slot_count = slots_ref.shape[0]
    width = rows_ref.shape[1] - LANES
    me = me_ref[0].astype(f32)
    extras = rows_ref[:, width:].astype(f32)
    first, second = extras[:, 0:1] == me, extras[:, 1:2] == me
    gate = jnp.where(first, extras[:, 2:3], 0.0) + jnp.where(second, extras[:, 3:4], 0.0)
    routed = jnp.where(first | second, 1.0, 0.0)
    row = lax.broadcasted_iota(jnp.int32, (row_count, row_count), 0)
    other = lax.broadcasted_iota(jnp.int32, (row_count, row_count), 1)
    earlier = ((other < row) & (other // tok_count == row // tok_count)).astype(bf16)
    position = jnp.dot(
        earlier, jnp.broadcast_to(routed, (row_count, LANES)).astype(bf16), preferred_element_type=f32
    )[:, 0:1]
    block = lax.broadcasted_iota(jnp.int32, (row_count, 1), 0) // tok_count
    slot = block.astype(f32) * CAP + position
    lane = lax.broadcasted_iota(jnp.int32, (row_count, slot_count), 1).astype(f32)
    place = jnp.where((lane == slot) & (routed > 0.0), 1.0, 0.0).astype(bf16)
    place_ref[...] = place
    contract = (((0,), (0,)), ((), ()))
    slots_ref[:, :width] = lax.dot_general(
        place, rows_ref[:, :width], contract, preferred_element_type=f32
    ).astype(bf16)
    slots_ref[:, width:] = lax.dot_general(
        place,
        jnp.broadcast_to(gate, (row_count, LANES)).astype(bf16),
        contract,
        preferred_element_type=f32,
    ).astype(bf16)


def hidden_kernel(
    d_part, gate_ref, own_g, own_u, own_b, got_g, got_u, got_b, w_gate, w_up, d_gate, d_up, scaled, back
):
    gate = gate_ref[:, 0:1].astype(f32)
    pre_gate = own_g[...] + got_g[...].astype(f32)
    pre_up = own_u[...] + got_u[...].astype(f32)
    back_proj = own_b[...] + got_b[...].astype(f32)
    sig = jax.nn.sigmoid(pre_gate)
    activated = pre_gate * sig
    hidden = activated * pre_up
    share = jnp.sum(back_proj * hidden, axis=1, keepdims=True)
    scaled[...] = (gate * hidden).astype(bf16)
    d_hidden = gate * back_proj
    d_gate[...] = (d_hidden * pre_up * sig * (1.0 + pre_gate * (1.0 - sig))).astype(bf16)
    d_up[...] = (d_hidden * activated).astype(bf16)
    contract = (((1,), (1,)), ((), ()))
    back[:, :d_part] = (
        lax.dot_general(d_gate[...], w_gate[...], contract, preferred_element_type=f32)
        + lax.dot_general(d_up[...], w_up[...], contract, preferred_element_type=f32)
    ).astype(bf16)
    high = share.astype(bf16)
    low = (share - high.astype(f32)).astype(bf16)
    lane = lax.broadcasted_iota(jnp.int32, (share.shape[0], LANES), 1)
    back[:, d_part:] = jnp.where(lane == 0, high, jnp.where(lane == 1, low, jnp.zeros_like(low)))


def expand_kernel(place_ref, a_ref, b_ref, out_ref):
    total = (a_ref[...].astype(f32) + b_ref[...].astype(f32)).astype(bf16)
    out_ref[...] = jnp.dot(place_ref[...], total, preferred_element_type=f32).astype(bf16)


def call(kernel, out_shape, in_specs, name, flops=0, bytes_accessed=0):
    return pl.pallas_call(
        kernel,
        out_shape=out_shape,
        in_specs=in_specs,
        out_specs=jax.tree.map(lambda _: pl.BlockSpec(memory_space=pltpu.VMEM), out_shape),
        compiler_params=pltpu.CompilerParams(vmem_limit_bytes=VMEM_LIMIT),
        cost_estimate=pl.CostEstimate(flops=flops, bytes_accessed=bytes_accessed, transcendentals=0),
        name=name,
    )


def on_device(tokens, cotangent, expert_ids, gate_values, w_gate, w_up, w_down_t):
    micro_count, tok_count, d_model = tokens.shape
    top_count = expert_ids.shape[2]
    pipe_size = lax.axis_size("pipe")
    expert_size = lax.axis_size("expert")
    group_size = expert_size // EXPERTS
    bits = [1 << i for i in reversed(range(group_size.bit_length() - 1))]
    d_part, f_part = w_gate.shape
    seg = -(-d_part // LANES) * LANES
    width = 2 * seg + LANES
    own_rows = micro_count * tok_count
    expert = lax.axis_index("expert") // group_size

    def shares(x):
        x = x.reshape(own_rows, pipe_size, d_part)
        return jnp.pad(x, ((0, 0), (0, 0), (0, seg - d_part)))

    ids = expert_ids.reshape(own_rows, top_count)
    extras = jnp.concatenate([ids.astype(bf16), gate_values.reshape(own_rows, top_count)], 1)
    extras = jnp.pad(extras, ((0, 0), (0, LANES - 2 * top_count)))
    extras = jnp.broadcast_to(extras[:, None], (own_rows, pipe_size, LANES))
    send = jnp.concatenate([shares(tokens), shares(cotangent), extras], 2)
    send = jnp.swapaxes(send, 0, 1)

    layer_rows = lax.all_to_all(send, "pipe", split_axis=0, concat_axis=0, tiled=True)
    layer_rows = layer_rows.reshape(pipe_size * own_rows, width)
    rows = jnp.concatenate(
        [layer_rows] + [swap(layer_rows, "expert", k * group_size) for k in range(1, EXPERTS)], 0
    )
    row_count = rows.shape[0]
    slot_count = row_count // tok_count * CAP
    vmem = pl.BlockSpec(memory_space=pltpu.VMEM)
    smem = pl.BlockSpec(memory_space=pltpu.SMEM)
    slots, place = call(
        functools.partial(compact_kernel, tok_count),
        (
            jax.ShapeDtypeStruct((slot_count, width), bf16),
            jax.ShapeDtypeStruct((row_count, slot_count), bf16),
        ),
        [smem, vmem],
        "compact",
    )(expert.reshape(1).astype(jnp.int32), rows)

    for bit in bits:
        slots = jnp.concatenate([slots, swap(slots, "expert", bit)], 0)
    total = slots.shape[0]
    tok_rows, cot_rows = slots[:, :d_part], slots[:, seg : seg + d_part]
    gate_col = slots[:, 2 * seg :]

    own, got = [], []
    for left, weight in ((tok_rows, w_gate), (tok_rows, w_up), (cot_rows, w_down_t)):
        part = jnp.dot(left, weight, preferred_element_type=f32)
        bit = pipe_size // 2
        while bit > 1:
            part = part + swap(part.astype(bf16), "pipe", bit).astype(f32)
            bit //= 2
        own.append(part)
        got.append(swap(part.astype(bf16), "pipe", 1) if pipe_size > 1 else jnp.zeros_like(part, bf16))

    hidden_shape = jax.ShapeDtypeStruct((total, f_part), bf16)
    d_gate, d_up, scaled, back = call(
        functools.partial(hidden_kernel, d_part),
        (hidden_shape,) * 3 + (jax.ShapeDtypeStruct((total, d_part + LANES), bf16),),
        [vmem] * 9,
        "hidden",
    )(gate_col, *own, *got, w_gate, w_up)

    tokens_total = own_rows * pipe_size * expert_size
    scale = 1.0 / math.sqrt(tokens_total * top_count / EXPERTS)
    contract = (((0,), (0,)), ((), ()))

    def weight_grad(left, right):
        return (lax.dot_general(left, right, contract, preferred_element_type=f32) * scale).astype(bf16)

    dw_gate = weight_grad(tok_rows, d_gate)
    dw_up = weight_grad(tok_rows, d_up)
    dw_down_t = weight_grad(cot_rows, scaled)

    for bit in reversed(bits[1:]):
        half = back.shape[0] // 2
        back = (back[:half].astype(f32) + swap(back[half:], "expert", bit).astype(f32)).astype(bf16)
    half = back.shape[0] // 2
    got_back = swap(back[half:], "expert", bits[0])
    rows_back = call(
        expand_kernel,
        jax.ShapeDtypeStruct((row_count, d_part + LANES), bf16),
        [vmem] * 3,
        "expand",
    )(place, back[:half], got_back)

    block = pipe_size * own_rows
    pieces = [rows_back[:block]] + [
        swap(rows_back[k * block : (k + 1) * block], "expert", k * group_size) for k in range(1, EXPERTS)
    ]
    summed = sum(piece[:, :d_part].astype(f32) for piece in pieces).astype(bf16)
    summed = summed.reshape(pipe_size, own_rows, d_part)
    d_tokens = lax.all_to_all(summed, "pipe", split_axis=0, concat_axis=0, tiled=True)
    d_tokens = jnp.swapaxes(d_tokens, 0, 1).reshape(micro_count, tok_count, d_model)
    start = lax.axis_index("pipe") * own_rows
    gate_grad = jnp.zeros((own_rows, top_count), f32)
    for k, piece in enumerate(pieces):
        share = lax.dynamic_slice_in_dim(piece[:, d_part : d_part + 2].astype(f32), start, own_rows, 0)
        gate_grad = gate_grad + jnp.where(ids == (expert ^ k), share[:, 0:1] + share[:, 1:2], 0.0)
    gate_weight_gradient = gate_grad.reshape(micro_count, tok_count, top_count)
    return (d_tokens, gate_weight_gradient, dw_gate, dw_up, dw_down_t)


def solution(mesh):
    rows = P(None, ("pipe", "expert"), None)
    weights = P("pipe", "expert")
    return jax.shard_map(
        on_device,
        mesh=mesh,
        in_specs=(rows, rows, rows, rows, weights, weights, weights),
        out_specs=(rows, rows, weights, weights, weights),
        check_vma=False,
    )
```

```python
import functools
import math

import jax
import jax.numpy as jnp
from jax import lax
from jax.experimental import pallas as pl
from jax.experimental.pallas import tpu as pltpu
from jax.sharding import PartitionSpec as P

EXPERTS = 4
CAP = 3
GROUPS = 2
LANES = 128
f32, bf16, i32 = jnp.float32, jnp.bfloat16, jnp.int32
ROWS_BY_ROWS = (((0,), (0,)), ((), ()))
COLUMNS_BY_COLUMNS = (((1,), (1,)), ((), ()))


def swap(x, axis, bit):
    return lax.ppermute(x, axis, [(i, i ^ bit) for i in range(lax.axis_size(axis))])


def prep_kernel(d_part, tok_ref, cot_ref, ids_ref, gate_ref, out_ref):
    micro_count = tok_ref.shape[0]
    seg = out_ref.shape[2] - LANES

    def flat(ref):
        return jnp.concatenate([ref[m].astype(f32) for m in range(micro_count)], 0)

    ids, gates = flat(ids_ref), flat(gate_ref)
    lane = lax.broadcasted_iota(i32, (ids.shape[0], LANES), 1)
    extras = jnp.zeros((ids.shape[0], LANES), f32)
    for k in range(ids.shape[1]):
        extras = jnp.where(lane == k, ids[:, k : k + 1], extras)
        extras = jnp.where(lane == ids.shape[1] + k, gates[:, k : k + 1], extras)
    both = jnp.concatenate([flat(tok_ref), flat(cot_ref)], 0).astype(bf16)
    extras = jnp.concatenate([extras, extras], 0).astype(bf16)
    for p in range(out_ref.shape[0]):
        out_ref[p, :, :d_part] = both[:, p * d_part : (p + 1) * d_part]
        if seg > d_part:
            out_ref[p, :, d_part:seg] = jnp.zeros((both.shape[0], seg - d_part), bf16)
        out_ref[p, :, seg:] = extras


def pack_kernel(tok_count, top_count, me_ref, rows_ref, *out_refs):
    slot_refs, place_ref, info_ref = out_refs[:EXPERTS], out_refs[EXPERTS], out_refs[EXPERTS + 1]
    pipe_size, both_rows, width = rows_ref.shape
    own_rows = both_rows // 2
    total = pipe_size * both_rows
    slot_count = slot_refs[0].shape[0] // 2
    me = me_ref[0]
    rows = jnp.concatenate([rows_ref[p] for p in range(pipe_size)], 0)
    extras = rows[:, width - LANES :].astype(f32)
    row = lax.broadcasted_iota(i32, (total, total), 0)
    other = lax.broadcasted_iota(i32, (total, total), 1)
    earlier = ((other < row) & (other // tok_count == row // tok_count)).astype(bf16)
    at = (lax.broadcasted_iota(i32, (total, LANES), 1) ^ me).astype(f32)
    routed = jnp.zeros((total, LANES), f32)
    for k in range(top_count):
        routed = jnp.where(extras[:, k : k + 1] == at, 1.0, routed)
    position = jnp.dot(earlier, routed.astype(bf16), preferred_element_type=f32)
    index = lax.broadcasted_iota(i32, (total, 1), 0)
    within = index % both_rows
    kind = within // own_rows
    block = index // both_rows * (own_rows // tok_count) + within % own_rows // tok_count
    base = (kind * slot_count + block * CAP).astype(f32)
    lane = lax.broadcasted_iota(i32, (total, 2 * slot_count), 1).astype(f32)
    for k in range(EXPERTS):
        chosen = (lane == base + position[:, k : k + 1]) & (routed[:, k : k + 1] > 0.0)
        place = jnp.where(chosen, 1.0, 0.0)
        slot_refs[k][...] = lax.dot_general(
            place.astype(bf16), rows, ROWS_BY_ROWS, preferred_element_type=f32
        ).astype(bf16)
        for p in range(pipe_size):
            start = p * both_rows
            place_ref[k, p * own_rows : (p + 1) * own_rows, :] = place[start : start + own_rows, :slot_count]
    for p in range(pipe_size):
        start = p * both_rows
        info_ref[p * own_rows : (p + 1) * own_rows, :] = extras[start : start + own_rows]


def hidden_kernel(d_part, top_count, me_ref, *refs):
    groups = [refs[7 * g : 7 * (g + 1)] for g in range(GROUPS)]
    w_gate, w_up, d_gate, d_up, scaled, low_back, high_back = refs[7 * GROUPS :]
    me = me_ref[0].astype(f32)
    shares = []
    for g, (info, own_g, own_u, own_b, got_g, got_u, got_b) in enumerate(groups):
        count = info.shape[0]
        extras = info[...].astype(f32)
        gate = jnp.zeros((count, 1), f32)
        for k in range(top_count):
            gate = gate + jnp.where(
                extras[:, k : k + 1] == me, extras[:, top_count + k : top_count + k + 1], 0.0
            )
        pre_gate = own_g[...] + got_g[...].astype(f32)
        pre_up = own_u[...] + got_u[...].astype(f32)
        back_proj = own_b[...] + got_b[...].astype(f32)
        sig = jax.nn.sigmoid(pre_gate)
        activated = pre_gate * sig
        hidden = activated * pre_up
        shares.append(jnp.sum(back_proj * hidden, axis=1, keepdims=True))
        d_hidden = gate * back_proj
        here = slice(g * count, (g + 1) * count)
        scaled[here] = (gate * hidden).astype(bf16)
        d_gate[here] = (d_hidden * pre_up * sig * (1.0 + pre_gate * (1.0 - sig))).astype(bf16)
        d_up[here] = (d_hidden * activated).astype(bf16)
    back = lax.dot_general(
        d_gate[...], w_gate[...], COLUMNS_BY_COLUMNS, preferred_element_type=f32
    ) + lax.dot_general(d_up[...], w_up[...], COLUMNS_BY_COLUMNS, preferred_element_type=f32)
    share = jnp.concatenate(shares, 0)
    high = share.astype(bf16).astype(f32)
    lane = lax.broadcasted_iota(i32, (share.shape[0], LANES), 1)
    tail = jnp.where(lane == 0, high, jnp.where(lane == 1, share - high, 0.0))
    half, rows = low_back.shape[0], low_back.shape[1] // GROUPS
    for member in range(2 * half):
        out = low_back if member < half else high_back
        starts = [g * 2 * half * rows + member * rows for g in range(GROUPS)]
        out[member % half, :, :d_part] = jnp.concatenate([back[s : s + rows] for s in starts], 0).astype(bf16)
        out[member % half, :, d_part:] = jnp.concatenate([tail[s : s + rows] for s in starts], 0).astype(bf16)


def owner_kernel(d_part, top_count, me_ref, place_ref, info_ref, *refs):
    slot_refs, rows_ref, grad_ref = refs[:EXPERTS], refs[EXPERTS], refs[EXPERTS + 1]
    total = jnp.zeros((info_ref.shape[0], d_part), f32)
    grad = jnp.zeros((info_ref.shape[0], LANES), f32)
    lane = lax.broadcasted_iota(i32, grad.shape, 1)
    for k in range(EXPERTS):
        rows = jnp.dot(place_ref[k].astype(bf16), slot_refs[k][...], preferred_element_type=f32)
        total = total + rows[:, :d_part]
        share = rows[:, d_part : d_part + 1] + rows[:, d_part + 1 : d_part + 2]
        expert = (me_ref[0] ^ k).astype(f32)
        grad = jnp.where((info_ref[...] == expert) & (lane < top_count), share, grad)
    pipe_size, own_rows = rows_ref.shape[0], rows_ref.shape[1]
    for p in range(pipe_size):
        rows_ref[p] = total[p * own_rows : (p + 1) * own_rows].astype(bf16)
        grad_ref[p] = grad[p * own_rows : (p + 1) * own_rows]


def call(kernel, out_shape, operand_count, name, smem=1, mib=8, flops=0, bytes_accessed=0):
    vmem = pl.BlockSpec(memory_space=pltpu.VMEM)
    return pl.pallas_call(
        kernel,
        out_shape=out_shape,
        in_specs=[pl.BlockSpec(memory_space=pltpu.SMEM)] * smem + [vmem] * operand_count,
        out_specs=jax.tree.map(lambda _: vmem, out_shape),
        compiler_params=pltpu.CompilerParams(vmem_limit_bytes=mib << 20),
        cost_estimate=pl.CostEstimate(flops=flops, bytes_accessed=bytes_accessed, transcendentals=0),
        name=name,
    )


def pipe_exchange(blocks):
    pipe_size = blocks.shape[0]
    if pipe_size != 2:
        return lax.all_to_all(blocks, "pipe", split_axis=0, concat_axis=0, tiled=True)
    first = lax.axis_index("pipe") == 0
    got = swap(jnp.where(first, blocks[1], blocks[0]), "pipe", 1)
    return jnp.where(first, jnp.stack([blocks[0], got]), jnp.stack([got, blocks[1]]))


def on_device(tokens, cotangent, expert_ids, gate_values, w_gate, w_up, w_down_t):
    micro_count, tok_count, d_model = tokens.shape
    top_count = expert_ids.shape[2]
    pipe_size = lax.axis_size("pipe")
    expert_size = lax.axis_size("expert")
    group_size = expert_size // EXPERTS
    bits = [1 << i for i in reversed(range(group_size.bit_length() - 1))]
    d_part, f_part = w_gate.shape
    width = -(-d_part // LANES) * LANES + LANES
    own_rows = micro_count * tok_count
    slot_count = pipe_size * micro_count * CAP
    expert = (lax.axis_index("expert") // group_size).astype(i32)
    me = expert.reshape(1)
    shape = jax.ShapeDtypeStruct

    send = call(
        functools.partial(prep_kernel, d_part), shape((pipe_size, 2 * own_rows, width), bf16), 4, "prep", smem=0
    )(tokens, cotangent, expert_ids, gate_values)
    layer_rows = pipe_exchange(send)
    *slots, place, info = call(
        functools.partial(pack_kernel, tok_count, top_count),
        tuple(shape((2 * slot_count, width), bf16) for _ in range(EXPERTS))
        + (
            shape((EXPERTS, pipe_size * own_rows, slot_count), f32),
            shape((pipe_size * own_rows, LANES), f32),
        ),
        1,
        "pack",
    )(me, layer_rows)

    gathered = [slots[0]] + [swap(slots[k], "expert", k * group_size) for k in range(1, EXPERTS)]
    per_group = EXPERTS // GROUPS
    operands, tok_groups, cot_groups = [], [], []
    for g in range(GROUPS):
        blocks = gathered[g * per_group : (g + 1) * per_group]
        rows = jnp.stack(
            [jnp.concatenate([b[a * slot_count : (a + 1) * slot_count] for b in blocks], 0) for a in range(2)]
        )
        for bit in bits:
            rows = jnp.concatenate([rows, swap(rows, "expert", bit)], 1)
        tok_rows, cot_rows = rows[0, :, :d_part], rows[1, :, :d_part]
        tok_groups.append(tok_rows)
        cot_groups.append(cot_rows)
        own, got = [], []
        for left, weight in ((tok_rows, w_gate), (tok_rows, w_up), (cot_rows, w_down_t)):
            part = jnp.dot(left, weight, preferred_element_type=f32)
            bit = pipe_size // 2
            while bit > 1:
                part = part + swap(part.astype(bf16), "pipe", bit).astype(f32)
                bit //= 2
            own.append(part)
            got.append(swap(part.astype(bf16), "pipe", 1) if pipe_size > 1 else jnp.zeros_like(part, bf16))
        operands += [rows[0, :, width - LANES :]] + own + got

    total = GROUPS * operands[0].shape[0]
    hidden_shape = shape((total, f_part), bf16)
    half_shape = shape((group_size // 2, EXPERTS * slot_count, d_part + LANES), bf16)
    moved = total * f_part * 4 * 5 + total * d_part * 8 + 4 * d_part * f_part
    d_gate, d_up, scaled, low, high = call(
        functools.partial(hidden_kernel, d_part, top_count),
        (hidden_shape,) * 3 + (half_shape,) * 2,
        7 * GROUPS + 2,
        "hidden",
        mib=min(52, 8 + 2 * moved // (1 << 20)),
        flops=4 * total * d_part * f_part,
        bytes_accessed=moved,
    )(me, *operands, w_gate, w_up)

    back = None
    for bit in reversed(bits):
        if back is not None:
            half = back.shape[0] // 2
            low, high = back[:half], back[half:]
        back = (low.astype(f32) + swap(high, "expert", bit).astype(f32)).astype(bf16)
    back = back[0]
    pieces = [back[k * slot_count : (k + 1) * slot_count] for k in range(EXPERTS)]
    pieces = [pieces[0]] + [swap(pieces[k], "expert", k * group_size) for k in range(1, EXPERTS)]

    tokens_total = own_rows * pipe_size * expert_size
    scale = 1.0 / math.sqrt(tokens_total * top_count / EXPERTS)
    tok_all, cot_all = jnp.concatenate(tok_groups, 0), jnp.concatenate(cot_groups, 0)

    def weight_grad(left, right):
        return (lax.dot_general(left, right, ROWS_BY_ROWS, preferred_element_type=f32) * scale).astype(bf16)

    dw_gate = weight_grad(tok_all, d_gate)
    dw_up = weight_grad(tok_all, d_up)
    dw_down_t = weight_grad(cot_all, scaled)

    summed, grads = call(
        functools.partial(owner_kernel, d_part, top_count),
        (shape((pipe_size, own_rows, d_part), bf16), shape((pipe_size, own_rows, LANES), f32)),
        2 + EXPERTS,
        "owner",
    )(me, place, info, *pieces)
    d_tokens = jnp.swapaxes(pipe_exchange(summed), 0, 1).reshape(micro_count, tok_count, d_model)
    grads = lax.dynamic_index_in_dim(grads, lax.axis_index("pipe"), 0, keepdims=False)
    gate_weight_gradient = grads[:, :top_count].reshape(micro_count, tok_count, top_count)
    return (d_tokens, gate_weight_gradient, dw_gate, dw_up, dw_down_t)


def solution(mesh):
    rows = P(None, ("pipe", "expert"), None)
    weights = P("pipe", "expert")
    return jax.shard_map(
        on_device,
        mesh=mesh,
        in_specs=(rows, rows, rows, rows, weights, weights, weights),
        out_specs=(rows, rows, weights, weights, weights),
        check_vma=False,
    )
```

```python
import functools
import math

import jax
import jax.numpy as jnp
from jax import lax
from jax.experimental import pallas as pl
from jax.experimental.pallas import tpu as pltpu
from jax.sharding import PartitionSpec as P

EXPERTS = 4
CAP = 3
GROUPS = 2
PER_GROUP = EXPERTS // GROUPS
LANES = 128
ROWS = 8
PREP_MIB = 56
f32, bf16, i32 = jnp.float32, jnp.bfloat16, jnp.int32
ROWS_BY_ROWS = (((0,), (0,)), ((), ()))
COLUMNS_BY_COLUMNS = (((1,), (1,)), ((), ()))
shape = jax.ShapeDtypeStruct


def swap(x, axis, bit):
    return lax.ppermute(x, axis, [(i, i ^ bit) for i in range(lax.axis_size(axis))])


def swap_both(x, bit):
    count = lax.axis_size("expert")
    pairs = [(p * count + e, (p ^ 1) * count + (e ^ bit)) for p in range(2) for e in range(count)]
    return lax.ppermute(x, ("pipe", "expert"), pairs)


def prep_kernel(d_part, tok_hbm, cot_hbm, ids_hbm, gate_hbm, out_ref, tok_ref, cot_ref, ids_ref, gate_ref, sems):
    pairs = ((tok_hbm, tok_ref), (cot_hbm, cot_ref), (ids_hbm, ids_ref), (gate_hbm, gate_ref))
    copies = [pltpu.make_async_copy(src, dst, sems.at[i]) for i, (src, dst) in enumerate(pairs)]
    for copy in copies:
        copy.start()
    for copy in copies:
        copy.wait()
    micro_count, tok_count = tok_ref.shape[:2]
    top_count = ids_ref.shape[1]
    seg = out_ref.shape[2] - LANES

    def flat(ref):
        return jnp.concatenate([ref[m].astype(f32) for m in range(micro_count)], 0)

    lane = lax.broadcasted_iota(i32, (tok_count, LANES), 1)
    diagonal = lax.broadcasted_iota(i32, (tok_count, tok_count), 0) == lax.broadcasted_iota(
        i32, (tok_count, tok_count), 1
    )
    blocks = []
    for m in range(micro_count):
        block = jnp.zeros((tok_count, LANES), f32)
        for at, ref in enumerate((ids_ref, gate_ref)):
            values = ref[m].astype(f32)
            for k in range(top_count):
                row = jnp.broadcast_to(values[k : k + 1], (tok_count, tok_count))
                column = jnp.sum(jnp.where(diagonal, row, 0.0), axis=1, keepdims=True)
                block = jnp.where(lane == at * top_count + k, column, block)
        blocks.append(block)
    extras = jnp.concatenate(blocks + blocks, 0).astype(bf16)
    both = jnp.concatenate([flat(tok_ref), flat(cot_ref)], 0).astype(bf16)
    for p in range(out_ref.shape[0]):
        out_ref[p, :, :d_part] = both[:, p * d_part : (p + 1) * d_part]
        if seg > d_part:
            out_ref[p, :, d_part:seg] = jnp.zeros((both.shape[0], seg - d_part), bf16)
        out_ref[p, :, seg:] = extras


def pack_kernel(tok_count, top_count, where_ref, rows_ref, *out_refs):
    slot_refs, place_ref = out_refs[:EXPERTS], out_refs[EXPERTS]
    pipe_size, both_rows, width = rows_ref.shape
    own_rows = both_rows // 2
    total = pipe_size * both_rows
    slot_count = slot_refs[0].shape[0] // 2
    me = where_ref[0]
    rows = jnp.concatenate([rows_ref[p] for p in range(pipe_size)], 0)
    extras = rows[:, width - LANES :].astype(f32)
    row = lax.broadcasted_iota(i32, (total, total), 0)
    other = lax.broadcasted_iota(i32, (total, total), 1)
    earlier = ((other < row) & (other // tok_count == row // tok_count)).astype(bf16)
    at = (lax.broadcasted_iota(i32, (total, LANES), 1) ^ me).astype(f32)
    routed = jnp.zeros((total, LANES), f32)
    for k in range(top_count):
        routed = jnp.where(extras[:, k : k + 1] == at, 1.0, routed)
    position = jnp.dot(earlier, routed.astype(bf16), preferred_element_type=f32)
    index = lax.broadcasted_iota(i32, (total, 1), 0)
    within = index % both_rows
    block = within % own_rows // tok_count
    device = index // both_rows
    base = within // own_rows * slot_count + (device * (own_rows // tok_count) + block) * CAP
    lane = lax.broadcasted_iota(i32, (total, EXPERTS * 2 * slot_count), 1).astype(f32)
    chosen = jnp.zeros(lane.shape, f32)
    small_lane = lax.broadcasted_iota(i32, (total, LANES), 1).astype(f32)
    places = jnp.zeros((total, LANES), f32)
    for k in range(EXPERTS):
        here = routed[:, k : k + 1] > 0.0
        target = (k * 2 * slot_count + base).astype(f32) + position[:, k : k + 1]
        chosen = chosen + jnp.where((lane == target) & here, 1.0, 0.0)
        local = (k * ROWS + block * CAP).astype(f32) + position[:, k : k + 1]
        places = places + jnp.where((small_lane == local) & here, 1.0, 0.0)
    slots = lax.dot_general(chosen.astype(bf16), rows, ROWS_BY_ROWS, preferred_element_type=f32)
    for k in range(EXPERTS):
        slot_refs[k][...] = slots[2 * k * slot_count : 2 * (k + 1) * slot_count].astype(bf16)
    for p in range(pipe_size):
        start = p * both_rows
        place_ref[p, :, :LANES] = places[start : start + own_rows]
        place_ref[p, :, LANES:] = extras[start : start + own_rows]


def join_kernel(pipe_size, *refs):
    blocks, out_ref = [ref[...].astype(f32) for ref in refs[:PER_GROUP]], refs[-1]
    rows = blocks[0].shape[0] // 2 // pipe_size
    for a in range(2):
        starts = [(a * pipe_size + p) * rows for p in range(pipe_size)]
        out_ref[a] = jnp.concatenate([b[s : s + rows] for s in starts for b in blocks], 0).astype(bf16)


def hidden_kernel(d_part, top_count, pipe_size, where_ref, *refs):
    pieces = [refs[5 * i : 5 * (i + 1)] for i in range(2 * GROUPS)]
    w_gate, w_up = refs[10 * GROUPS : 10 * GROUPS + 2]
    d_gate, d_up, scaled, low_back, high_back = refs[-5:]
    me = where_ref[0].astype(f32)
    shares = []
    for i, (info, own_g, own_u, own_b, got) in enumerate(pieces):
        count = own_g.shape[0]
        extras = info[...].astype(f32)
        gate = jnp.zeros((count, 1), f32)
        for k in range(top_count):
            gate = gate + jnp.where(
                extras[:, k : k + 1] == me, extras[:, top_count + k : top_count + k + 1], 0.0
            )
        pre_gate = own_g[...] + got[0].astype(f32)
        pre_up = own_u[...] + got[1].astype(f32)
        back_proj = own_b[...] + got[2].astype(f32)
        sig = jax.nn.sigmoid(pre_gate)
        activated = pre_gate * sig
        hidden = activated * pre_up
        shares.append(jnp.sum(back_proj * hidden, axis=1, keepdims=True))
        d_hidden = gate * back_proj
        here = slice(i * count, (i + 1) * count)
        scaled[here] = (gate * hidden).astype(bf16)
        d_gate[here] = (d_hidden * pre_up * sig * (1.0 + pre_gate * (1.0 - sig))).astype(bf16)
        d_up[here] = (d_hidden * activated).astype(bf16)
    back = lax.dot_general(
        d_gate[...], w_gate[...], COLUMNS_BY_COLUMNS, preferred_element_type=f32
    ) + lax.dot_general(d_up[...], w_up[...], COLUMNS_BY_COLUMNS, preferred_element_type=f32)
    share = jnp.concatenate(shares, 0)
    high = share.astype(bf16).astype(f32)
    lane = lax.broadcasted_iota(i32, (share.shape[0], LANES), 1)
    tail = jnp.where(lane == 0, high, jnp.where(lane == 1, share - high, 0.0))
    members = low_back.shape[1] // pipe_size * 2
    used = count // members // pipe_size
    for h in range(2):
        for member in range(members):
            ref = low_back if member < members // 2 else high_back
            for p in range(pipe_size):
                starts = [(2 * g + h) * count + (member * pipe_size + p) * used for g in range(GROUPS)]
                at = member % (members // 2) * pipe_size + (p ^ where_ref[1] if pipe_size == 2 else p)
                for columns, values in ((slice(0, d_part), back), (slice(d_part, None), tail)):
                    block = jnp.concatenate([values[start : start + used] for start in starts], 0)
                    ref[h, at, :, columns] = block.astype(bf16)


def fold_kernel(a_ref, b_ref, *out_refs):
    for i, ref in enumerate(out_refs):
        here = i // a_ref.shape[1], i % a_ref.shape[1]
        ref[...] = (a_ref[here].astype(f32) + b_ref[here].astype(f32)).astype(bf16)


def fold_pairs_kernel(used, a_ref, b_ref, c_ref, d_ref, *out_refs):
    totals = (
        a_ref[...].astype(f32) + b_ref[...].astype(f32),
        c_ref[...].astype(f32) + d_ref[...].astype(f32),
    )
    for k, ref in enumerate(out_refs):
        for h, total in enumerate(totals):
            rows = total[k * used : (k + 1) * used]
            pad = jnp.zeros((ROWS - used, rows.shape[1]), f32)
            ref[h] = jnp.concatenate([rows, pad], 0).astype(bf16)


def owner_kernel(d_part, where_ref, place_ref, *refs):
    piece_refs, tok_ref, grad_ref = refs[:EXPERTS], refs[EXPERTS], refs[EXPERTS + 1]
    micro_count, tok_count = tok_ref.shape[:2]
    top_count = grad_ref.shape[1]
    pipe_size = piece_refs[0].shape[0]
    mine = place_ref[where_ref[1]]
    place = mine[:, : EXPERTS * ROWS].astype(bf16)
    ids = mine[:, LANES:]
    halves = []
    for h in range(pipe_size):
        rows = jnp.concatenate([ref[h].astype(f32) for ref in piece_refs], 0)
        halves.append(rows)
    sums = [jnp.dot(place, h.astype(bf16), preferred_element_type=f32)[:, :d_part] for h in halves]
    if pipe_size == 2:
        first = where_ref[1] == 0
        sums = [jnp.where(first, sums[0], sums[1]), jnp.where(first, sums[1], sums[0])]
    tail = halves[0][:, d_part:]
    shares = tail[:, 0:1] + tail[:, 1:2]
    slot_lane = lax.broadcasted_iota(i32, place.shape, 1)
    diagonal = lax.broadcasted_iota(i32, (tok_count, tok_count), 0) == lax.broadcasted_iota(
        i32, (tok_count, tok_count), 1
    )
    square = EXPERTS * ROWS
    eye = lax.broadcasted_iota(i32, (square, square), 0) == lax.broadcasted_iota(i32, (square, square), 1)
    share_row = jnp.sum(jnp.where(eye, jnp.broadcast_to(shares, (square, square)), 0.0), axis=0, keepdims=True)
    picked = mine[:, : EXPERTS * ROWS] * share_row
    expert_of = ((slot_lane // ROWS) ^ where_ref[0]).astype(f32)
    for k in range(top_count):
        grad = jnp.sum(jnp.where(expert_of == ids[:, k : k + 1], picked, 0.0), axis=1, keepdims=True)
        for m in range(micro_count):
            part = jnp.broadcast_to(grad[m * tok_count : (m + 1) * tok_count], (tok_count, tok_count))
            grad_ref[m, k : k + 1, :] = jnp.sum(jnp.where(diagonal, part, 0.0), axis=0, keepdims=True)
    for m in range(micro_count):
        for p in range(pipe_size):
            tok_ref[m, :, p * d_part : (p + 1) * d_part] = sums[p][m * tok_count : (m + 1) * tok_count].astype(bf16)


def flip_kernel(*refs):
    refs[-1][...] = jnp.concatenate([ref[...] for ref in refs[:-1]], 0).T


def weight_kernel(scale, block, tok_ref, cot_ref, d_gate, d_up, scaled, after, *refs):
    del after
    out_refs, held, sems = refs[:3], refs[3], refs[4]
    copies = []
    for i in range(tok_ref.shape[0] // block):
        here = slice(i * block, (i + 1) * block)
        for w, (left, right) in enumerate(((tok_ref, d_gate), (tok_ref, d_up), (cot_ref, scaled))):
            rows = jnp.dot(left[here], right[...], preferred_element_type=f32)
            held[w, here] = (rows * scale).astype(bf16)
            copies.append(pltpu.make_async_copy(held.at[w, here], out_refs[w].at[here], sems.at[w, i]))
            copies[-1].start()
    for copy in copies:
        copy.wait()


def tie_kernel(*refs):
    del refs


def call(kernel, out_shape, in_specs, name, mib=8, flops=0, moved=0, **more):
    specs = {"s": pl.BlockSpec(memory_space=pltpu.SMEM), "v": pl.BlockSpec(memory_space=pltpu.VMEM)}
    specs["a"] = pl.BlockSpec(memory_space=pl.ANY)
    specs["h"] = pl.BlockSpec(memory_space=pltpu.HBM)
    more.setdefault("out_specs", jax.tree.map(lambda _: specs["v"], out_shape))
    return pl.pallas_call(
        kernel,
        out_shape=out_shape,
        in_specs=[specs[c] for c in in_specs],
        compiler_params=pltpu.CompilerParams(vmem_limit_bytes=mib << 20),
        cost_estimate=pl.CostEstimate(flops=flops, bytes_accessed=moved, transcendentals=0),
        name=name,
        **more,
    )


def tie(values, after):
    return call(
        tie_kernel,
        [shape(v.shape, v.dtype) for v in values],
        "a" * (len(values) + 1),
        "tie",
        out_specs=[pl.BlockSpec(memory_space=pl.ANY)] * len(values),
        input_output_aliases={i: i for i in range(len(values))},
    )(*values, after)


def on_device(tokens, cotangent, expert_ids, gate_values, w_gate, w_up, w_down_t):
    micro_count, tok_count, d_model = tokens.shape
    top_count = expert_ids.shape[2]
    pipe_size = lax.axis_size("pipe")
    expert_size = lax.axis_size("expert")
    group_size = expert_size // EXPERTS
    bits = [1 << i for i in reversed(range(group_size.bit_length() - 1))]
    d_part, f_part = w_gate.shape
    width = -(-d_part // LANES) * LANES + LANES
    own_rows = micro_count * tok_count
    slots_here = micro_count * CAP
    slot_count = pipe_size * slots_here
    pipe = lax.axis_index("pipe")
    where = jnp.stack([lax.axis_index("expert") // group_size, pipe]).astype(i32)

    send = call(
        functools.partial(prep_kernel, d_part),
        shape((pipe_size, 2 * own_rows, width), bf16),
        "hhhh",
        "prep",
        scratch_shapes=[
            pltpu.VMEM(tokens.shape, bf16),
            pltpu.VMEM(tokens.shape, bf16),
            pltpu.VMEM((micro_count, top_count, tok_count), i32),
            pltpu.VMEM((micro_count, top_count, tok_count), bf16),
            pltpu.SemaphoreType.DMA((4,)),
        ],
        mib=PREP_MIB,
    )(tokens, cotangent, jnp.swapaxes(expert_ids, 1, 2), jnp.swapaxes(gate_values, 1, 2))
    if pipe_size == 2:
        first = pipe == 0
        got = swap(jnp.where(first, send[1], send[0]), "pipe", 1)
        layer_rows = jnp.where(first, jnp.stack([send[0], got]), jnp.stack([got, send[1]]))
    else:
        layer_rows = lax.all_to_all(send, "pipe", split_axis=0, concat_axis=0, tiled=True)
    *slots, place = call(
        functools.partial(pack_kernel, tok_count, top_count),
        tuple(shape((2 * slot_count, width), bf16) for _ in range(EXPERTS))
        + (shape((pipe_size, own_rows, 2 * LANES), f32),),
        "sv",
        "pack",
    )(where, layer_rows)

    gathered = [slots[0]] + [swap(slots[k], "expert", k * group_size) for k in range(1, EXPERTS)]
    groups, after = [], ()
    for g in range(GROUPS):
        joined = call(
            functools.partial(join_kernel, pipe_size),
            shape((2, PER_GROUP * slot_count, width), bf16),
            "v" * PER_GROUP + "a" * len(after),
            "join",
        )(*gathered[g * PER_GROUP : (g + 1) * PER_GROUP], *after)
        after = (joined,)
        sent = joined if g == 0 else tie([joined], groups[-1][1])[0]
        groups.append([joined, swap(sent, "expert", bits[0])])
    for halves in groups:
        for h in range(2):
            for bit in bits[1:]:
                halves[h] = jnp.concatenate([halves[h], swap(halves[h], "expert", bit)], 1)

    exchanged = []
    for halves in groups:
        for rows in halves:
            tok_rows, cot_rows = rows[0, :, :d_part], rows[1, :, :d_part]
            own = []
            for left, weight in ((tok_rows, w_gate), (tok_rows, w_up), (cot_rows, w_down_t)):
                own.append(jnp.dot(left, weight, preferred_element_type=f32))
            bit = pipe_size // 2
            while bit > 1:
                got = swap(jnp.stack([part.astype(bf16) for part in own]), "pipe", bit)
                own = [part + got[i].astype(f32) for i, part in enumerate(own)]
                bit //= 2
            got = swap(jnp.stack([part.astype(bf16) for part in own]), "pipe", 1)
            exchanged.append([rows[0, :, width - LANES :], *own, got])
    count = exchanged[0][0].shape[0]

    flipped = [
        call(flip_kernel, shape((d_part, 2 * GROUPS * count), bf16), "v" * (2 * GROUPS), "flip", mib=24)(
            *[rows[a, :, :d_part] for halves in groups for rows in halves]
        )
        for a in range(2)
    ]

    out_width = d_part + LANES
    total = 2 * GROUPS * count
    padded = EXPERTS * slots_here
    half_shape = shape((2, group_size // 4 * pipe_size, padded, out_width), bf16)
    moved = total * (f_part * 24 + d_part * 8) + 4 * d_part * f_part
    operands = [x for piece in exchanged for x in piece]
    *grads, low, high = call(
        functools.partial(hidden_kernel, d_part, top_count, pipe_size),
        (shape((total, f_part), bf16),) * 3 + (half_shape,) * 2,
        "s" + "v" * (len(operands) + 2) + "a" * len(flipped),
        "hidden",
        mib=min(52, 8 + 2 * moved // (1 << 20)),
    )(where, *operands, w_gate, w_up, *flipped)
    piece_shapes = [shape((pipe_size, ROWS, out_width), bf16) for _ in range(EXPERTS)]
    if pipe_size == 2 and group_size == 4:
        parts = call(fold_kernel, [shape((padded, out_width), bf16) for _ in range(4)], "vv", "fold")(
            low, swap(high, "expert", bits[1])
        )
        after = parts[0]
        got_both = swap_both(parts[3], bits[0])
        got_member = swap(parts[2], "expert", bits[0])
        got_pipe = swap(parts[1], "pipe", 1)
        pieces = call(functools.partial(fold_pairs_kernel, slots_here), piece_shapes, "vvvv", "fold_pairs")(
            parts[0], got_member, got_pipe, got_both
        )
    else:
        for bit in reversed(bits[1:]):
            sums = (low.astype(f32) + swap(high, "expert", bit).astype(f32)).astype(bf16)
            low, high = jnp.split(sums, 2, 1) if bit != bits[1] else (sums[0], sums[1])
        sums = (low.astype(f32) + swap(high, "expert", bits[0]).astype(f32)).astype(bf16)
        after = sums
        if pipe_size == 2:
            sums = jnp.stack([sums[0], swap(sums[1], "pipe", 1)])
        else:
            sums = lax.all_to_all(sums, "pipe", split_axis=0, concat_axis=0, tiled=True)
        pieces = [
            jnp.pad(sums[:, k * slots_here : (k + 1) * slots_here], ((0, 0), (0, ROWS - slots_here), (0, 0)))
            for k in range(EXPERTS)
        ]
    pieces = [swap(piece, "expert", k * group_size) if k else piece for k, piece in enumerate(pieces)]

    tokens_total = own_rows * pipe_size * expert_size
    scale = 1.0 / math.sqrt(tokens_total * top_count / EXPERTS)
    block = 256 if d_part % 256 == 0 else d_part
    dw_gate, dw_up, dw_down_t = call(
        functools.partial(weight_kernel, scale, block),
        [shape((d_part, f_part), bf16)] * 3,
        "vvvvva",
        "weight_grads",
        mib=min(52, 12 + (d_part * (total * 4 + f_part * 8) >> 20)),
        out_specs=[pl.BlockSpec(memory_space=pl.ANY)] * 3,
        scratch_shapes=[
            pltpu.VMEM((3, d_part, f_part), bf16),
            pltpu.SemaphoreType.DMA((3, d_part // block)),
        ],
    )(*flipped, *grads, after)

    d_tokens, gate_grads = call(
        functools.partial(owner_kernel, d_part),
        (shape(tokens.shape, bf16), shape((micro_count, top_count, tok_count), f32)),
        "sv" + "v" * EXPERTS,
        "owner",
    )(where, place, *pieces)
    return (d_tokens, jnp.swapaxes(gate_grads, 1, 2), dw_gate, dw_up, dw_down_t)


def solution(mesh):
    rows = P(None, ("pipe", "expert"), None)
    weights = P("pipe", "expert")
    return jax.shard_map(
        on_device,
        mesh=mesh,
        in_specs=(rows, rows, rows, rows, weights, weights, weights),
        out_specs=(rows, rows, weights, weights, weights),
        check_vma=False,
    )
```

```python
import functools
import math

import jax
import jax.numpy as jnp
from jax import lax
from jax.experimental import pallas as pl
from jax.experimental.pallas import tpu as pltpu
from jax.sharding import PartitionSpec as P

EXPERTS = 4
CAP = 3
GROUPS = 2
PER_GROUP = EXPERTS // GROUPS
LANES = 128
ROWS = 8
PIECES = 3
JOIN_COST = dict(flops=4_000_000_000, moved=12_000_000)
f32, bf16, i32 = jnp.float32, jnp.bfloat16, jnp.int32
ROWS_BY_ROWS = (((0,), (0,)), ((), ()))
shape = jax.ShapeDtypeStruct


def swap(x, axis, bit):
    return lax.ppermute(x, axis, [(i, i ^ bit) for i in range(lax.axis_size(axis))])


def swap_both(x, bit):
    count = lax.axis_size("expert")
    pairs = [(p * count + e, (p ^ 1) * count + (e ^ bit)) for p in range(2) for e in range(count)]
    return lax.ppermute(x, ("pipe", "expert"), pairs)


def prep_kernel(d_part, tok_hbm, cot_hbm, ids_hbm, gate_hbm, *refs):
    out_refs, (tok_ref, cot_ref, ids_ref, gate_ref, sems) = refs[:-5], refs[-5:]
    pairs = ((tok_hbm, tok_ref), (cot_hbm, cot_ref), (ids_hbm, ids_ref), (gate_hbm, gate_ref))
    copies = [pltpu.make_async_copy(src, dst, sems.at[i]) for i, (src, dst) in enumerate(pairs)]
    for copy in copies:
        copy.start()
    for copy in copies:
        copy.wait()
    micro_count, tok_count = tok_ref.shape[:2]
    top_count = ids_ref.shape[1]
    seg = out_refs[0].shape[-1] - LANES

    def flat(ref):
        return jnp.concatenate([ref[m].astype(f32) for m in range(micro_count)], 0)

    lane = lax.broadcasted_iota(i32, (tok_count, LANES), 1)
    diagonal = lax.broadcasted_iota(i32, (tok_count, tok_count), 0) == lax.broadcasted_iota(
        i32, (tok_count, tok_count), 1
    )
    blocks = []
    for m in range(micro_count):
        block = jnp.zeros((tok_count, LANES), f32)
        for at, ref in enumerate((ids_ref, gate_ref)):
            values = ref[m].astype(f32)
            for k in range(top_count):
                row = jnp.broadcast_to(values[k : k + 1], (tok_count, tok_count))
                column = jnp.sum(jnp.where(diagonal, row, 0.0), axis=1, keepdims=True)
                block = jnp.where(lane == at * top_count + k, column, block)
        blocks.append(block)
    extras = jnp.concatenate(blocks + blocks, 0).astype(bf16)
    both = jnp.concatenate([flat(tok_ref), flat(cot_ref)], 0).astype(bf16)
    for p, ref in enumerate(out_refs):
        ref[:, :d_part] = both[:, p * d_part : (p + 1) * d_part]
        if seg > d_part:
            ref[:, d_part:seg] = jnp.zeros((both.shape[0], seg - d_part), bf16)
        ref[:, seg:] = extras


def pack_kernel(tok_count, top_count, pipe_size, where_ref, *refs):
    blocks, slot_refs, place_ref = [ref[...] for ref in refs[:pipe_size]], refs[pipe_size:-1], refs[-1]
    both_rows, width = blocks[0].shape
    own_rows = both_rows // 2
    total = pipe_size * both_rows
    slot_count = slot_refs[0].shape[0] // 2
    me = where_ref[0]
    if pipe_size == 2:
        first = where_ref[1] == 0
        blocks = [jnp.where(first, blocks[0], blocks[1]), jnp.where(first, blocks[1], blocks[0])]
    rows = jnp.concatenate(blocks, 0)
    extras = rows[:, width - LANES :].astype(f32)
    row = lax.broadcasted_iota(i32, (total, total), 0)
    other = lax.broadcasted_iota(i32, (total, total), 1)
    earlier = ((other < row) & (other // tok_count == row // tok_count)).astype(bf16)
    at = (lax.broadcasted_iota(i32, (total, LANES), 1) ^ me).astype(f32)
    routed = jnp.zeros((total, LANES), f32)
    for k in range(top_count):
        routed = jnp.where(extras[:, k : k + 1] == at, 1.0, routed)
    position = jnp.dot(earlier, routed.astype(bf16), preferred_element_type=f32)
    index = lax.broadcasted_iota(i32, (total, 1), 0)
    within = index % both_rows
    block = within % own_rows // tok_count
    device = index // both_rows
    base = within // own_rows * slot_count + (device * (own_rows // tok_count) + block) * CAP
    lane = lax.broadcasted_iota(i32, (total, EXPERTS * 2 * slot_count), 1).astype(f32)
    chosen = jnp.zeros(lane.shape, f32)
    small_lane = lax.broadcasted_iota(i32, (total, LANES), 1).astype(f32)
    places = jnp.zeros((total, LANES), f32)
    for k in range(EXPERTS):
        here = routed[:, k : k + 1] > 0.0
        target = (k * 2 * slot_count + base).astype(f32) + position[:, k : k + 1]
        chosen = chosen + jnp.where((lane == target) & here, 1.0, 0.0)
        local = (k * ROWS + block * CAP).astype(f32) + position[:, k : k + 1]
        places = places + jnp.where((small_lane == local) & here, 1.0, 0.0)
    slots = lax.dot_general(chosen.astype(bf16), rows, ROWS_BY_ROWS, preferred_element_type=f32)
    for k in range(EXPERTS):
        slot_refs[k][...] = slots[2 * k * slot_count : 2 * (k + 1) * slot_count].astype(bf16)
    for p in range(pipe_size):
        start = p * both_rows
        place_ref[p, :, :LANES] = places[start : start + own_rows]
        place_ref[p, :, LANES:] = extras[start : start + own_rows]


def join_kernel(pipe_size, *refs):
    blocks, out_ref = [ref[...].astype(f32) for ref in refs[:PER_GROUP]], refs[-1]
    rows = blocks[0].shape[0] // 2 // pipe_size
    for a in range(2):
        starts = [(a * pipe_size + p) * rows for p in range(pipe_size)]
        out_ref[a] = jnp.concatenate([b[s : s + rows] for s in starts for b in blocks], 0).astype(bf16)


def hidden_kernel(d_part, top_count, pipe_size, where_ref, *refs):
    pieces = [refs[5 * i : 5 * (i + 1)] for i in range(PIECES)]
    w_gate, w_up = refs[5 * PIECES : 5 * PIECES + 2]
    d_gate, d_up, scaled, low_back, high_back = refs[-5:]
    me = where_ref[0].astype(f32)
    shares, base = [], 0
    for info, own_g, own_u, own_b, got in pieces:
        count = own_g.shape[0]
        extras = info[...].astype(f32)
        gate = jnp.zeros((count, 1), f32)
        for k in range(top_count):
            gate = gate + jnp.where(
                extras[:, k : k + 1] == me, extras[:, top_count + k : top_count + k + 1], 0.0
            )
        pre_gate = own_g[...] + got[0].astype(f32)
        pre_up = own_u[...] + got[1].astype(f32)
        back_proj = own_b[...] + got[2].astype(f32)
        sig = jax.nn.sigmoid(pre_gate)
        activated = pre_gate * sig
        hidden = activated * pre_up
        shares.append(jnp.sum(back_proj * hidden, axis=1, keepdims=True))
        d_hidden = gate * back_proj
        here = slice(base, base + count)
        base += count
        scaled[here] = (gate * hidden).astype(bf16)
        d_gate[here] = (d_hidden * pre_up * sig * (1.0 + pre_gate * (1.0 - sig))).astype(bf16)
        d_up[here] = (d_hidden * activated).astype(bf16)
    back = jnp.dot(d_gate[...], w_gate[...], preferred_element_type=f32)
    back = back + jnp.dot(d_up[...], w_up[...], preferred_element_type=f32)
    share = jnp.concatenate(shares, 0)
    high = share.astype(bf16).astype(f32)
    lane = lax.broadcasted_iota(i32, (share.shape[0], LANES), 1)
    tail = jnp.where(lane == 0, high, jnp.where(lane == 1, share - high, 0.0))
    members = low_back.shape[1] // pipe_size * 2
    used = count // members // pipe_size
    for h in range(2):
        for member in range(members):
            ref = low_back if member < members // 2 else high_back
            for p in range(pipe_size):
                at_p = (member * pipe_size + p) * used
                between = count + ((2 * member + 1 - h) * pipe_size + p) * used
                starts = [at_p, between] if h == 0 else [between, 3 * count + at_p]
                at = member % (members // 2) * pipe_size + (p ^ where_ref[1] if pipe_size == 2 else p)
                for columns, values in ((slice(0, d_part), back), (slice(d_part, None), tail)):
                    block = jnp.concatenate([values[start : start + used] for start in starts], 0)
                    ref[h, at, :, columns] = block.astype(bf16)


def fold_kernel(a_ref, b_ref, *out_refs):
    for i, ref in enumerate(out_refs):
        here = i // a_ref.shape[1], i % a_ref.shape[1]
        ref[...] = (a_ref[here].astype(f32) + b_ref[here].astype(f32)).astype(bf16)


def fold_pairs_kernel(used, a_ref, b_ref, c_ref, d_ref, *out_refs):
    totals = (
        a_ref[...].astype(f32) + b_ref[...].astype(f32),
        c_ref[...].astype(f32) + d_ref[...].astype(f32),
    )
    for k, ref in enumerate(out_refs):
        for h, total in enumerate(totals):
            rows = total[k * used : (k + 1) * used]
            pad = jnp.zeros((ROWS - used, rows.shape[1]), f32)
            ref[h] = jnp.concatenate([rows, pad], 0).astype(bf16)


def owner_kernel(d_part, where_ref, place_ref, *refs):
    piece_refs, tok_ref, grad_ref = refs[:EXPERTS], refs[EXPERTS], refs[EXPERTS + 1]
    micro_count, tok_count = tok_ref.shape[:2]
    top_count = grad_ref.shape[1]
    pipe_size = piece_refs[0].shape[0]
    mine = place_ref[where_ref[1]]
    place = mine[:, : EXPERTS * ROWS].astype(bf16)
    ids = mine[:, LANES:]
    halves = []
    for h in range(pipe_size):
        rows = jnp.concatenate([ref[h].astype(f32) for ref in piece_refs], 0)
        halves.append(rows)
    sums = [jnp.dot(place, h.astype(bf16), preferred_element_type=f32)[:, :d_part] for h in halves]
    if pipe_size == 2:
        first = where_ref[1] == 0
        sums = [jnp.where(first, sums[0], sums[1]), jnp.where(first, sums[1], sums[0])]
    tail = halves[0][:, d_part:]
    shares = tail[:, 0:1] + tail[:, 1:2]
    slot_lane = lax.broadcasted_iota(i32, place.shape, 1)
    diagonal = lax.broadcasted_iota(i32, (tok_count, tok_count), 0) == lax.broadcasted_iota(
        i32, (tok_count, tok_count), 1
    )
    square = EXPERTS * ROWS
    eye = lax.broadcasted_iota(i32, (square, square), 0) == lax.broadcasted_iota(i32, (square, square), 1)
    share_row = jnp.sum(jnp.where(eye, jnp.broadcast_to(shares, (square, square)), 0.0), axis=0, keepdims=True)
    picked = mine[:, : EXPERTS * ROWS] * share_row
    expert_of = ((slot_lane // ROWS) ^ where_ref[0]).astype(f32)
    for k in range(top_count):
        grad = jnp.sum(jnp.where(expert_of == ids[:, k : k + 1], picked, 0.0), axis=1, keepdims=True)
        for m in range(micro_count):
            part = jnp.broadcast_to(grad[m * tok_count : (m + 1) * tok_count], (tok_count, tok_count))
            grad_ref[m, k : k + 1, :] = jnp.sum(jnp.where(diagonal, part, 0.0), axis=0, keepdims=True)
    for m in range(micro_count):
        for p in range(pipe_size):
            tok_ref[m, :, p * d_part : (p + 1) * d_part] = sums[p][m * tok_count : (m + 1) * tok_count].astype(bf16)


def flip_kernel(*refs):
    refs[-1][...] = jnp.concatenate([ref[...] for ref in refs[:-1]], 0).T


def flip_weight_kernel(weight_ref, after, out_ref):
    del after
    out_ref[...] = weight_ref[...].T


def weight_kernel(scale, block, tok_ref, cot_ref, d_gate, d_up, scaled, after, *refs):
    del after
    out_refs, held, sems = refs[:3], refs[3], refs[4]
    copies = []
    for i in range(tok_ref.shape[0] // block):
        here = slice(i * block, (i + 1) * block)
        for w, (left, right) in enumerate(((tok_ref, d_gate), (tok_ref, d_up), (cot_ref, scaled))):
            rows = jnp.dot(left[here], right[...], preferred_element_type=f32)
            held[w, here] = (rows * scale).astype(bf16)
            copies.append(pltpu.make_async_copy(held.at[w, here], out_refs[w].at[here], sems.at[w, i]))
            copies[-1].start()
    for copy in copies:
        copy.wait()


def tie_kernel(*refs):
    del refs


def call(kernel, out_shape, in_specs, name, mib=8, flops=0, moved=0, **more):
    specs = {"s": pl.BlockSpec(memory_space=pltpu.SMEM), "v": pl.BlockSpec(memory_space=pltpu.VMEM)}
    specs["a"] = pl.BlockSpec(memory_space=pl.ANY)
    specs["h"] = pl.BlockSpec(memory_space=pltpu.HBM)
    more.setdefault("out_specs", jax.tree.map(lambda _: specs["v"], out_shape))
    return pl.pallas_call(
        kernel,
        out_shape=out_shape,
        in_specs=[specs[c] for c in in_specs],
        compiler_params=pltpu.CompilerParams(vmem_limit_bytes=mib << 20),
        cost_estimate=pl.CostEstimate(flops=flops, bytes_accessed=moved, transcendentals=0),
        name=name,
        **more,
    )


def tie(values, after):
    return call(
        tie_kernel,
        [shape(v.shape, v.dtype) for v in values],
        "a" * (len(values) + 1),
        "tie",
        out_specs=[pl.BlockSpec(memory_space=pl.ANY)] * len(values),
        input_output_aliases={i: i for i in range(len(values))},
    )(*values, after)


def on_device(tokens, cotangent, expert_ids, gate_values, w_gate, w_up, w_down_t):
    micro_count, tok_count, d_model = tokens.shape
    top_count = expert_ids.shape[2]
    pipe_size = lax.axis_size("pipe")
    expert_size = lax.axis_size("expert")
    group_size = expert_size // EXPERTS
    bits = [1 << i for i in reversed(range(group_size.bit_length() - 1))]
    d_part, f_part = w_gate.shape
    width = -(-d_part // LANES) * LANES + LANES
    own_rows = micro_count * tok_count
    slots_here = micro_count * CAP
    slot_count = pipe_size * slots_here
    pipe = lax.axis_index("pipe")
    where = jnp.stack([lax.axis_index("expert") // group_size, pipe]).astype(i32)

    inputs = (tokens, cotangent, jnp.swapaxes(expert_ids, 1, 2), jnp.swapaxes(gate_values, 1, 2))
    blocks = call(
        functools.partial(prep_kernel, d_part),
        [shape((2 * own_rows, width), bf16) for _ in range(pipe_size)],
        "aaaa",
        "prep",
        scratch_shapes=[
            pltpu.VMEM(tokens.shape, bf16),
            pltpu.VMEM(tokens.shape, bf16),
            pltpu.VMEM((micro_count, top_count, tok_count), i32),
            pltpu.VMEM((micro_count, top_count, tok_count), bf16),
            pltpu.SemaphoreType.DMA((4,)),
        ],
    )(*[pltpu.with_memory_space_constraint(x, pltpu.HBM) for x in inputs])
    if pipe_size == 2:
        first = pipe == 0
        kept, sent = jnp.where(first, blocks[0], blocks[1]), jnp.where(first, blocks[1], blocks[0])
        blocks = [kept, swap(sent, "pipe", 1)]
    else:
        got = lax.all_to_all(jnp.stack(blocks), "pipe", split_axis=0, concat_axis=0, tiled=True)
        blocks = [got[p] for p in range(pipe_size)]
    *slots, place = call(
        functools.partial(pack_kernel, tok_count, top_count, pipe_size),
        tuple(shape((2 * slot_count, width), bf16) for _ in range(EXPERTS))
        + (shape((pipe_size, own_rows, 2 * LANES), f32),),
        "s" + "v" * pipe_size,
        "pack",
    )(where, *blocks)

    gathered = [slots[0]] + [swap(slots[k], "expert", k * group_size) for k in range(1, EXPERTS)]
    joined = [
        call(
            functools.partial(join_kernel, pipe_size),
            shape((2, PER_GROUP * slot_count, width), bf16),
            "v" * PER_GROUP,
            "join",
            **(JOIN_COST if g else {}),
        )(*gathered[g * PER_GROUP : (g + 1) * PER_GROUP])
        for g in range(GROUPS)
    ]

    def spread(rows):
        for bit in bits[1:]:
            rows = jnp.concatenate([rows, swap(rows, "expert", bit)], 1)
        return rows

    def project(rows):
        tok_rows, cot_rows = rows[0, :, :d_part], rows[1, :, :d_part]
        own = []
        for left, weight in ((tok_rows, w_gate), (tok_rows, w_up), (cot_rows, w_down_t)):
            own.append(jnp.dot(left, weight, preferred_element_type=f32))
        return own

    def exchange(rows, own):
        bit = pipe_size // 2
        while bit > 1:
            got = swap(jnp.stack([part.astype(bf16) for part in own]), "pipe", bit)
            own = [part + got[i].astype(f32) for i, part in enumerate(own)]
            bit //= 2
        got = swap(jnp.stack([part.astype(bf16) for part in own]), "pipe", 1)
        return [rows[0, :, width - LANES :], *own, got]

    there = swap(joined[0], "expert", bits[0])
    later = tie([joined[1]], there)[0]
    later_there = swap(later, "expert", bits[0])
    first = spread(joined[0])
    first_own = project(first)
    middle = spread(jnp.concatenate([there, later], 1))
    middle_own = project(middle)
    last = spread(tie([later_there], middle_own[2])[0])
    pieces, owns = [first, middle, last], [first_own, middle_own, project(last)]
    exchanged = [exchange(rows, own) for rows, own in zip(pieces, owns)]
    total = sum(piece[0].shape[0] for piece in exchanged)

    flipped = [
        call(flip_kernel, shape((d_part, total), bf16), "v" * len(pieces), "flip", mib=24)(
            *[rows[a, :, :d_part] for rows in pieces]
        )
        for a in range(2)
    ]

    flipped_weights = [
        call(flip_weight_kernel, shape((f_part, d_part), bf16), "va", "flip_weight", mib=24)(w, exchanged[-1][3])
        for w in (w_gate, w_up)
    ]

    out_width = d_part + LANES
    padded = EXPERTS * slots_here
    half_shape = shape((2, group_size // 4 * pipe_size, padded, out_width), bf16)
    moved = total * (f_part * 24 + d_part * 8) + 4 * d_part * f_part
    operands = [x for piece in exchanged for x in piece]
    *grads, low, high = call(
        functools.partial(hidden_kernel, d_part, top_count, pipe_size),
        (shape((total, f_part), bf16),) * 3 + (half_shape,) * 2,
        "s" + "v" * (len(operands) + 2) + "a" * len(flipped),
        "hidden",
        mib=min(52, 8 + 2 * moved // (1 << 20)),
    )(where, *operands, *flipped_weights, *flipped)
    piece_shapes = [shape((pipe_size, ROWS, out_width), bf16) for _ in range(EXPERTS)]
    if pipe_size == 2 and group_size == 4:
        parts = call(fold_kernel, [shape((padded, out_width), bf16) for _ in range(4)], "vv", "fold")(
            low, swap(high, "expert", bits[1])
        )
        after = parts[0]
        got_both = swap_both(parts[3], bits[0])
        got_member = swap(parts[2], "expert", bits[0])
        got_pipe = swap(parts[1], "pipe", 1)
        contributions = call(functools.partial(fold_pairs_kernel, slots_here), piece_shapes, "vvvv", "fold_pairs")(
            parts[0], got_member, got_pipe, got_both
        )
    else:
        for bit in reversed(bits[1:]):
            sums = (low.astype(f32) + swap(high, "expert", bit).astype(f32)).astype(bf16)
            low, high = jnp.split(sums, 2, 1) if bit != bits[1] else (sums[0], sums[1])
        sums = (low.astype(f32) + swap(high, "expert", bits[0]).astype(f32)).astype(bf16)
        after = sums
        if pipe_size == 2:
            sums = jnp.stack([sums[0], swap(sums[1], "pipe", 1)])
        else:
            sums = lax.all_to_all(sums, "pipe", split_axis=0, concat_axis=0, tiled=True)
        contributions = [
            jnp.pad(sums[:, k * slots_here : (k + 1) * slots_here], ((0, 0), (0, ROWS - slots_here), (0, 0)))
            for k in range(EXPERTS)
        ]
    contributions = [swap(x, "expert", k * group_size) if k else x for k, x in enumerate(contributions)]

    tokens_total = own_rows * pipe_size * expert_size
    scale = 1.0 / math.sqrt(tokens_total * top_count / EXPERTS)
    block = 256 if d_part % 256 == 0 else d_part
    dw_gate, dw_up, dw_down_t = call(
        functools.partial(weight_kernel, scale, block),
        [shape((d_part, f_part), bf16)] * 3,
        "vvvvva",
        "weight_grads",
        mib=min(52, 12 + (d_part * (total * 4 + f_part * 8) >> 20)),
        out_specs=[pl.BlockSpec(memory_space=pl.ANY)] * 3,
        scratch_shapes=[
            pltpu.VMEM((3, d_part, f_part), bf16),
            pltpu.SemaphoreType.DMA((3, d_part // block)),
        ],
    )(*flipped, *grads, after)

    d_tokens, gate_grads = call(
        functools.partial(owner_kernel, d_part),
        (shape(tokens.shape, bf16), shape((micro_count, top_count, tok_count), f32)),
        "sv" + "v" * EXPERTS,
        "owner",
    )(where, place, *contributions)
    return (d_tokens, jnp.swapaxes(gate_grads, 1, 2), dw_gate, dw_up, dw_down_t)


def solution(mesh):
    rows = P(None, ("pipe", "expert"), None)
    weights = P("pipe", "expert")
    return jax.shard_map(
        on_device,
        mesh=mesh,
        in_specs=(rows, rows, rows, rows, weights, weights, weights),
        out_specs=(rows, rows, weights, weights, weights),
        check_vma=False,
    )
```

```python
import functools
import math

import jax
import jax.numpy as jnp
from jax import lax
from jax.experimental import pallas as pl
from jax.experimental.pallas import tpu as pltpu
from jax.sharding import PartitionSpec as P

EXPERTS = 4
CAP = 3
GROUPS = 2
PER_GROUP = EXPERTS // GROUPS
LANES = 128
ROWS = 8
PIECES = 3
SQUARE = EXPERTS * ROWS
RETURN_ORDER = (0, 2, 3, 1)
JOIN_COST = dict(flops=4_000_000_000, moved=12_000_000)
f32, bf16, i32 = jnp.float32, jnp.bfloat16, jnp.int32
ROWS_BY_ROWS = (((0,), (0,)), ((), ()))
shape = jax.ShapeDtypeStruct


def swap(x, axis, bit):
    return lax.ppermute(x, axis, [(i, i ^ bit) for i in range(lax.axis_size(axis))])


def swap_both(x, bit):
    count = lax.axis_size("expert")
    pairs = [(p * count + e, (p ^ 1) * count + (e ^ bit)) for p in range(2) for e in range(count)]
    return lax.ppermute(x, ("pipe", "expert"), pairs)


def prep_kernel(d_part, tok_hbm, cot_hbm, ids_hbm, gate_hbm, *refs):
    out_refs, (tok_ref, cot_ref, ids_ref, gate_ref, sems) = refs[:-5], refs[-5:]
    pairs = ((tok_hbm, tok_ref), (cot_hbm, cot_ref), (ids_hbm, ids_ref), (gate_hbm, gate_ref))
    copies = [pltpu.make_async_copy(src, dst, sems.at[i]) for i, (src, dst) in enumerate(pairs)]
    for copy in copies:
        copy.start()
    for copy in copies:
        copy.wait()
    micro_count, tok_count = tok_ref.shape[:2]
    top_count = ids_ref.shape[1]
    seg = out_refs[0].shape[-1] - LANES

    def flat(ref):
        return jnp.concatenate([ref[m].astype(f32) for m in range(micro_count)], 0)

    lane = lax.broadcasted_iota(i32, (tok_count, LANES), 1)
    diagonal = lax.broadcasted_iota(i32, (tok_count, tok_count), 0) == lax.broadcasted_iota(
        i32, (tok_count, tok_count), 1
    )
    blocks = []
    for m in range(micro_count):
        block = jnp.zeros((tok_count, LANES), f32)
        for at, ref in enumerate((ids_ref, gate_ref)):
            values = ref[m].astype(f32)
            for k in range(top_count):
                row = jnp.broadcast_to(values[k : k + 1], (tok_count, tok_count))
                column = jnp.sum(jnp.where(diagonal, row, 0.0), axis=1, keepdims=True)
                block = jnp.where(lane == at * top_count + k, column, block)
        blocks.append(block)
    extras = jnp.concatenate(blocks + blocks, 0).astype(bf16)
    both = jnp.concatenate([flat(tok_ref), flat(cot_ref)], 0).astype(bf16)
    for p, ref in enumerate(out_refs):
        ref[:, :d_part] = both[:, p * d_part : (p + 1) * d_part]
        if seg > d_part:
            ref[:, d_part:seg] = jnp.zeros((both.shape[0], seg - d_part), bf16)
        ref[:, seg:] = extras


def pack_kernel(tok_count, top_count, pipe_size, where_ref, *refs):
    blocks, slot_refs, place_ref = [ref[...] for ref in refs[:pipe_size]], refs[pipe_size:-1], refs[-1]
    both_rows, width = blocks[0].shape
    own_rows = both_rows // 2
    total = pipe_size * both_rows
    slot_count = slot_refs[0].shape[0] // 2
    me = where_ref[0]
    if pipe_size == 2:
        first = where_ref[1] == 0
        blocks = [jnp.where(first, blocks[0], blocks[1]), jnp.where(first, blocks[1], blocks[0])]
    rows = jnp.concatenate(blocks, 0)
    extras = rows[:, width - LANES :].astype(f32)
    row = lax.broadcasted_iota(i32, (total, total), 0)
    other = lax.broadcasted_iota(i32, (total, total), 1)
    earlier = ((other < row) & (other // tok_count == row // tok_count)).astype(bf16)
    at = (lax.broadcasted_iota(i32, (total, LANES), 1) ^ me).astype(f32)
    routed = jnp.zeros((total, LANES), f32)
    for k in range(top_count):
        routed = jnp.where(extras[:, k : k + 1] == at, 1.0, routed)
    position = jnp.dot(earlier, routed.astype(bf16), preferred_element_type=f32)
    index = lax.broadcasted_iota(i32, (total, 1), 0)
    within = index % both_rows
    block = within % own_rows // tok_count
    device = index // both_rows
    base = within // own_rows * slot_count + (device * (own_rows // tok_count) + block) * CAP
    lane = lax.broadcasted_iota(i32, (total, EXPERTS * 2 * slot_count), 1).astype(f32)
    chosen = jnp.zeros(lane.shape, f32)
    small_lane = lax.broadcasted_iota(i32, (total, LANES), 1)
    used = own_rows // tok_count * CAP
    per_row = used // (ROWS - used)
    places = jnp.zeros((total, LANES), f32)
    for k in range(EXPERTS):
        here = routed[:, k : k + 1] > 0.0
        target = (k * 2 * slot_count + base).astype(f32) + position[:, k : k + 1]
        chosen = chosen + jnp.where((lane == target) & here, 1.0, 0.0)
        local = block * CAP + position[:, k : k + 1].astype(i32)
        spare = SQUARE * (1 + local % per_row) + k * ROWS + used + local // per_row
        at_slot = (small_lane == k * ROWS + local) | (small_lane == spare)
        places = places + jnp.where(at_slot & here, 1.0, 0.0)
    slots = lax.dot_general(chosen.astype(bf16), rows, ROWS_BY_ROWS, preferred_element_type=f32)
    for k in range(EXPERTS):
        slot_refs[k][...] = slots[2 * k * slot_count : 2 * (k + 1) * slot_count].astype(bf16)
    for p in range(pipe_size):
        start = p * both_rows
        place_ref[p, :, :LANES] = places[start : start + own_rows]
        place_ref[p, :, LANES:] = extras[start : start + own_rows]


def join_kernel(pipe_size, *refs):
    blocks, out_ref = [ref[...].astype(f32) for ref in refs[:PER_GROUP]], refs[-1]
    rows = blocks[0].shape[0] // 2 // pipe_size
    for a in range(2):
        starts = [(a * pipe_size + p) * rows for p in range(pipe_size)]
        out_ref[a] = jnp.concatenate([b[s : s + rows] for s in starts for b in blocks], 0).astype(bf16)


def hidden_gradients(top_count, me, info, own_g, own_u, own_b, got):
    extras = info[...].astype(f32)
    gate = jnp.zeros((extras.shape[0], 1), f32)
    for k in range(top_count):
        gate = gate + jnp.where(extras[:, k : k + 1] == me, extras[:, top_count + k : top_count + k + 1], 0.0)
    pre_gate = own_g[...] + got[0].astype(f32)
    pre_up = own_u[...] + got[1].astype(f32)
    back_proj = own_b[...] + got[2].astype(f32)
    sig = jax.nn.sigmoid(pre_gate)
    activated = pre_gate * sig
    hidden = activated * pre_up
    share = jnp.sum(back_proj * hidden, axis=1, keepdims=True)
    high = share.astype(bf16).astype(f32)
    lane = lax.broadcasted_iota(i32, (share.shape[0], LANES), 1)
    tail = jnp.where(lane == 0, high, jnp.where(lane == 1, share - high, 0.0))
    d_hidden = gate * back_proj
    d_gate = d_hidden * pre_up * sig * (1.0 + pre_gate * (1.0 - sig))
    return d_gate, d_hidden * activated, gate * hidden, tail


def store_halves(values, refs):
    for value, ref in zip(values, refs):
        half = value.shape[0] // 2
        ref[0] = value[:half].astype(bf16)
        ref[1] = value[half:].astype(bf16)


def act_kernel(top_count, where_ref, *refs):
    store_halves(hidden_gradients(top_count, where_ref[0].astype(f32), *refs[:5]), refs[6:])


def back_rows(d_part, pipe_size, where_ref, grads, w_gate, w_up, out_ref):
    left = [jnp.concatenate([g[i].astype(f32) for g in grads], 0) for i in (0, 1, 3)]
    back = jnp.dot(left[0].astype(bf16), w_gate[...], preferred_element_type=f32)
    back = back + jnp.dot(left[1].astype(bf16), w_up[...], preferred_element_type=f32)
    count = back.shape[0] // 4
    members = out_ref.shape[1] // pipe_size
    used = count // members // pipe_size
    for h in range(2):
        for member in range(members):
            for p in range(pipe_size):
                at_p = (member * pipe_size + p) * used
                between = count + ((2 * member + 1 - h) * pipe_size + p) * used
                starts = [at_p, between] if h == 0 else [between, 3 * count + at_p]
                at = member * pipe_size + (p ^ where_ref[1] if pipe_size == 2 else p)
                for columns, values in ((slice(0, d_part), back), (slice(d_part, None), left[2])):
                    block = jnp.concatenate([values[start : start + used] for start in starts], 0)
                    out_ref[h, at, :, columns] = block.astype(bf16)


def last_act_kernel(d_part, top_count, pipe_size, where_ref, *refs):
    raw, first, middle, (w_gate, w_up), outs = refs[:5], refs[5:9], refs[9:13], refs[13:15], refs[-5:]
    last = hidden_gradients(top_count, where_ref[0].astype(f32), *raw)
    store_halves(last, outs[:4])
    half = last[0].shape[0] // 2
    grads = [[ref[1] for ref in first], [ref[1] for ref in middle], [value[half:] for value in last]]
    back_rows(d_part, pipe_size, where_ref, grads, w_gate, w_up, outs[4])


def own_back_kernel(d_part, pipe_size, where_ref, *refs):
    grads = [[ref[0] for ref in refs[4 * i : 4 * i + 4]] for i in range(PIECES)]
    back_rows(d_part, pipe_size, where_ref, grads, *refs[4 * PIECES : 4 * PIECES + 2], refs[-1])


def fold_kernel(a_ref, b_ref, *out_refs):
    for i, ref in enumerate(out_refs):
        here = i // a_ref.shape[1], i % a_ref.shape[1]
        ref[...] = (a_ref[here].astype(f32) + b_ref[here].astype(f32)).astype(bf16)


def pack_slots(used, columns, tail):
    main = columns.shape[1] // 4 * 3
    per_row = used // (ROWS - used)
    spare = [
        jnp.concatenate([columns[r * per_row + j : r * per_row + j + 1, main:] for j in range(per_row)], 1)
        for r in range(ROWS - used)
    ]
    rows = jnp.concatenate([columns[:, :main]] + spare, 0)
    tail = jnp.concatenate([tail, jnp.zeros((ROWS - used, LANES), f32)], 0)
    return jnp.concatenate([rows, tail], 1)


def fold_pairs_kernel(used, d_part, a_ref, b_ref, c_ref, d_ref, *out_refs):
    here = a_ref[...].astype(f32) + d_ref[...].astype(f32)
    there = b_ref[...].astype(f32) + c_ref[...].astype(f32)
    for k, ref in enumerate(out_refs):
        at = slice(k * used, (k + 1) * used)
        columns = jnp.concatenate([here[at, :d_part], there[at, :d_part]], 1)
        ref[...] = pack_slots(used, columns, here[at, d_part:]).astype(bf16)


def owner_kernel(d_part, packed, where_ref, place_ref, *refs):
    piece_refs, tok_ref, grad_ref = refs[:EXPERTS], refs[EXPERTS], refs[EXPERTS + 1]
    piece_refs = [piece_refs[RETURN_ORDER.index(k)] for k in range(EXPERTS)]
    micro_count, tok_count, d_model = tok_ref.shape
    top_count = grad_ref.shape[1]
    mine = place_ref[where_ref[1]]
    places = mine[:, :LANES].astype(bf16)
    place = places[:, :SQUARE]
    ids = mine[:, LANES:]
    rows = jnp.concatenate([ref[...].astype(f32) for ref in piece_refs], 0).astype(bf16)
    wide = rows.shape[1] - LANES
    out = jnp.dot(place, rows[:, :wide], preferred_element_type=f32)
    if packed:
        rest, quarter = 0.0, d_model - wide
        for j in range(wide // quarter):
            spare = places[:, (1 + j) * SQUARE : (2 + j) * SQUARE]
            columns = rows[:, j * quarter : (j + 1) * quarter]
            rest = rest + jnp.dot(spare, columns, preferred_element_type=f32)
        out = jnp.concatenate([out, rest], 1)
        first = where_ref[1] == 0
        here, there = out[:, :d_part], out[:, d_part:]
        out = jnp.concatenate([jnp.where(first, here, there), jnp.where(first, there, here)], 1)
    for m in range(micro_count):
        tok_ref[m] = out[m * tok_count : (m + 1) * tok_count].astype(bf16)

    expert_of = ((lax.broadcasted_iota(i32, place.shape, 1) // ROWS) ^ where_ref[0]).astype(f32)
    diagonal = lax.broadcasted_iota(i32, (tok_count, tok_count), 0) == lax.broadcasted_iota(
        i32, (tok_count, tok_count), 1
    )
    for k in range(top_count):
        picked = jnp.where(expert_of == ids[:, k : k + 1], mine[:, :SQUARE], 0.0).astype(bf16)
        grad = jnp.dot(picked, rows[:, wide:], preferred_element_type=f32)
        grad = grad[:, 0:1] + grad[:, 1:2]
        for m in range(micro_count):
            part = jnp.broadcast_to(grad[m * tok_count : (m + 1) * tok_count], (tok_count, tok_count))
            grad_ref[m, k : k + 1, :] = jnp.sum(jnp.where(diagonal, part, 0.0), axis=0, keepdims=True)


def flip_kernel(*refs):
    refs[-1][...] = jnp.concatenate([ref[...] for ref in refs[:-1]], 0).T


def flip_weight_kernel(weight_ref, after, out_ref):
    del after
    out_ref[...] = weight_ref[...].T


def weight_kernel(scale, block, tok_ref, cot_ref, *refs):
    pieces, (out_refs, held, sems) = refs[: 3 * PIECES], (refs[-5:-2], refs[-2], refs[-1])
    rights = []
    for w in range(3):
        halves = [ref[h].astype(f32) for ref in pieces[w::3] for h in range(2)]
        rights.append(jnp.concatenate(halves, 0).astype(bf16))
    copies = []
    for i in range(tok_ref.shape[0] // block):
        here = slice(i * block, (i + 1) * block)
        for w, left in enumerate((tok_ref, tok_ref, cot_ref)):
            rows = jnp.dot(left[here], rights[w], preferred_element_type=f32)
            held[w, here] = (rows * scale).astype(bf16)
            copies.append(pltpu.make_async_copy(held.at[w, here], out_refs[w].at[here], sems.at[w, i]))
            copies[-1].start()
    for copy in copies:
        copy.wait()


def tie_kernel(*refs):
    del refs


def call(kernel, out_shape, in_specs, name, mib=8, flops=0, moved=0, **more):
    specs = {"s": pl.BlockSpec(memory_space=pltpu.SMEM), "v": pl.BlockSpec(memory_space=pltpu.VMEM)}
    specs["a"] = pl.BlockSpec(memory_space=pl.ANY)
    specs["h"] = pl.BlockSpec(memory_space=pltpu.HBM)
    more.setdefault("out_specs", jax.tree.map(lambda _: specs["v"], out_shape))
    return pl.pallas_call(
        kernel,
        out_shape=out_shape,
        in_specs=[specs[c] for c in in_specs],
        compiler_params=pltpu.CompilerParams(vmem_limit_bytes=mib << 20),
        cost_estimate=pl.CostEstimate(flops=flops, bytes_accessed=moved, transcendentals=0),
        name=name,
        **more,
    )


def tie(values, after):
    return call(
        tie_kernel,
        [shape(v.shape, v.dtype) for v in values],
        "a" * (len(values) + 1),
        "tie",
        out_specs=[pl.BlockSpec(memory_space=pl.ANY)] * len(values),
        input_output_aliases={i: i for i in range(len(values))},
    )(*values, after)


def on_device(tokens, cotangent, expert_ids, gate_values, w_gate, w_up, w_down_t):
    micro_count, tok_count, d_model = tokens.shape
    top_count = expert_ids.shape[2]
    pipe_size = lax.axis_size("pipe")
    expert_size = lax.axis_size("expert")
    group_size = expert_size // EXPERTS
    bits = [1 << i for i in reversed(range(group_size.bit_length() - 1))]
    d_part, f_part = w_gate.shape
    width = -(-d_part // LANES) * LANES + LANES
    own_rows = micro_count * tok_count
    slots_here = micro_count * CAP
    slot_count = pipe_size * slots_here
    pipe = lax.axis_index("pipe")
    where = jnp.stack([lax.axis_index("expert") // group_size, pipe]).astype(i32)

    inputs = (tokens, cotangent, jnp.swapaxes(expert_ids, 1, 2), jnp.swapaxes(gate_values, 1, 2))
    blocks = call(
        functools.partial(prep_kernel, d_part),
        [shape((2 * own_rows, width), bf16) for _ in range(pipe_size)],
        "aaaa",
        "prep",
        scratch_shapes=[
            pltpu.VMEM(tokens.shape, bf16),
            pltpu.VMEM(tokens.shape, bf16),
            pltpu.VMEM((micro_count, top_count, tok_count), i32),
            pltpu.VMEM((micro_count, top_count, tok_count), bf16),
            pltpu.SemaphoreType.DMA((4,)),
        ],
    )(*[pltpu.with_memory_space_constraint(x, pltpu.HBM) for x in inputs])
    if pipe_size == 2:
        first = pipe == 0
        kept, sent = jnp.where(first, blocks[0], blocks[1]), jnp.where(first, blocks[1], blocks[0])
        blocks = [kept, swap(sent, "pipe", 1)]
    else:
        got = lax.all_to_all(jnp.stack(blocks), "pipe", split_axis=0, concat_axis=0, tiled=True)
        blocks = [got[p] for p in range(pipe_size)]
    *slots, place = call(
        functools.partial(pack_kernel, tok_count, top_count, pipe_size),
        tuple(shape((2 * slot_count, width), bf16) for _ in range(EXPERTS))
        + (shape((pipe_size, own_rows, 2 * LANES), f32),),
        "s" + "v" * pipe_size,
        "pack",
    )(where, *blocks)

    gathered = [slots[0]] + [swap(slots[k], "expert", k * group_size) for k in range(1, EXPERTS)]
    joined = [
        call(
            functools.partial(join_kernel, pipe_size),
            shape((2, PER_GROUP * slot_count, width), bf16),
            "v" * PER_GROUP,
            "join",
            **(JOIN_COST if g else {}),
        )(*gathered[g * PER_GROUP : (g + 1) * PER_GROUP])
        for g in range(GROUPS)
    ]

    def spread(rows):
        for bit in bits[1:]:
            rows = jnp.concatenate([rows, swap(rows, "expert", bit)], 1)
        return rows

    def project(rows):
        tok_rows, cot_rows = rows[0, :, :d_part], rows[1, :, :d_part]
        own = []
        for left, weight in ((tok_rows, w_gate), (tok_rows, w_up), (cot_rows, w_down_t)):
            own.append(jnp.dot(left, weight, preferred_element_type=f32))
        return own

    def exchange(rows, own):
        bit = pipe_size // 2
        while bit > 1:
            got = swap(jnp.stack([part.astype(bf16) for part in own]), "pipe", bit)
            own = [part + got[i].astype(f32) for i, part in enumerate(own)]
            bit //= 2
        got = swap(jnp.stack([part.astype(bf16) for part in own]), "pipe", 1)
        return [rows[0, :, width - LANES :], *own, got]

    there = swap(joined[0], "expert", bits[0])
    later = tie([joined[1]], there)[0]
    later_there = swap(later, "expert", bits[0])
    first = spread(joined[0])
    first_own = project(first)
    middle = spread(jnp.concatenate([there, later], 1))
    middle_own = project(middle)
    last = spread(tie([later_there], middle_own[2])[0])
    pieces, owns = [first, middle, last], [first_own, middle_own, project(last)]
    exchanged = [exchange(rows, own) for rows, own in zip(pieces, owns)]
    total = sum(piece[0].shape[0] for piece in exchanged)

    flipped = [
        call(flip_kernel, shape((d_part, total), bf16), "v" * len(pieces), "flip", mib=24)(
            *[rows[a, :, :d_part] for rows in pieces]
        )
        for a in range(2)
    ]

    flipped_weights = [
        call(flip_weight_kernel, shape((f_part, d_part), bf16), "va", "flip_weight", mib=24)(w, exchanged[-1][3])
        for w in (w_gate, w_up)
    ]

    out_width = d_part + LANES
    padded = EXPERTS * slots_here
    half_shape = shape((2, group_size // 4 * pipe_size, padded, out_width), bf16)
    moved = total * (f_part * 24 + d_part * 8) + 4 * d_part * f_part
    mib = min(52, 8 + 2 * moved // (1 << 20))

    def grad_shapes(piece):
        rows = piece[0].shape[0] // 2
        return [shape((2, rows, f_part), bf16)] * 3 + [shape((2, rows, LANES), bf16)]

    grads = [
        call(functools.partial(act_kernel, top_count), grad_shapes(piece), "svvvvva", "act", mib=mib)(
            where, *piece, exchanged[-1][3]
        )
        for piece in exchanged[:-1]
    ]
    *last_grad, high = call(
        functools.partial(last_act_kernel, d_part, top_count, pipe_size),
        grad_shapes(exchanged[-1]) + [half_shape],
        "s" + "v" * 15 + "a" * len(flipped),
        "last_act",
        mib=mib,
    )(where, *exchanged[-1], *grads[0], *grads[1], *flipped_weights, *flipped)
    grads.append(last_grad)
    low = call(
        functools.partial(own_back_kernel, d_part, pipe_size),
        half_shape,
        "s" + "v" * (4 * PIECES + 2) + "a",
        "own_back",
        mib=mib,
    )(where, *[x for grad in grads for x in grad], *flipped_weights, high)
    packed = pipe_size == 2 and group_size == 4
    if packed:
        parts = call(fold_kernel, [shape((padded, out_width), bf16) for _ in range(4)], "vv", "fold")(
            low, swap(high, "expert", bits[1])
        )
        after = parts[0]
        got_both = swap_both(parts[3], bits[0])
        got_member = swap(parts[2], "expert", bits[0])
        got_pipe = swap(parts[1], "pipe", 1)
        contributions = call(
            functools.partial(fold_pairs_kernel, slots_here, d_part),
            [shape((ROWS, d_model // 4 * 3 + LANES), bf16) for _ in range(EXPERTS)],
            "vvvv",
            "fold_pairs",
        )(parts[0], got_both, got_pipe, got_member)
    else:
        for bit in reversed(bits[1:]):
            sums = (low.astype(f32) + swap(high, "expert", bit).astype(f32)).astype(bf16)
            low, high = jnp.split(sums, 2, 1) if bit != bits[1] else (sums[0], sums[1])
        sums = (low.astype(f32) + swap(high, "expert", bits[0]).astype(f32)).astype(bf16)
        after = sums
        if pipe_size == 2:
            got = swap(sums[1], "pipe", 1)
            sums = jnp.where(pipe == 0, jnp.stack([sums[0], got]), jnp.stack([got, sums[0]]))
        else:
            sums = lax.all_to_all(sums, "pipe", split_axis=0, concat_axis=0, tiled=True)
        wide = jnp.swapaxes(sums[:, :, :d_part], 0, 1).reshape(padded, d_model)
        wide = jnp.concatenate([wide, sums[0, :, d_part:]], 1)
        contributions = [
            jnp.pad(wide[k * slots_here : (k + 1) * slots_here], ((0, ROWS - slots_here), (0, 0)))
            for k in range(EXPERTS)
        ]
    contributions = [swap(x, "expert", k * group_size) if k else x for k, x in enumerate(contributions)]

    tokens_total = own_rows * pipe_size * expert_size
    scale = 1.0 / math.sqrt(tokens_total * top_count / EXPERTS)
    block = 256 if d_part % 256 == 0 else d_part
    dw_gate, dw_up, dw_down_t = call(
        functools.partial(weight_kernel, scale, block),
        [shape((d_part, f_part), bf16)] * 3,
        "vv" + "v" * (3 * PIECES) + "a",
        "weight_grads",
        mib=min(52, 12 + (d_part * (total * 4 + f_part * 8) >> 20)),
        out_specs=[pl.BlockSpec(memory_space=pl.ANY)] * 3,
        scratch_shapes=[
            pltpu.VMEM((3, d_part, f_part), bf16),
            pltpu.SemaphoreType.DMA((3, d_part // block)),
        ],
    )(*flipped, *[x for grad in grads for x in grad[:3]], after)

    d_tokens, gate_grads = call(
        functools.partial(owner_kernel, d_part, packed),
        (shape(tokens.shape, bf16), shape((micro_count, top_count, tok_count), f32)),
        "sv" + "v" * EXPERTS,
        "owner",
    )(where, place, *[contributions[k] for k in RETURN_ORDER])
    return (d_tokens, jnp.swapaxes(gate_grads, 1, 2), dw_gate, dw_up, dw_down_t)


def solution(mesh):
    rows = P(None, ("pipe", "expert"), None)
    weights = P("pipe", "expert")
    return jax.shard_map(
        on_device,
        mesh=mesh,
        in_specs=(rows, rows, rows, rows, weights, weights, weights),
        out_specs=(rows, rows, weights, weights, weights),
        check_vma=False,
    )
```

```python
import functools
import math

import jax
import jax.numpy as jnp
from jax import lax
from jax.experimental import pallas as pl
from jax.experimental.pallas import tpu as pltpu
from jax.sharding import PartitionSpec as P

EXPERTS = 4
CAP = 3
GROUPS = 2
PER_GROUP = EXPERTS // GROUPS
LANES = 128
ROWS = 8
PIECES = 4
SQUARE = EXPERTS * ROWS
RETURN_ORDER = (0, 2, 3, 1)
JOIN_COST = dict(flops=4000000000, moved=12000000)
FILL_A = dict(flops=8000000000, moved=24000000)
FILL_B = dict(flops=8_000_000_000, moved=24_000_000)
f32, bf16, i32 = jnp.float32, jnp.bfloat16, jnp.int32
ROWS_BY_ROWS = (((0,), (0,)), ((), ()))
shape = jax.ShapeDtypeStruct


def swap(x, axis, bit):
    return lax.ppermute(x, axis, [(i, i ^ bit) for i in range(lax.axis_size(axis))])


def swap_both(x, bit):
    count = lax.axis_size("expert")
    pairs = [(p * count + e, (p ^ 1) * count + (e ^ bit)) for p in range(2) for e in range(count)]
    return lax.ppermute(x, ("pipe", "expert"), pairs)


def prep_kernel(d_part, tok_hbm, cot_hbm, ids_hbm, gate_hbm, *refs):
    out_refs, (tok_ref, cot_ref, ids_ref, gate_ref, sems) = refs[:-5], refs[-5:]
    pairs = ((tok_hbm, tok_ref), (cot_hbm, cot_ref), (ids_hbm, ids_ref), (gate_hbm, gate_ref))
    copies = [pltpu.make_async_copy(src, dst, sems.at[i]) for i, (src, dst) in enumerate(pairs)]
    for copy in copies:
        copy.start()
    for copy in copies:
        copy.wait()
    micro_count, tok_count = tok_ref.shape[:2]
    top_count = ids_ref.shape[1]
    seg = out_refs[0].shape[-1] - LANES

    def flat(ref):
        return jnp.concatenate([ref[m].astype(f32) for m in range(micro_count)], 0)

    lane = lax.broadcasted_iota(i32, (tok_count, LANES), 1)
    diagonal = lax.broadcasted_iota(i32, (tok_count, tok_count), 0) == lax.broadcasted_iota(
        i32, (tok_count, tok_count), 1
    )
    blocks = []
    for m in range(micro_count):
        block = jnp.zeros((tok_count, LANES), f32)
        for at, ref in enumerate((ids_ref, gate_ref)):
            values = ref[m].astype(f32)
            for k in range(top_count):
                row = jnp.broadcast_to(values[k : k + 1], (tok_count, tok_count))
                column = jnp.sum(jnp.where(diagonal, row, 0.0), axis=1, keepdims=True)
                block = jnp.where(lane == at * top_count + k, column, block)
        blocks.append(block)
    extras = jnp.concatenate(blocks + blocks, 0).astype(bf16)
    both = jnp.concatenate([flat(tok_ref), flat(cot_ref)], 0).astype(bf16)
    for p, ref in enumerate(out_refs):
        ref[:, :d_part] = both[:, p * d_part : (p + 1) * d_part]
        if seg > d_part:
            ref[:, d_part:seg] = jnp.zeros((both.shape[0], seg - d_part), bf16)
        ref[:, seg:] = extras


def pack_kernel(tok_count, top_count, pipe_size, where_ref, *refs):
    blocks, slot_refs, place_ref = [ref[...] for ref in refs[:pipe_size]], refs[pipe_size:-1], refs[-1]
    both_rows, width = blocks[0].shape
    own_rows = both_rows // 2
    total = pipe_size * both_rows
    slot_count = slot_refs[0].shape[0] // 2
    me = where_ref[0]
    if pipe_size == 2:
        first = where_ref[1] == 0
        blocks = [jnp.where(first, blocks[0], blocks[1]), jnp.where(first, blocks[1], blocks[0])]
    rows = jnp.concatenate(blocks, 0)
    extras = rows[:, width - LANES :].astype(f32)
    row = lax.broadcasted_iota(i32, (total, total), 0)
    other = lax.broadcasted_iota(i32, (total, total), 1)
    earlier = ((other < row) & (other // tok_count == row // tok_count)).astype(bf16)
    at = (lax.broadcasted_iota(i32, (total, LANES), 1) ^ me).astype(f32)
    routed = jnp.zeros((total, LANES), f32)
    for k in range(top_count):
        routed = jnp.where(extras[:, k : k + 1] == at, 1.0, routed)
    position = jnp.dot(earlier, routed.astype(bf16), preferred_element_type=f32)
    index = lax.broadcasted_iota(i32, (total, 1), 0)
    within = index % both_rows
    block = within % own_rows // tok_count
    device = index // both_rows
    base = within // own_rows * slot_count + (device * (own_rows // tok_count) + block) * CAP
    lane = lax.broadcasted_iota(i32, (total, EXPERTS * 2 * slot_count), 1).astype(f32)
    chosen = jnp.zeros(lane.shape, f32)
    small_lane = lax.broadcasted_iota(i32, (total, LANES), 1)
    used = own_rows // tok_count * CAP
    per_row = used // (ROWS - used)
    places = jnp.zeros((total, LANES), f32)
    for k in range(EXPERTS):
        here = routed[:, k : k + 1] > 0.0
        target = (k * 2 * slot_count + base).astype(f32) + position[:, k : k + 1]
        chosen = chosen + jnp.where((lane == target) & here, 1.0, 0.0)
        local = block * CAP + position[:, k : k + 1].astype(i32)
        spare = SQUARE * (1 + local % per_row) + k * ROWS + used + local // per_row
        at_slot = (small_lane == k * ROWS + local) | (small_lane == spare)
        places = places + jnp.where(at_slot & here, 1.0, 0.0)
    slots = lax.dot_general(chosen.astype(bf16), rows, ROWS_BY_ROWS, preferred_element_type=f32)
    for k in range(EXPERTS):
        slot_refs[k][...] = slots[2 * k * slot_count : 2 * (k + 1) * slot_count].astype(bf16)
    for p in range(pipe_size):
        start = p * both_rows
        place_ref[p, :, :LANES] = places[start : start + own_rows]
        place_ref[p, :, LANES:] = extras[start : start + own_rows]


def join_kernel(pipe_size, *refs):
    blocks, out_ref = [ref[...].astype(f32) for ref in refs[:PER_GROUP]], refs[-1]
    rows = blocks[0].shape[0] // 2 // pipe_size
    for a in range(2):
        starts = [(a * pipe_size + p) * rows for p in range(pipe_size)]
        out_ref[a] = jnp.concatenate([b[s : s + rows] for s in starts for b in blocks], 0).astype(bf16)


def hidden_gradients(top_count, me, info, own_g, own_u, own_b, got):
    extras = info[...].astype(f32)
    gate = jnp.zeros((extras.shape[0], 1), f32)
    for k in range(top_count):
        gate = gate + jnp.where(extras[:, k : k + 1] == me, extras[:, top_count + k : top_count + k + 1], 0.0)
    pre_gate = own_g[...] + got[0].astype(f32)
    pre_up = own_u[...] + got[1].astype(f32)
    back_proj = own_b[...] + got[2].astype(f32)
    sig = jax.nn.sigmoid(pre_gate)
    activated = pre_gate * sig
    hidden = activated * pre_up
    share = jnp.sum(back_proj * hidden, axis=1, keepdims=True)
    high = share.astype(bf16).astype(f32)
    lane = lax.broadcasted_iota(i32, (share.shape[0], LANES), 1)
    tail = jnp.where(lane == 0, high, jnp.where(lane == 1, share - high, 0.0))
    d_hidden = gate * back_proj
    d_gate = d_hidden * pre_up * sig * (1.0 + pre_gate * (1.0 - sig))
    return d_gate, d_hidden * activated, gate * hidden, tail


def store_halves(values, refs):
    for value, ref in zip(values, refs):
        half = value.shape[0] // 2
        ref[0] = value[:half].astype(bf16)
        ref[1] = value[half:].astype(bf16)


def act_kernel(top_count, where_ref, *refs):
    store_halves(hidden_gradients(top_count, where_ref[0].astype(f32), *refs[:5]), refs[6:])


def back_rows(d_part, pipe_size, where_ref, grads, w_gate, w_up, out_ref):
    left = [jnp.concatenate([g[i].astype(f32) for g in grads], 0) for i in (0, 1, 3)]
    back = jnp.dot(left[0].astype(bf16), w_gate[...], preferred_element_type=f32)
    back = back + jnp.dot(left[1].astype(bf16), w_up[...], preferred_element_type=f32)
    count = back.shape[0] // 4
    members = out_ref.shape[1] // pipe_size
    used = count // members // pipe_size
    for h in range(2):
        for member in range(members):
            for p in range(pipe_size):
                starts = [(2 * g + h) * count + (member * pipe_size + p) * used for g in range(GROUPS)]
                at = member * pipe_size + (p ^ where_ref[1] if pipe_size == 2 else p)
                for columns, values in ((slice(0, d_part), back), (slice(d_part, None), left[2])):
                    block = jnp.concatenate([values[start : start + used] for start in starts], 0)
                    out_ref[h, at, :, columns] = block.astype(bf16)


def last_act_kernel(d_part, top_count, pipe_size, where_ref, *refs):
    raw, outs = refs[:5], refs[-5:]
    others = [refs[5 + 4 * i : 9 + 4 * i] for i in range(PIECES - 1)]
    w_gate, w_up = refs[4 * PIECES + 1 : 4 * PIECES + 3]
    last = hidden_gradients(top_count, where_ref[0].astype(f32), *raw)
    store_halves(last, outs[:4])
    half = last[0].shape[0] // 2
    grads = [[ref[1] for ref in other] for other in others] + [[value[half:] for value in last]]
    back_rows(d_part, pipe_size, where_ref, grads, w_gate, w_up, outs[4])


def own_back_kernel(d_part, pipe_size, where_ref, *refs):
    grads = [[ref[0] for ref in refs[4 * i : 4 * i + 4]] for i in range(PIECES)]
    back_rows(d_part, pipe_size, where_ref, grads, *refs[4 * PIECES : 4 * PIECES + 2], refs[-1])


def fold_kernel(a_ref, b_ref, *out_refs):
    for i, ref in enumerate(out_refs):
        here = i // a_ref.shape[1], i % a_ref.shape[1]
        ref[...] = (a_ref[here].astype(f32) + b_ref[here].astype(f32)).astype(bf16)


def pack_slots(used, columns, tail):
    main = columns.shape[1] // 4 * 3
    per_row = used // (ROWS - used)
    spare = [
        jnp.concatenate([columns[r * per_row + j : r * per_row + j + 1, main:] for j in range(per_row)], 1)
        for r in range(ROWS - used)
    ]
    rows = jnp.concatenate([columns[:, :main]] + spare, 0)
    tail = jnp.concatenate([tail, jnp.zeros((ROWS - used, LANES), f32)], 0)
    return jnp.concatenate([rows, tail], 1)


def fold_pairs_kernel(used, d_part, a_ref, b_ref, c_ref, d_ref, *out_refs):
    here = a_ref[...].astype(f32) + d_ref[...].astype(f32)
    there = b_ref[...].astype(f32) + c_ref[...].astype(f32)
    for k, ref in enumerate(out_refs):
        at = slice(k * used, (k + 1) * used)
        columns = jnp.concatenate([here[at, :d_part], there[at, :d_part]], 1)
        ref[...] = pack_slots(used, columns, here[at, d_part:]).astype(bf16)


def owner_kernel(d_part, packed, where_ref, place_ref, *refs):
    piece_refs, tok_ref, grad_ref = refs[:EXPERTS], refs[EXPERTS], refs[EXPERTS + 1]
    piece_refs = [piece_refs[RETURN_ORDER.index(k)] for k in range(EXPERTS)]
    micro_count, tok_count, d_model = tok_ref.shape
    top_count = grad_ref.shape[1]
    mine = place_ref[where_ref[1]]
    places = mine[:, :LANES].astype(bf16)
    place = places[:, :SQUARE]
    ids = mine[:, LANES:]
    rows = jnp.concatenate([ref[...].astype(f32) for ref in piece_refs], 0).astype(bf16)
    wide = rows.shape[1] - LANES
    out = jnp.dot(place, rows[:, :wide], preferred_element_type=f32)
    if packed:
        rest, quarter = 0.0, d_model - wide
        for j in range(wide // quarter):
            spare = places[:, (1 + j) * SQUARE : (2 + j) * SQUARE]
            columns = rows[:, j * quarter : (j + 1) * quarter]
            rest = rest + jnp.dot(spare, columns, preferred_element_type=f32)
        out = jnp.concatenate([out, rest], 1)
        first = where_ref[1] == 0
        here, there = out[:, :d_part], out[:, d_part:]
        out = jnp.concatenate([jnp.where(first, here, there), jnp.where(first, there, here)], 1)
    for m in range(micro_count):
        tok_ref[m] = out[m * tok_count : (m + 1) * tok_count].astype(bf16)

    expert_of = ((lax.broadcasted_iota(i32, place.shape, 1) // ROWS) ^ where_ref[0]).astype(f32)
    diagonal = lax.broadcasted_iota(i32, (tok_count, tok_count), 0) == lax.broadcasted_iota(
        i32, (tok_count, tok_count), 1
    )
    for k in range(top_count):
        picked = jnp.where(expert_of == ids[:, k : k + 1], mine[:, :SQUARE], 0.0).astype(bf16)
        grad = jnp.dot(picked, rows[:, wide:], preferred_element_type=f32)
        grad = grad[:, 0:1] + grad[:, 1:2]
        for m in range(micro_count):
            part = jnp.broadcast_to(grad[m * tok_count : (m + 1) * tok_count], (tok_count, tok_count))
            grad_ref[m, k : k + 1, :] = jnp.sum(jnp.where(diagonal, part, 0.0), axis=0, keepdims=True)


def flip_kernel(*refs):
    refs[-1][...] = jnp.concatenate([ref[...] for ref in refs[:-1]], 0).T


def flip_weight_kernel(weight_ref, after, out_ref):
    del after
    out_ref[...] = weight_ref[...].T


def weight_kernel(scale, block, tok_ref, cot_ref, *refs):
    pieces, (out_refs, held, sems) = refs[: 3 * PIECES], (refs[-5:-2], refs[-2], refs[-1])
    rights = []
    for w in range(3):
        halves = [ref[h].astype(f32) for ref in pieces[w::3] for h in range(2)]
        rights.append(jnp.concatenate(halves, 0).astype(bf16))
    copies = []
    for i in range(tok_ref.shape[0] // block):
        here = slice(i * block, (i + 1) * block)
        for w, left in enumerate((tok_ref, tok_ref, cot_ref)):
            rows = jnp.dot(left[here], rights[w], preferred_element_type=f32)
            held[w, here] = (rows * scale).astype(bf16)
            copies.append(pltpu.make_async_copy(held.at[w, here], out_refs[w].at[here], sems.at[w, i]))
            copies[-1].start()
    for copy in copies:
        copy.wait()


def tie_kernel(*refs):
    del refs


def call(kernel, out_shape, in_specs, name, mib=8, flops=0, moved=0, **more):
    specs = {"s": pl.BlockSpec(memory_space=pltpu.SMEM), "v": pl.BlockSpec(memory_space=pltpu.VMEM)}
    specs["a"] = pl.BlockSpec(memory_space=pl.ANY)
    specs["h"] = pl.BlockSpec(memory_space=pltpu.HBM)
    more.setdefault("out_specs", jax.tree.map(lambda _: specs["v"], out_shape))
    return pl.pallas_call(
        kernel,
        out_shape=out_shape,
        in_specs=[specs[c] for c in in_specs],
        compiler_params=pltpu.CompilerParams(vmem_limit_bytes=mib << 20),
        cost_estimate=pl.CostEstimate(flops=flops, bytes_accessed=moved, transcendentals=0),
        name=name,
        **more,
    )


def tie(values, after, **cost):
    return call(
        tie_kernel,
        [shape(v.shape, v.dtype) for v in values],
        "a" * (len(values) + 1),
        "tie",
        out_specs=[pl.BlockSpec(memory_space=pl.ANY)] * len(values),
        input_output_aliases={i: i for i in range(len(values))},
        **cost,
    )(*values, after)


def on_device(tokens, cotangent, expert_ids, gate_values, w_gate, w_up, w_down_t):
    micro_count, tok_count, d_model = tokens.shape
    top_count = expert_ids.shape[2]
    pipe_size = lax.axis_size("pipe")
    expert_size = lax.axis_size("expert")
    group_size = expert_size // EXPERTS
    bits = [1 << i for i in reversed(range(group_size.bit_length() - 1))]
    d_part, f_part = w_gate.shape
    width = -(-d_part // LANES) * LANES + LANES
    own_rows = micro_count * tok_count
    slots_here = micro_count * CAP
    slot_count = pipe_size * slots_here
    pipe = lax.axis_index("pipe")
    where = jnp.stack([lax.axis_index("expert") // group_size, pipe]).astype(i32)

    inputs = (tokens, cotangent, jnp.swapaxes(expert_ids, 1, 2), jnp.swapaxes(gate_values, 1, 2))
    blocks = call(
        functools.partial(prep_kernel, d_part),
        [shape((2 * own_rows, width), bf16) for _ in range(pipe_size)],
        "aaaa",
        "prep",
        scratch_shapes=[
            pltpu.VMEM(tokens.shape, bf16),
            pltpu.VMEM(tokens.shape, bf16),
            pltpu.VMEM((micro_count, top_count, tok_count), i32),
            pltpu.VMEM((micro_count, top_count, tok_count), bf16),
            pltpu.SemaphoreType.DMA((4,)),
        ],
    )(*[pltpu.with_memory_space_constraint(x, pltpu.HBM) for x in inputs])
    if pipe_size == 2:
        first = pipe == 0
        kept, sent = jnp.where(first, blocks[0], blocks[1]), jnp.where(first, blocks[1], blocks[0])
        blocks = [kept, swap(sent, "pipe", 1)]
    else:
        got = lax.all_to_all(jnp.stack(blocks), "pipe", split_axis=0, concat_axis=0, tiled=True)
        blocks = [got[p] for p in range(pipe_size)]
    *slots, place = call(
        functools.partial(pack_kernel, tok_count, top_count, pipe_size),
        tuple(shape((2 * slot_count, width), bf16) for _ in range(EXPERTS))
        + (shape((pipe_size, own_rows, 2 * LANES), f32),),
        "s" + "v" * pipe_size,
        "pack",
    )(where, *blocks)

    gathered = [slots[0]] + [swap(slots[k], "expert", k * group_size) for k in range(1, EXPERTS)]
    def join(g, *after, **cost):
        return call(
            functools.partial(join_kernel, pipe_size),
            shape((2, PER_GROUP * slot_count, width), bf16),
            "v" * PER_GROUP + "a" * len(after),
            "join",
            **cost,
        )(*gathered[g * PER_GROUP : (g + 1) * PER_GROUP], *after)

    def spread(rows):
        for bit in bits[1:]:
            rows = jnp.concatenate([rows, swap(rows, "expert", bit)], 1)
        return rows

    def project(rows):
        tok_rows, cot_rows = rows[0, :, :d_part], rows[1, :, :d_part]
        own = []
        for left, weight in ((tok_rows, w_gate), (tok_rows, w_up), (cot_rows, w_down_t)):
            own.append(jnp.dot(left, weight, preferred_element_type=f32))
        return own

    def exchange(rows, own):
        bit = pipe_size // 2
        while bit > 1:
            got = swap(jnp.stack([part.astype(bf16) for part in own]), "pipe", bit)
            own = [part + got[i].astype(f32) for i, part in enumerate(own)]
            bit //= 2
        got = swap(jnp.stack([part.astype(bf16) for part in own]), "pipe", 1)
        return [rows[0, :, width - LANES :], *own, got]

    first = join(0)
    there = swap(first, "expert", bits[0])
    first = spread(first)
    filler = tie([jnp.zeros((8, LANES), f32) + pipe.astype(f32)], place, **FILL_A)[0]
    first = tie([first], filler)[0]
    first_own = project(first)
    later = join(1, *first_own, **JOIN_COST)
    later_there = swap(later, "expert", bits[0])
    there, here = spread(there), spread(later)
    there_own, here_own = project(there), project(here)
    last = spread(tie([later_there], there_own[2])[0])
    pieces, owns = [first, there, here, last], [first_own, there_own, here_own, project(last)]
    exchanged = [exchange(rows, own) for rows, own in zip(pieces, owns)]
    total = sum(piece[0].shape[0] for piece in exchanged)

    flipped = [
        call(flip_kernel, shape((d_part, total), bf16), "v" * len(pieces), "flip", mib=24)(
            *[rows[a, :, :d_part] for rows in pieces]
        )
        for a in range(2)
    ]

    flipped_weights = [
        call(flip_weight_kernel, shape((f_part, d_part), bf16), "va", "flip_weight", mib=24)(w, exchanged[-1][3])
        for w in (w_gate, w_up)
    ]

    out_width = d_part + LANES
    padded = EXPERTS * slots_here
    half_shape = shape((2, group_size // 4 * pipe_size, padded, out_width), bf16)
    moved = total * (f_part * 24 + d_part * 8) + 4 * d_part * f_part
    mib = min(52, 8 + 2 * moved // (1 << 20))

    def grad_shapes(piece):
        rows = piece[0].shape[0] // 2
        return [shape((2, rows, f_part), bf16)] * 3 + [shape((2, rows, LANES), bf16)]

    grads = [
        call(functools.partial(act_kernel, top_count), grad_shapes(piece), "svvvvva", "act", mib=mib)(
            where, *piece, exchanged[-1][3]
        )
        for piece in exchanged[:-1]
    ]
    *last_grad, high = call(
        functools.partial(last_act_kernel, d_part, top_count, pipe_size),
        grad_shapes(exchanged[-1]) + [half_shape],
        "s" + "v" * (4 * PIECES + 3) + "a" * len(flipped),
        "last_act",
        mib=mib,
    )(where, *exchanged[-1], *[x for grad in grads for x in grad], *flipped_weights, *flipped)
    grads.append(last_grad)
    low = call(
        functools.partial(own_back_kernel, d_part, pipe_size),
        half_shape,
        "s" + "v" * (4 * PIECES + 2) + "a",
        "own_back",
        mib=mib,
    )(where, *[x for grad in grads for x in grad], *flipped_weights, high)
    packed = pipe_size == 2 and group_size == 4
    if packed:
        parts = call(fold_kernel, [shape((padded, out_width), bf16) for _ in range(4)], "vv", "fold")(
            low, swap(high, "expert", bits[1])
        )
        after = parts[0]
        got_both = swap_both(parts[3], bits[0])
        got_member = swap(parts[2], "expert", bits[0])
        got_pipe = swap(parts[1], "pipe", 1)
        contributions = call(
            functools.partial(fold_pairs_kernel, slots_here, d_part),
            [shape((ROWS, d_model // 4 * 3 + LANES), bf16) for _ in range(EXPERTS)],
            "vvvv",
            "fold_pairs",
        )(parts[0], got_both, got_pipe, got_member)
    else:
        for bit in reversed(bits[1:]):
            sums = (low.astype(f32) + swap(high, "expert", bit).astype(f32)).astype(bf16)
            low, high = jnp.split(sums, 2, 1) if bit != bits[1] else (sums[0], sums[1])
        sums = (low.astype(f32) + swap(high, "expert", bits[0]).astype(f32)).astype(bf16)
        after = sums
        if pipe_size == 2:
            got = swap(sums[1], "pipe", 1)
            sums = jnp.where(pipe == 0, jnp.stack([sums[0], got]), jnp.stack([got, sums[0]]))
        else:
            sums = lax.all_to_all(sums, "pipe", split_axis=0, concat_axis=0, tiled=True)
        wide = jnp.swapaxes(sums[:, :, :d_part], 0, 1).reshape(padded, d_model)
        wide = jnp.concatenate([wide, sums[0, :, d_part:]], 1)
        contributions = [
            jnp.pad(wide[k * slots_here : (k + 1) * slots_here], ((0, ROWS - slots_here), (0, 0)))
            for k in range(EXPERTS)
        ]
    contributions = [swap(x, "expert", k * group_size) if k else x for k, x in enumerate(contributions)]

    tokens_total = own_rows * pipe_size * expert_size
    scale = 1.0 / math.sqrt(tokens_total * top_count / EXPERTS)
    block = 256 if d_part % 256 == 0 else d_part
    dw_gate, dw_up, dw_down_t = call(
        functools.partial(weight_kernel, scale, block),
        [shape((d_part, f_part), bf16)] * 3,
        "vv" + "v" * (3 * PIECES) + "a",
        "weight_grads",
        mib=min(52, 12 + (d_part * (total * 4 + f_part * 8) >> 20)),
        out_specs=[pl.BlockSpec(memory_space=pl.ANY)] * 3,
        scratch_shapes=[
            pltpu.VMEM((3, d_part, f_part), bf16),
            pltpu.SemaphoreType.DMA((3, d_part // block)),
        ],
    )(*flipped, *[x for grad in grads for x in grad[:3]], after)

    d_tokens, gate_grads = call(
        functools.partial(owner_kernel, d_part, packed),
        (shape(tokens.shape, bf16), shape((micro_count, top_count, tok_count), f32)),
        "sv" + "v" * EXPERTS,
        "owner",
    )(where, place, *[contributions[k] for k in RETURN_ORDER])
    return (d_tokens, jnp.swapaxes(gate_grads, 1, 2), dw_gate, dw_up, dw_down_t)


def solution(mesh):
    rows = P(None, ("pipe", "expert"), None)
    weights = P("pipe", "expert")
    return jax.shard_map(
        on_device,
        mesh=mesh,
        in_specs=(rows, rows, rows, rows, weights, weights, weights),
        out_specs=(rows, rows, weights, weights, weights),
        check_vma=False,
    )
```

```python
import functools
import math

import jax
import jax.numpy as jnp
from jax import lax
from jax.experimental import pallas as pl
from jax.experimental.pallas import tpu as pltpu
from jax.sharding import PartitionSpec as P

EXPERTS = 4
CAP = 3
GROUPS = 2
PER_GROUP = EXPERTS // GROUPS
LANES = 128
ROWS = 8
PIECES = 4
SQUARE = EXPERTS * ROWS
RETURN_ORDER = (0, 2, 3, 1)
JOIN_COST = dict(flops=4000000000, moved=12000000)
FILL_A = dict(flops=8000000000, moved=24000000)
FILL_B = dict(flops=8_000_000_000, moved=24_000_000)
f32, bf16, i32 = jnp.float32, jnp.bfloat16, jnp.int32
ROWS_BY_ROWS = (((0,), (0,)), ((), ()))
shape = jax.ShapeDtypeStruct


def swap(x, axis, bit):
    return lax.ppermute(x, axis, [(i, i ^ bit) for i in range(lax.axis_size(axis))])


def swap_both(x, bit):
    count = lax.axis_size("expert")
    pairs = [(p * count + e, (p ^ 1) * count + (e ^ bit)) for p in range(2) for e in range(count)]
    return lax.ppermute(x, ("pipe", "expert"), pairs)


def prep_kernel(d_part, tok_hbm, cot_hbm, ids_hbm, gate_hbm, *refs):
    out_refs, (tok_ref, cot_ref, ids_ref, gate_ref, sems) = refs[:-5], refs[-5:]
    pairs = ((tok_hbm, tok_ref), (cot_hbm, cot_ref), (ids_hbm, ids_ref), (gate_hbm, gate_ref))
    copies = [pltpu.make_async_copy(src, dst, sems.at[i]) for i, (src, dst) in enumerate(pairs)]
    for copy in copies:
        copy.start()
    for copy in copies:
        copy.wait()
    micro_count, tok_count = tok_ref.shape[:2]
    top_count = ids_ref.shape[1]
    seg = out_refs[0].shape[-1] - LANES

    def flat(ref):
        return jnp.concatenate([ref[m].astype(f32) for m in range(micro_count)], 0)

    lane = lax.broadcasted_iota(i32, (tok_count, LANES), 1)
    diagonal = lax.broadcasted_iota(i32, (tok_count, tok_count), 0) == lax.broadcasted_iota(
        i32, (tok_count, tok_count), 1
    )
    blocks = []
    for m in range(micro_count):
        block = jnp.zeros((tok_count, LANES), f32)
        for at, ref in enumerate((ids_ref, gate_ref)):
            values = ref[m].astype(f32)
            for k in range(top_count):
                row = jnp.broadcast_to(values[k : k + 1], (tok_count, tok_count))
                column = jnp.sum(jnp.where(diagonal, row, 0.0), axis=1, keepdims=True)
                block = jnp.where(lane == at * top_count + k, column, block)
        blocks.append(block)
    extras = jnp.concatenate(blocks + blocks, 0).astype(bf16)
    both = jnp.concatenate([flat(tok_ref), flat(cot_ref)], 0).astype(bf16)
    for p, ref in enumerate(out_refs):
        ref[:, :d_part] = both[:, p * d_part : (p + 1) * d_part]
        if seg > d_part:
            ref[:, d_part:seg] = jnp.zeros((both.shape[0], seg - d_part), bf16)
        ref[:, seg:] = extras


def pack_kernel(tok_count, top_count, pipe_size, where_ref, *refs):
    blocks, slot_refs, place_ref = [ref[...] for ref in refs[:pipe_size]], refs[pipe_size:-1], refs[-1]
    both_rows, width = blocks[0].shape
    own_rows = both_rows // 2
    total = pipe_size * both_rows
    slot_count = slot_refs[0].shape[0] // 2
    me = where_ref[0]
    if pipe_size == 2:
        first = where_ref[1] == 0
        blocks = [jnp.where(first, blocks[0], blocks[1]), jnp.where(first, blocks[1], blocks[0])]
    rows = jnp.concatenate(blocks, 0)
    extras = rows[:, width - LANES :].astype(f32)
    at = (lax.broadcasted_iota(i32, (total, LANES), 1) ^ me).astype(f32)
    routed = jnp.zeros((total, LANES), f32)
    for k in range(top_count):
        routed = jnp.where(extras[:, k : k + 1] == at, 1.0, routed)
    at_row = lax.broadcasted_iota(i32, (total, LANES), 0) % tok_count
    position = jnp.zeros((total, LANES), f32)
    for d in range(1, tok_count):
        position = position + jnp.where(at_row >= d, pltpu.roll(routed, d, 0), 0.0)
    index = lax.broadcasted_iota(i32, (total, 1), 0)
    within = index % both_rows
    block = within % own_rows // tok_count
    device = index // both_rows
    base = within // own_rows * slot_count + (device * (own_rows // tok_count) + block) * CAP
    lane = lax.broadcasted_iota(i32, (total, EXPERTS * 2 * slot_count), 1).astype(f32)
    chosen = jnp.zeros(lane.shape, f32)
    small_lane = lax.broadcasted_iota(i32, (total, LANES), 1)
    used = own_rows // tok_count * CAP
    per_row = used // (ROWS - used)
    places = jnp.zeros((total, LANES), f32)
    for k in range(EXPERTS):
        here = routed[:, k : k + 1] > 0.0
        target = (k * 2 * slot_count + base).astype(f32) + position[:, k : k + 1]
        chosen = chosen + jnp.where((lane == target) & here, 1.0, 0.0)
        local = block * CAP + position[:, k : k + 1].astype(i32)
        spare = SQUARE * (1 + local % per_row) + k * ROWS + used + local // per_row
        at_slot = (small_lane == k * ROWS + local) | (small_lane == spare)
        places = places + jnp.where(at_slot & here, 1.0, 0.0)
    slots = lax.dot_general(chosen.astype(bf16), rows, ROWS_BY_ROWS, preferred_element_type=f32)
    for k in range(EXPERTS):
        slot_refs[k][...] = slots[2 * k * slot_count : 2 * (k + 1) * slot_count].astype(bf16)
    for p in range(pipe_size):
        start = p * both_rows
        place_ref[p, :, :LANES] = places[start : start + own_rows]
        place_ref[p, :, LANES:] = extras[start : start + own_rows]


def join_kernel(pipe_size, *refs):
    blocks, out_ref = [ref[...].astype(f32) for ref in refs[:PER_GROUP]], refs[-1]
    rows = blocks[0].shape[0] // 2 // pipe_size
    for a in range(2):
        starts = [(a * pipe_size + p) * rows for p in range(pipe_size)]
        out_ref[a] = jnp.concatenate([b[s : s + rows] for s in starts for b in blocks], 0).astype(bf16)


def hidden_gradients(top_count, me, info, own_g, own_u, own_b, got):
    extras = info[...].astype(f32)
    gate = jnp.zeros((extras.shape[0], 1), f32)
    for k in range(top_count):
        gate = gate + jnp.where(extras[:, k : k + 1] == me, extras[:, top_count + k : top_count + k + 1], 0.0)
    pre_gate = own_g[...] + got[0].astype(f32)
    pre_up = own_u[...] + got[1].astype(f32)
    back_proj = own_b[...] + got[2].astype(f32)
    sig = jax.nn.sigmoid(pre_gate)
    activated = pre_gate * sig
    hidden = activated * pre_up
    share = jnp.sum(back_proj * hidden, axis=1, keepdims=True)
    high = share.astype(bf16).astype(f32)
    lane = lax.broadcasted_iota(i32, (share.shape[0], LANES), 1)
    tail = jnp.where(lane == 0, high, jnp.where(lane == 1, share - high, 0.0))
    d_hidden = gate * back_proj
    d_gate = d_hidden * pre_up * sig * (1.0 + pre_gate * (1.0 - sig))
    return d_gate, d_hidden * activated, gate * hidden, tail


def store_halves(values, refs):
    for value, ref in zip(values, refs):
        half = value.shape[0] // 2
        ref[0] = value[:half].astype(bf16)
        ref[1] = value[half:].astype(bf16)


def act_kernel(top_count, where_ref, *refs):
    store_halves(hidden_gradients(top_count, where_ref[0].astype(f32), *refs[:5]), refs[6:])


def back_rows(d_part, pipe_size, where_ref, grads, w_gate, w_up, out_ref):
    left = [jnp.concatenate([g[i].astype(f32) for g in grads], 0) for i in (0, 1, 3)]
    back = jnp.dot(left[0].astype(bf16), w_gate[...], preferred_element_type=f32)
    back = back + jnp.dot(left[1].astype(bf16), w_up[...], preferred_element_type=f32)
    count = back.shape[0] // 4
    members = out_ref.shape[1] // pipe_size
    used = count // members // pipe_size
    for h in range(2):
        for member in range(members):
            for p in range(pipe_size):
                starts = [(2 * g + h) * count + (member * pipe_size + p) * used for g in range(GROUPS)]
                at = member * pipe_size + (p ^ where_ref[1] if pipe_size == 2 else p)
                for columns, values in ((slice(0, d_part), back), (slice(d_part, None), left[2])):
                    block = jnp.concatenate([values[start : start + used] for start in starts], 0)
                    out_ref[h, at, :, columns] = block.astype(bf16)


def last_act_kernel(d_part, top_count, pipe_size, where_ref, *refs):
    raw, outs = refs[:5], refs[-5:]
    others = [refs[5 + 4 * i : 9 + 4 * i] for i in range(PIECES - 1)]
    w_gate, w_up = refs[4 * PIECES + 1 : 4 * PIECES + 3]
    last = hidden_gradients(top_count, where_ref[0].astype(f32), *raw)
    store_halves(last, outs[:4])
    half = last[0].shape[0] // 2
    grads = [[ref[1] for ref in other] for other in others] + [[value[half:] for value in last]]
    back_rows(d_part, pipe_size, where_ref, grads, w_gate, w_up, outs[4])


def own_back_kernel(d_part, pipe_size, where_ref, *refs):
    grads = [[ref[0] for ref in refs[4 * i : 4 * i + 4]] for i in range(PIECES)]
    back_rows(d_part, pipe_size, where_ref, grads, *refs[4 * PIECES : 4 * PIECES + 2], refs[-1])


def fold_kernel(a_ref, b_ref, *out_refs):
    for i, ref in enumerate(out_refs):
        here = i // a_ref.shape[1], i % a_ref.shape[1], slice(None), slice(0, ref.shape[1])
        ref[...] = (a_ref[here].astype(f32) + b_ref[here].astype(f32)).astype(bf16)


def pack_slots(used, columns, tail):
    main = columns.shape[1] // 4 * 3
    per_row = used // (ROWS - used)
    spare = [
        jnp.concatenate([columns[r * per_row + j : r * per_row + j + 1, main:] for j in range(per_row)], 1)
        for r in range(ROWS - used)
    ]
    rows = jnp.concatenate([columns[:, :main]] + spare, 0)
    tail = jnp.concatenate([tail, jnp.zeros((ROWS - used, LANES), f32)], 0)
    return jnp.concatenate([rows, tail], 1)


def fold_pairs_kernel(used, d_part, a_ref, b_ref, c_ref, d_ref, *out_refs):
    here = a_ref[...].astype(f32) + d_ref[...].astype(f32)
    there = b_ref[...].astype(f32) + c_ref[...].astype(f32)
    for k, ref in enumerate(out_refs):
        at = slice(k * used, (k + 1) * used)
        columns = jnp.concatenate([here[at, :d_part], there[at, :d_part]], 1)
        ref[...] = pack_slots(used, columns, here[at, d_part:]).astype(bf16)


def owner_kernel(d_part, packed, where_ref, place_ref, *refs):
    piece_refs, tok_ref, grad_ref = refs[:EXPERTS], refs[EXPERTS], refs[EXPERTS + 1]
    piece_refs = [piece_refs[RETURN_ORDER.index(k)] for k in range(EXPERTS)]
    micro_count, tok_count, d_model = tok_ref.shape
    top_count = grad_ref.shape[1]
    mine = place_ref[where_ref[1]]
    places = mine[:, :LANES].astype(bf16)
    place = places[:, :SQUARE]
    ids = mine[:, LANES:]
    rows = jnp.concatenate([ref[...].astype(f32) for ref in piece_refs], 0).astype(bf16)
    wide = rows.shape[1] - LANES
    out = jnp.dot(place, rows[:, :wide], preferred_element_type=f32)
    if packed:
        rest, quarter = 0.0, d_model - wide
        for j in range(wide // quarter):
            spare = places[:, (1 + j) * SQUARE : (2 + j) * SQUARE]
            columns = rows[:, j * quarter : (j + 1) * quarter]
            rest = rest + jnp.dot(spare, columns, preferred_element_type=f32)
        out = jnp.concatenate([out, rest], 1)
        first = where_ref[1] == 0
        here, there = out[:, :d_part], out[:, d_part:]
        out = jnp.concatenate([jnp.where(first, here, there), jnp.where(first, there, here)], 1)
    for m in range(micro_count):
        tok_ref[m] = out[m * tok_count : (m + 1) * tok_count].astype(bf16)

    expert_of = ((lax.broadcasted_iota(i32, place.shape, 1) // ROWS) ^ where_ref[0]).astype(f32)
    diagonal = lax.broadcasted_iota(i32, (tok_count, tok_count), 0) == lax.broadcasted_iota(
        i32, (tok_count, tok_count), 1
    )
    for k in range(top_count):
        picked = jnp.where(expert_of == ids[:, k : k + 1], mine[:, :SQUARE], 0.0).astype(bf16)
        grad = jnp.dot(picked, rows[:, wide:], preferred_element_type=f32)
        grad = grad[:, 0:1] + grad[:, 1:2]
        for m in range(micro_count):
            part = jnp.broadcast_to(grad[m * tok_count : (m + 1) * tok_count], (tok_count, tok_count))
            grad_ref[m, k : k + 1, :] = jnp.sum(jnp.where(diagonal, part, 0.0), axis=0, keepdims=True)


def flip_kernel(*refs):
    refs[-1][...] = jnp.concatenate([ref[...] for ref in refs[:-1]], 0).T


def flip_weight_kernel(weight_ref, after, out_ref):
    del after
    out_ref[...] = weight_ref[...].T


def weight_kernel(scale, block, tok_ref, cot_ref, *refs):
    pieces, (out_refs, held, sems) = refs[: 3 * PIECES], (refs[-5:-2], refs[-2], refs[-1])
    rights = []
    for w in range(3):
        halves = [ref[h].astype(f32) for ref in pieces[w::3] for h in range(2)]
        rights.append(jnp.concatenate(halves, 0).astype(bf16))
    copies = []
    for i in range(tok_ref.shape[0] // block):
        here = slice(i * block, (i + 1) * block)
        for w, left in enumerate((tok_ref, tok_ref, cot_ref)):
            rows = jnp.dot(left[here], rights[w], preferred_element_type=f32)
            held[w, here] = (rows * scale).astype(bf16)
            copies.append(pltpu.make_async_copy(held.at[w, here], out_refs[w].at[here], sems.at[w, i]))
            copies[-1].start()
    for copy in copies:
        copy.wait()


def tie_kernel(*refs):
    del refs


def call(kernel, out_shape, in_specs, name, mib=8, flops=0, moved=0, **more):
    specs = {"s": pl.BlockSpec(memory_space=pltpu.SMEM), "v": pl.BlockSpec(memory_space=pltpu.VMEM)}
    specs["a"] = pl.BlockSpec(memory_space=pl.ANY)
    specs["h"] = pl.BlockSpec(memory_space=pltpu.HBM)
    more.setdefault("out_specs", jax.tree.map(lambda _: specs["v"], out_shape))
    return pl.pallas_call(
        kernel,
        out_shape=out_shape,
        in_specs=[specs[c] for c in in_specs],
        compiler_params=pltpu.CompilerParams(vmem_limit_bytes=mib << 20),
        cost_estimate=pl.CostEstimate(flops=flops, bytes_accessed=moved, transcendentals=0),
        name=name,
        **more,
    )


def tie(values, after, **cost):
    return call(
        tie_kernel,
        [shape(v.shape, v.dtype) for v in values],
        "a" * (len(values) + 1),
        "tie",
        out_specs=[pl.BlockSpec(memory_space=pl.ANY)] * len(values),
        input_output_aliases={i: i for i in range(len(values))},
        **cost,
    )(*values, after)


def on_device(tokens, cotangent, expert_ids, gate_values, w_gate, w_up, w_down_t):
    micro_count, tok_count, d_model = tokens.shape
    top_count = expert_ids.shape[2]
    pipe_size = lax.axis_size("pipe")
    expert_size = lax.axis_size("expert")
    group_size = expert_size // EXPERTS
    bits = [1 << i for i in reversed(range(group_size.bit_length() - 1))]
    d_part, f_part = w_gate.shape
    width = -(-d_part // LANES) * LANES + LANES
    own_rows = micro_count * tok_count
    slots_here = micro_count * CAP
    slot_count = pipe_size * slots_here
    pipe = lax.axis_index("pipe")
    where = jnp.stack([lax.axis_index("expert") // group_size, pipe]).astype(i32)

    inputs = (tokens, cotangent, jnp.swapaxes(expert_ids, 1, 2), jnp.swapaxes(gate_values, 1, 2))
    blocks = call(
        functools.partial(prep_kernel, d_part),
        [shape((2 * own_rows, width), bf16) for _ in range(pipe_size)],
        "aaaa",
        "prep",
        scratch_shapes=[
            pltpu.VMEM(tokens.shape, bf16),
            pltpu.VMEM(tokens.shape, bf16),
            pltpu.VMEM((micro_count, top_count, tok_count), i32),
            pltpu.VMEM((micro_count, top_count, tok_count), bf16),
            pltpu.SemaphoreType.DMA((4,)),
        ],
    )(*[pltpu.with_memory_space_constraint(x, pltpu.HBM) for x in inputs])
    if pipe_size == 2:
        first = pipe == 0
        kept, sent = jnp.where(first, blocks[0], blocks[1]), jnp.where(first, blocks[1], blocks[0])
        blocks = [kept, swap(sent, "pipe", 1)]
    else:
        got = lax.all_to_all(jnp.stack(blocks), "pipe", split_axis=0, concat_axis=0, tiled=True)
        blocks = [got[p] for p in range(pipe_size)]
    *slots, place = call(
        functools.partial(pack_kernel, tok_count, top_count, pipe_size),
        tuple(shape((2 * slot_count, width), bf16) for _ in range(EXPERTS))
        + (shape((pipe_size, own_rows, 2 * LANES), f32),),
        "s" + "v" * pipe_size,
        "pack",
    )(where, *blocks)

    gathered = [slots[0]] + [swap(slots[k], "expert", k * group_size) for k in range(1, EXPERTS)]
    def join(g, *after, **cost):
        return call(
            functools.partial(join_kernel, pipe_size),
            shape((2, PER_GROUP * slot_count, width), bf16),
            "v" * PER_GROUP + "a" * len(after),
            "join",
            **cost,
        )(*gathered[g * PER_GROUP : (g + 1) * PER_GROUP], *after)

    def spread(rows):
        for bit in bits[1:]:
            rows = jnp.concatenate([rows, swap(rows, "expert", bit)], 1)
        return rows

    def project(rows):
        tok_rows, cot_rows = rows[0, :, :d_part], rows[1, :, :d_part]
        own = []
        for left, weight in ((tok_rows, w_gate), (tok_rows, w_up), (cot_rows, w_down_t)):
            own.append(jnp.dot(left, weight, preferred_element_type=f32))
        return own

    def exchange(rows, own):
        bit = pipe_size // 2
        while bit > 1:
            got = swap(jnp.stack([part.astype(bf16) for part in own]), "pipe", bit)
            own = [part + got[i].astype(f32) for i, part in enumerate(own)]
            bit //= 2
        got = swap(jnp.stack([part.astype(bf16) for part in own]), "pipe", 1)
        return [rows[0, :, width - LANES :], *own, got]

    first = join(0)
    there = swap(first, "expert", bits[0])
    first = spread(first)
    filler = tie([jnp.zeros((8, LANES), f32) + pipe.astype(f32)], place, **FILL_A)[0]
    first = tie([first], filler)[0]
    first_own = project(first)
    first_sent = jnp.stack([part.astype(bf16) for part in first_own])
    later = join(1, *first_own, first_sent, **JOIN_COST)
    later_there = swap(later, "expert", bits[0])
    here = spread(later)
    here_own = project(here)
    there = spread(tie([there], here_own[2])[0])
    there_own = project(there)
    last = spread(tie([later_there], there_own[2])[0])
    pieces, owns = [first, there, here, last], [first_own, there_own, here_own, project(last)]
    exchanged = [exchange(rows, own) for rows, own in zip(pieces, owns)]
    total = sum(piece[0].shape[0] for piece in exchanged)

    flipped = [
        call(flip_kernel, shape((d_part, total), bf16), "v" * len(pieces), "flip", mib=24)(
            *[rows[a, :, :d_part] for rows in pieces]
        )
        for a in range(2)
    ]

    flipped_weights = [
        call(flip_weight_kernel, shape((f_part, d_part), bf16), "va", "flip_weight", mib=24)(w, exchanged[-1][3])
        for w in (w_gate, w_up)
    ]

    out_width = d_part + LANES
    padded = EXPERTS * slots_here
    half_shape = shape((2, group_size // 4 * pipe_size, padded, out_width), bf16)
    moved = total * (f_part * 24 + d_part * 8) + 4 * d_part * f_part
    mib = min(52, 8 + 2 * moved // (1 << 20))

    def grad_shapes(piece):
        rows = piece[0].shape[0] // 2
        return [shape((2, rows, f_part), bf16)] * 3 + [shape((2, rows, LANES), bf16)]

    grads = [
        call(functools.partial(act_kernel, top_count), grad_shapes(piece), "svvvvva", "act", mib=mib)(
            where, *piece, exchanged[-1][3]
        )
        for piece in exchanged[:-1]
    ]
    *last_grad, high = call(
        functools.partial(last_act_kernel, d_part, top_count, pipe_size),
        grad_shapes(exchanged[-1]) + [half_shape],
        "s" + "v" * (4 * PIECES + 3) + "a" * len(flipped),
        "last_act",
        mib=mib,
    )(where, *exchanged[-1], *[x for grad in grads for x in grad], *flipped_weights, *flipped)
    grads.append(last_grad)
    low = call(
        functools.partial(own_back_kernel, d_part, pipe_size),
        half_shape,
        "s" + "v" * (4 * PIECES + 2) + "a",
        "own_back",
        mib=mib,
    )(where, *[x for grad in grads for x in grad], *flipped_weights, high)
    packed = pipe_size == 2 and group_size == 4
    if packed:
        parts = call(fold_kernel, [shape((padded, w), bf16) for w in (out_width, d_part) * 2], "vv", "fold")(
            low, swap(high, "expert", bits[1])
        )
        after = parts[0]
        got_both = swap_both(parts[3], bits[0])
        got_member = swap(parts[2], "expert", bits[0])
        got_pipe = swap(parts[1], "pipe", 1)
        contributions = call(
            functools.partial(fold_pairs_kernel, slots_here, d_part),
            [shape((ROWS, d_model // 4 * 3 + LANES), bf16) for _ in range(EXPERTS)],
            "vvvv",
            "fold_pairs",
        )(parts[0], got_both, got_pipe, got_member)
    else:
        for bit in reversed(bits[1:]):
            sums = (low.astype(f32) + swap(high, "expert", bit).astype(f32)).astype(bf16)
            low, high = jnp.split(sums, 2, 1) if bit != bits[1] else (sums[0], sums[1])
        sums = (low.astype(f32) + swap(high, "expert", bits[0]).astype(f32)).astype(bf16)
        after = sums
        if pipe_size == 2:
            got = swap(sums[1], "pipe", 1)
            sums = jnp.where(pipe == 0, jnp.stack([sums[0], got]), jnp.stack([got, sums[0]]))
        else:
            sums = lax.all_to_all(sums, "pipe", split_axis=0, concat_axis=0, tiled=True)
        wide = jnp.swapaxes(sums[:, :, :d_part], 0, 1).reshape(padded, d_model)
        wide = jnp.concatenate([wide, sums[0, :, d_part:]], 1)
        contributions = [
            jnp.pad(wide[k * slots_here : (k + 1) * slots_here], ((0, ROWS - slots_here), (0, 0)))
            for k in range(EXPERTS)
        ]
    contributions = [swap(x, "expert", k * group_size) if k else x for k, x in enumerate(contributions)]

    tokens_total = own_rows * pipe_size * expert_size
    scale = 1.0 / math.sqrt(tokens_total * top_count / EXPERTS)
    block = 256 if d_part % 256 == 0 else d_part
    dw_gate, dw_up, dw_down_t = call(
        functools.partial(weight_kernel, scale, block),
        [shape((d_part, f_part), bf16)] * 3,
        "vv" + "v" * (3 * PIECES) + "a",
        "weight_grads",
        mib=min(52, 12 + (d_part * (total * 4 + f_part * 8) >> 20)),
        out_specs=[pl.BlockSpec(memory_space=pl.ANY)] * 3,
        scratch_shapes=[
            pltpu.VMEM((3, d_part, f_part), bf16),
            pltpu.SemaphoreType.DMA((3, d_part // block)),
        ],
    )(*flipped, *[x for grad in grads for x in grad[:3]], after)

    d_tokens, gate_grads = call(
        functools.partial(owner_kernel, d_part, packed),
        (shape(tokens.shape, bf16), shape((micro_count, top_count, tok_count), f32)),
        "sv" + "v" * EXPERTS,
        "owner",
    )(where, place, *[contributions[k] for k in RETURN_ORDER])
    return (d_tokens, jnp.swapaxes(gate_grads, 1, 2), dw_gate, dw_up, dw_down_t)


def solution(mesh):
    rows = P(None, ("pipe", "expert"), None)
    weights = P("pipe", "expert")
    return jax.shard_map(
        on_device,
        mesh=mesh,
        in_specs=(rows, rows, rows, rows, weights, weights, weights),
        out_specs=(rows, rows, weights, weights, weights),
        check_vma=False,
    )
```

```python
import functools
import math

import jax
import jax.numpy as jnp
from jax import lax
from jax.experimental import pallas as pl
from jax.experimental.pallas import tpu as pltpu
from jax.sharding import PartitionSpec as P

EXPERTS = 4
CAP = 3
GROUPS = 2
PER_GROUP = EXPERTS // GROUPS
LANES = 128
ROWS = 8
PIECES = 4
SQUARE = EXPERTS * ROWS
RETURN_ORDER = (0, 2, 3, 1)
JOIN_COST = dict(flops=4000000000, moved=12000000)
FILL_A = dict(flops=8000000000, moved=24000000)
FILL_B = dict(flops=8_000_000_000, moved=24_000_000)
f32, bf16, i32 = jnp.float32, jnp.bfloat16, jnp.int32
ROWS_BY_ROWS = (((0,), (0,)), ((), ()))
shape = jax.ShapeDtypeStruct


def swap(x, axis, bit):
    return lax.ppermute(x, axis, [(i, i ^ bit) for i in range(lax.axis_size(axis))])


def swap_both(x, bit):
    count = lax.axis_size("expert")
    pairs = [(p * count + e, (p ^ 1) * count + (e ^ bit)) for p in range(2) for e in range(count)]
    return lax.ppermute(x, ("pipe", "expert"), pairs)


def prep_kernel(d_part, tok_ref, cot_ref, ids_ref, gate_ref, *out_refs):
    micro_count, tok_count = tok_ref.shape[:2]
    top_count = ids_ref.shape[1]
    seg = out_refs[0].shape[-1] - LANES

    def flat(ref):
        return jnp.concatenate([ref[m].astype(f32) for m in range(micro_count)], 0)

    lane = lax.broadcasted_iota(i32, (tok_count, LANES), 1)
    diagonal = lax.broadcasted_iota(i32, (tok_count, tok_count), 0) == lax.broadcasted_iota(
        i32, (tok_count, tok_count), 1
    )
    blocks = []
    for m in range(micro_count):
        block = jnp.zeros((tok_count, LANES), f32)
        for at, ref in enumerate((ids_ref, gate_ref)):
            values = ref[m].astype(f32)
            for k in range(top_count):
                row = jnp.broadcast_to(values[k : k + 1], (tok_count, tok_count))
                column = jnp.sum(jnp.where(diagonal, row, 0.0), axis=1, keepdims=True)
                block = jnp.where(lane == at * top_count + k, column, block)
        blocks.append(block)
    extras = jnp.concatenate(blocks + blocks, 0).astype(bf16)
    both = jnp.concatenate([flat(tok_ref), flat(cot_ref)], 0).astype(bf16)
    for p, ref in enumerate(out_refs):
        ref[:, :d_part] = both[:, p * d_part : (p + 1) * d_part]
        if seg > d_part:
            ref[:, d_part:seg] = jnp.zeros((both.shape[0], seg - d_part), bf16)
        ref[:, seg:] = extras


def pack_kernel(tok_count, top_count, pipe_size, where_ref, *refs):
    blocks, slot_refs, place_ref = [ref[...] for ref in refs[:pipe_size]], refs[pipe_size:-1], refs[-1]
    both_rows, width = blocks[0].shape
    own_rows = both_rows // 2
    total = pipe_size * both_rows
    slot_count = slot_refs[0].shape[0] // 2
    me = where_ref[0]
    if pipe_size == 2:
        first = where_ref[1] == 0
        blocks = [jnp.where(first, blocks[0], blocks[1]), jnp.where(first, blocks[1], blocks[0])]
    rows = jnp.concatenate(blocks, 0)
    extras = rows[:, width - LANES :].astype(f32)
    at = (lax.broadcasted_iota(i32, (total, LANES), 1) ^ me).astype(f32)
    routed = jnp.zeros((total, LANES), f32)
    for k in range(top_count):
        routed = jnp.where(extras[:, k : k + 1] == at, 1.0, routed)
    at_row = lax.broadcasted_iota(i32, (total, LANES), 0) % tok_count
    position = jnp.zeros((total, LANES), f32)
    for d in range(1, tok_count):
        position = position + jnp.where(at_row >= d, pltpu.roll(routed, d, 0), 0.0)
    index = lax.broadcasted_iota(i32, (total, 1), 0)
    within = index % both_rows
    block = within % own_rows // tok_count
    device = index // both_rows
    base = within // own_rows * slot_count + (device * (own_rows // tok_count) + block) * CAP
    lane = lax.broadcasted_iota(i32, (total, EXPERTS * 2 * slot_count), 1).astype(f32)
    chosen = jnp.zeros(lane.shape, f32)
    small_lane = lax.broadcasted_iota(i32, (total, LANES), 1)
    used = own_rows // tok_count * CAP
    per_row = used // (ROWS - used)
    places = jnp.zeros((total, LANES), f32)
    for k in range(EXPERTS):
        here = routed[:, k : k + 1] > 0.0
        target = (k * 2 * slot_count + base).astype(f32) + position[:, k : k + 1]
        chosen = chosen + jnp.where((lane == target) & here, 1.0, 0.0)
        local = block * CAP + position[:, k : k + 1].astype(i32)
        spare = SQUARE * (1 + local % per_row) + k * ROWS + used + local // per_row
        at_slot = (small_lane == k * ROWS + local) | (small_lane == spare)
        places = places + jnp.where(at_slot & here, 1.0, 0.0)
    slots = lax.dot_general(chosen.astype(bf16), rows, ROWS_BY_ROWS, preferred_element_type=f32)
    for k in range(EXPERTS):
        slot_refs[k][...] = slots[2 * k * slot_count : 2 * (k + 1) * slot_count].astype(bf16)
    for p in range(pipe_size):
        start = p * both_rows
        place_ref[p, :, :LANES] = places[start : start + own_rows]
        place_ref[p, :, LANES:] = extras[start : start + own_rows]


def join_kernel(pipe_size, *refs):
    blocks, out_ref = [ref[...].astype(f32) for ref in refs[:PER_GROUP]], refs[-1]
    rows = blocks[0].shape[0] // 2 // pipe_size
    for a in range(2):
        starts = [(a * pipe_size + p) * rows for p in range(pipe_size)]
        out_ref[a] = jnp.concatenate([b[s : s + rows] for s in starts for b in blocks], 0).astype(bf16)


def hidden_gradients(top_count, me, info, own_g, own_u, own_b, got):
    extras = info[...].astype(f32)
    gate = jnp.zeros((extras.shape[0], 1), f32)
    for k in range(top_count):
        gate = gate + jnp.where(extras[:, k : k + 1] == me, extras[:, top_count + k : top_count + k + 1], 0.0)
    pre_gate = own_g[...] + got[0].astype(f32)
    pre_up = own_u[...] + got[1].astype(f32)
    back_proj = own_b[...] + got[2].astype(f32)
    sig = jax.nn.sigmoid(pre_gate)
    activated = pre_gate * sig
    hidden = activated * pre_up
    share = jnp.sum(back_proj * hidden, axis=1, keepdims=True)
    high = share.astype(bf16).astype(f32)
    lane = lax.broadcasted_iota(i32, (share.shape[0], LANES), 1)
    tail = jnp.where(lane == 0, high, jnp.where(lane == 1, share - high, 0.0))
    d_hidden = gate * back_proj
    d_gate = d_hidden * pre_up * sig * (1.0 + pre_gate * (1.0 - sig))
    return d_gate, d_hidden * activated, gate * hidden, tail


def store_halves(values, refs):
    for value, ref in zip(values, refs):
        half = value.shape[0] // 2
        ref[0] = value[:half].astype(bf16)
        ref[1] = value[half:].astype(bf16)


def act_kernel(top_count, where_ref, *refs):
    store_halves(hidden_gradients(top_count, where_ref[0].astype(f32), *refs[:5]), refs[6:])


def back_rows(d_part, pipe_size, where_ref, grads, w_gate, w_up, out_ref):
    left = [jnp.concatenate([g[i].astype(f32) for g in grads], 0) for i in (0, 1, 3)]
    back = jnp.dot(left[0].astype(bf16), w_gate[...], preferred_element_type=f32)
    back = back + jnp.dot(left[1].astype(bf16), w_up[...], preferred_element_type=f32)
    count = back.shape[0] // 4
    members = out_ref.shape[1] // pipe_size
    used = count // members // pipe_size
    for h in range(2):
        for member in range(members):
            for p in range(pipe_size):
                starts = [(2 * g + h) * count + (member * pipe_size + p) * used for g in range(GROUPS)]
                at = member * pipe_size + (p ^ where_ref[1] if pipe_size == 2 else p)
                for columns, values in ((slice(0, d_part), back), (slice(d_part, None), left[2])):
                    block = jnp.concatenate([values[start : start + used] for start in starts], 0)
                    out_ref[h, at, :, columns] = block.astype(bf16)


def last_act_kernel(d_part, top_count, pipe_size, where_ref, *refs):
    raw, outs = refs[:5], refs[-5:]
    others = [refs[5 + 4 * i : 9 + 4 * i] for i in range(PIECES - 1)]
    w_gate, w_up = refs[4 * PIECES + 1 : 4 * PIECES + 3]
    last = hidden_gradients(top_count, where_ref[0].astype(f32), *raw)
    store_halves(last, outs[:4])
    half = last[0].shape[0] // 2
    grads = [[ref[1] for ref in other] for other in others] + [[value[half:] for value in last]]
    back_rows(d_part, pipe_size, where_ref, grads, w_gate, w_up, outs[4])


def own_back_kernel(d_part, pipe_size, where_ref, *refs):
    grads = [[ref[0] for ref in refs[4 * i : 4 * i + 4]] for i in range(PIECES)]
    back_rows(d_part, pipe_size, where_ref, grads, *refs[4 * PIECES : 4 * PIECES + 2], refs[-1])


def fold_kernel(a_ref, b_ref, *out_refs):
    for i, ref in enumerate(out_refs):
        here = i // a_ref.shape[1], i % a_ref.shape[1], slice(None), slice(0, ref.shape[1])
        ref[...] = (a_ref[here].astype(f32) + b_ref[here].astype(f32)).astype(bf16)


def pack_slots(used, columns, tail):
    main = columns.shape[1] // 4 * 3
    per_row = used // (ROWS - used)
    spare = [
        jnp.concatenate([columns[r * per_row + j : r * per_row + j + 1, main:] for j in range(per_row)], 1)
        for r in range(ROWS - used)
    ]
    rows = jnp.concatenate([columns[:, :main]] + spare, 0)
    tail = jnp.concatenate([tail, jnp.zeros((ROWS - used, LANES), f32)], 0)
    return jnp.concatenate([rows, tail], 1)


def fold_pairs_kernel(used, d_part, a_ref, b_ref, c_ref, d_ref, *out_refs):
    here = a_ref[...].astype(f32) + d_ref[...].astype(f32)
    there = b_ref[...].astype(f32) + c_ref[...].astype(f32)
    for k, ref in enumerate(out_refs):
        at = slice(k * used, (k + 1) * used)
        columns = jnp.concatenate([here[at, :d_part], there[at, :d_part]], 1)
        ref[...] = pack_slots(used, columns, here[at, d_part:]).astype(bf16)


def owner_kernel(d_part, packed, where_ref, place_ref, *refs):
    piece_refs, tok_ref, grad_ref = refs[:EXPERTS], refs[EXPERTS], refs[EXPERTS + 1]
    piece_refs = [piece_refs[RETURN_ORDER.index(k)] for k in range(EXPERTS)]
    micro_count, tok_count, d_model = tok_ref.shape
    top_count = grad_ref.shape[1]
    mine = place_ref[where_ref[1]]
    places = mine[:, :LANES].astype(bf16)
    place = places[:, :SQUARE]
    ids = mine[:, LANES:]
    rows = jnp.concatenate([ref[...].astype(f32) for ref in piece_refs], 0).astype(bf16)
    wide = rows.shape[1] - LANES
    out = jnp.dot(place, rows[:, :wide], preferred_element_type=f32)
    if packed:
        rest, quarter = 0.0, d_model - wide
        for j in range(wide // quarter):
            spare = places[:, (1 + j) * SQUARE : (2 + j) * SQUARE]
            columns = rows[:, j * quarter : (j + 1) * quarter]
            rest = rest + jnp.dot(spare, columns, preferred_element_type=f32)
        out = jnp.concatenate([out, rest], 1)
        first = where_ref[1] == 0
        here, there = out[:, :d_part], out[:, d_part:]
        out = jnp.concatenate([jnp.where(first, here, there), jnp.where(first, there, here)], 1)
    for m in range(micro_count):
        tok_ref[m] = out[m * tok_count : (m + 1) * tok_count].astype(bf16)

    expert_of = ((lax.broadcasted_iota(i32, place.shape, 1) // ROWS) ^ where_ref[0]).astype(f32)
    diagonal = lax.broadcasted_iota(i32, (tok_count, tok_count), 0) == lax.broadcasted_iota(
        i32, (tok_count, tok_count), 1
    )
    for k in range(top_count):
        picked = jnp.where(expert_of == ids[:, k : k + 1], mine[:, :SQUARE], 0.0).astype(bf16)
        grad = jnp.dot(picked, rows[:, wide:], preferred_element_type=f32)
        grad = grad[:, 0:1] + grad[:, 1:2]
        for m in range(micro_count):
            part = jnp.broadcast_to(grad[m * tok_count : (m + 1) * tok_count], (tok_count, tok_count))
            grad_ref[m, k : k + 1, :] = jnp.sum(jnp.where(diagonal, part, 0.0), axis=0, keepdims=True)


def flip_kernel(*refs):
    refs[-1][...] = jnp.concatenate([ref[...] for ref in refs[:-1]], 0).T


def flip_weight_kernel(weight_ref, after, out_ref):
    del after
    out_ref[...] = weight_ref[...].T


def weight_kernel(scale, block, tok_ref, cot_ref, *refs):
    pieces, (out_refs, held, sems) = refs[: 3 * PIECES], (refs[-5:-2], refs[-2], refs[-1])
    rights = []
    for w in range(3):
        halves = [ref[h].astype(f32) for ref in pieces[w::3] for h in range(2)]
        rights.append(jnp.concatenate(halves, 0).astype(bf16))
    copies = []
    for i in range(tok_ref.shape[0] // block):
        here = slice(i * block, (i + 1) * block)
        for w, left in enumerate((tok_ref, tok_ref, cot_ref)):
            rows = jnp.dot(left[here], rights[w], preferred_element_type=f32)
            held[w, here] = (rows * scale).astype(bf16)
            copies.append(pltpu.make_async_copy(held.at[w, here], out_refs[w].at[here], sems.at[w, i]))
            copies[-1].start()
    for copy in copies:
        copy.wait()


def tie_kernel(*refs):
    del refs


def call(kernel, out_shape, operands, name, mib=8, flops=0, moved=0, **more):
    specs = {"s": pl.BlockSpec(memory_space=pltpu.SMEM), "v": pl.BlockSpec(memory_space=pltpu.VMEM)}
    specs["a"] = pl.BlockSpec(memory_space=pl.ANY)
    more.setdefault("in_specs", [specs[c] for c in operands])
    more.setdefault("out_specs", jax.tree.map(lambda _: specs["v"], out_shape))
    return pl.pallas_call(
        kernel,
        out_shape=out_shape,
        compiler_params=pltpu.CompilerParams(vmem_limit_bytes=mib << 20),
        cost_estimate=pl.CostEstimate(flops=flops, bytes_accessed=moved, transcendentals=0),
        name=name,
        **more,
    )


def tie(values, after, **cost):
    return call(
        tie_kernel,
        [shape(v.shape, v.dtype) for v in values],
        "a" * (len(values) + 1),
        "tie",
        out_specs=[pl.BlockSpec(memory_space=pl.ANY)] * len(values),
        input_output_aliases={i: i for i in range(len(values))},
        **cost,
    )(*values, after)


def on_device(tokens, cotangent, expert_ids, gate_values, w_gate, w_up, w_down_t):
    micro_count, tok_count, d_model = tokens.shape
    top_count = expert_ids.shape[2]
    pipe_size = lax.axis_size("pipe")
    expert_size = lax.axis_size("expert")
    group_size = expert_size // EXPERTS
    bits = [1 << i for i in reversed(range(group_size.bit_length() - 1))]
    d_part, f_part = w_gate.shape
    width = -(-d_part // LANES) * LANES + LANES
    own_rows = micro_count * tok_count
    slots_here = micro_count * CAP
    slot_count = pipe_size * slots_here
    pipe = lax.axis_index("pipe")
    where = jnp.stack([lax.axis_index("expert") // group_size, pipe]).astype(i32)

    inputs = (tokens, cotangent, jnp.swapaxes(expert_ids, 1, 2), jnp.swapaxes(gate_values, 1, 2))
    blocks = call(
        functools.partial(prep_kernel, d_part),
        [shape((2 * own_rows, width), bf16) for _ in range(pipe_size)],
        "aaaa",
        "prep",
        grid=(1,),
        in_specs=[pl.BlockSpec(x.shape, lambda i: (0, 0, 0)) for x in inputs],
    )(*[pltpu.with_memory_space_constraint(x, pltpu.HBM) for x in inputs])
    if pipe_size == 2:
        first = pipe == 0
        kept, sent = jnp.where(first, blocks[0], blocks[1]), jnp.where(first, blocks[1], blocks[0])
        blocks = [kept, swap(sent, "pipe", 1)]
    else:
        got = lax.all_to_all(jnp.stack(blocks), "pipe", split_axis=0, concat_axis=0, tiled=True)
        blocks = [got[p] for p in range(pipe_size)]
    *slots, place = call(
        functools.partial(pack_kernel, tok_count, top_count, pipe_size),
        tuple(shape((2 * slot_count, width), bf16) for _ in range(EXPERTS))
        + (shape((pipe_size, own_rows, 2 * LANES), f32),),
        "s" + "v" * pipe_size,
        "pack",
    )(where, *blocks)

    gathered = [slots[0]] + [swap(slots[k], "expert", k * group_size) for k in range(1, EXPERTS)]
    def join(g, *after, **cost):
        return call(
            functools.partial(join_kernel, pipe_size),
            shape((2, PER_GROUP * slot_count, width), bf16),
            "v" * PER_GROUP + "a" * len(after),
            "join",
            **cost,
        )(*gathered[g * PER_GROUP : (g + 1) * PER_GROUP], *after)

    def spread(rows):
        for bit in bits[1:]:
            rows = jnp.concatenate([rows, swap(rows, "expert", bit)], 1)
        return rows

    def project(rows):
        tok_rows, cot_rows = rows[0, :, :d_part], rows[1, :, :d_part]
        own = []
        for left, weight in ((tok_rows, w_gate), (tok_rows, w_up), (cot_rows, w_down_t)):
            own.append(jnp.dot(left, weight, preferred_element_type=f32))
        return own

    def exchange(rows, own):
        bit = pipe_size // 2
        while bit > 1:
            got = swap(jnp.stack([part.astype(bf16) for part in own]), "pipe", bit)
            own = [part + got[i].astype(f32) for i, part in enumerate(own)]
            bit //= 2
        got = swap(jnp.stack([part.astype(bf16) for part in own]), "pipe", 1)
        return [rows[0, :, width - LANES :], *own, got]

    first = join(0)
    there = swap(first, "expert", bits[0])
    first = spread(first)
    filler = tie([jnp.zeros((8, LANES), f32) + pipe.astype(f32)], place, **FILL_A)[0]
    first = tie([first], filler)[0]
    first_own = project(first)
    first_sent = jnp.stack([part.astype(bf16) for part in first_own])
    later = join(1, *first_own, first_sent, **JOIN_COST)
    later_there = swap(later, "expert", bits[0])
    here = spread(later)
    here_own = project(here)
    there = spread(tie([there], here_own[2])[0])
    there_own = project(there)
    last = spread(tie([later_there], there_own[2])[0])
    pieces, owns = [first, there, here, last], [first_own, there_own, here_own, project(last)]
    exchanged = [exchange(rows, own) for rows, own in zip(pieces, owns)]
    total = sum(piece[0].shape[0] for piece in exchanged)

    flipped = [
        call(flip_kernel, shape((d_part, total), bf16), "v" * len(pieces), "flip", mib=24)(
            *[rows[a, :, :d_part] for rows in pieces]
        )
        for a in range(2)
    ]

    flipped_weights = [
        call(flip_weight_kernel, shape((f_part, d_part), bf16), "va", "flip_weight", mib=24)(w, exchanged[-1][3])
        for w in (w_gate, w_up)
    ]

    out_width = d_part + LANES
    padded = EXPERTS * slots_here
    half_shape = shape((2, group_size // 4 * pipe_size, padded, out_width), bf16)
    moved = total * (f_part * 24 + d_part * 8) + 4 * d_part * f_part
    mib = min(52, 8 + 2 * moved // (1 << 20))

    def grad_shapes(piece):
        rows = piece[0].shape[0] // 2
        return [shape((2, rows, f_part), bf16)] * 3 + [shape((2, rows, LANES), bf16)]

    grads = [
        call(functools.partial(act_kernel, top_count), grad_shapes(piece), "svvvvva", "act", mib=mib)(
            where, *piece, exchanged[-1][3]
        )
        for piece in exchanged[:-1]
    ]
    *last_grad, high = call(
        functools.partial(last_act_kernel, d_part, top_count, pipe_size),
        grad_shapes(exchanged[-1]) + [half_shape],
        "s" + "v" * (4 * PIECES + 3) + "a" * len(flipped),
        "last_act",
        mib=mib,
    )(where, *exchanged[-1], *[x for grad in grads for x in grad], *flipped_weights, *flipped)
    grads.append(last_grad)
    low = call(
        functools.partial(own_back_kernel, d_part, pipe_size),
        half_shape,
        "s" + "v" * (4 * PIECES + 2) + "a",
        "own_back",
        mib=mib,
    )(where, *[x for grad in grads for x in grad], *flipped_weights, high)
    packed = pipe_size == 2 and group_size == 4
    if packed:
        parts = call(fold_kernel, [shape((padded, w), bf16) for w in (out_width, d_part) * 2], "vv", "fold")(
            low, swap(high, "expert", bits[1])
        )
        after = parts[0]
        got_both = swap_both(parts[3], bits[0])
        got_member = swap(parts[2], "expert", bits[0])
        got_pipe = swap(parts[1], "pipe", 1)
        contributions = call(
            functools.partial(fold_pairs_kernel, slots_here, d_part),
            [shape((ROWS, d_model // 4 * 3 + LANES), bf16) for _ in range(EXPERTS)],
            "vvvv",
            "fold_pairs",
        )(parts[0], got_both, got_pipe, got_member)
    else:
        for bit in reversed(bits[1:]):
            sums = (low.astype(f32) + swap(high, "expert", bit).astype(f32)).astype(bf16)
            low, high = jnp.split(sums, 2, 1) if bit != bits[1] else (sums[0], sums[1])
        sums = (low.astype(f32) + swap(high, "expert", bits[0]).astype(f32)).astype(bf16)
        after = sums
        if pipe_size == 2:
            got = swap(sums[1], "pipe", 1)
            sums = jnp.where(pipe == 0, jnp.stack([sums[0], got]), jnp.stack([got, sums[0]]))
        else:
            sums = lax.all_to_all(sums, "pipe", split_axis=0, concat_axis=0, tiled=True)
        wide = jnp.swapaxes(sums[:, :, :d_part], 0, 1).reshape(padded, d_model)
        wide = jnp.concatenate([wide, sums[0, :, d_part:]], 1)
        contributions = [
            jnp.pad(wide[k * slots_here : (k + 1) * slots_here], ((0, ROWS - slots_here), (0, 0)))
            for k in range(EXPERTS)
        ]
    contributions = [swap(x, "expert", k * group_size) if k else x for k, x in enumerate(contributions)]

    tokens_total = own_rows * pipe_size * expert_size
    scale = 1.0 / math.sqrt(tokens_total * top_count / EXPERTS)
    block = 256 if d_part % 256 == 0 else d_part
    dw_gate, dw_up, dw_down_t = call(
        functools.partial(weight_kernel, scale, block),
        [shape((d_part, f_part), bf16)] * 3,
        "vv" + "v" * (3 * PIECES) + "a",
        "weight_grads",
        mib=min(52, 12 + (d_part * (total * 4 + f_part * 8) >> 20)),
        out_specs=[pl.BlockSpec(memory_space=pl.ANY)] * 3,
        scratch_shapes=[
            pltpu.VMEM((3, d_part, f_part), bf16),
            pltpu.SemaphoreType.DMA((3, d_part // block)),
        ],
    )(*flipped, *[x for grad in grads for x in grad[:3]], after)

    d_tokens, gate_grads = call(
        functools.partial(owner_kernel, d_part, packed),
        (shape(tokens.shape, bf16), shape((micro_count, top_count, tok_count), f32)),
        "sv" + "v" * EXPERTS,
        "owner",
    )(where, place, *[contributions[k] for k in RETURN_ORDER])
    return (d_tokens, jnp.swapaxes(gate_grads, 1, 2), dw_gate, dw_up, dw_down_t)


def solution(mesh):
    rows = P(None, ("pipe", "expert"), None)
    weights = P("pipe", "expert")
    return jax.shard_map(
        on_device,
        mesh=mesh,
        in_specs=(rows, rows, rows, rows, weights, weights, weights),
        out_specs=(rows, rows, weights, weights, weights),
        check_vma=False,
    )
```

```python
import functools
import math

import jax
import jax.numpy as jnp
from jax import lax
from jax.experimental import pallas as pl
from jax.experimental.pallas import tpu as pltpu
from jax.sharding import PartitionSpec as P

EXPERTS = 4
CAP = 3
GROUPS = 2
PER_GROUP = EXPERTS // GROUPS
LANES = 128
ROWS = 8
PIECES = 4
SQUARE = EXPERTS * ROWS
RETURN_ORDER = (0, 3, 2, 1)
JOIN_COST = dict(flops=4000000000, moved=12000000)
FILL_A = dict(flops=8000000000, moved=24000000)
FILL_B = dict(flops=8_000_000_000, moved=24_000_000)
f32, bf16, i32 = jnp.float32, jnp.bfloat16, jnp.int32
ROWS_BY_ROWS = (((0,), (0,)), ((), ()))
shape = jax.ShapeDtypeStruct


def swap(x, axis, bit):
    return lax.ppermute(x, axis, [(i, i ^ bit) for i in range(lax.axis_size(axis))])


def swap_both(x, bit):
    count = lax.axis_size("expert")
    pairs = [(p * count + e, (p ^ 1) * count + (e ^ bit)) for p in range(2) for e in range(count)]
    return lax.ppermute(x, ("pipe", "expert"), pairs)


def prep_kernel(d_part, tok_ref, cot_ref, ids_ref, gate_ref, *out_refs):
    micro_count, tok_count = tok_ref.shape[:2]
    top_count = ids_ref.shape[1]
    seg = out_refs[0].shape[-1] - LANES

    def flat(ref):
        return jnp.concatenate([ref[m].astype(f32) for m in range(micro_count)], 0)

    lane = lax.broadcasted_iota(i32, (tok_count, LANES), 1)
    diagonal = lax.broadcasted_iota(i32, (tok_count, tok_count), 0) == lax.broadcasted_iota(
        i32, (tok_count, tok_count), 1
    )
    blocks = []
    for m in range(micro_count):
        block = jnp.zeros((tok_count, LANES), f32)
        for at, ref in enumerate((ids_ref, gate_ref)):
            values = ref[m].astype(f32)
            for k in range(top_count):
                row = jnp.broadcast_to(values[k : k + 1], (tok_count, tok_count))
                column = jnp.sum(jnp.where(diagonal, row, 0.0), axis=1, keepdims=True)
                block = jnp.where(lane == at * top_count + k, column, block)
        blocks.append(block)
    extras = jnp.concatenate(blocks + blocks, 0).astype(bf16)
    both = jnp.concatenate([flat(tok_ref), flat(cot_ref)], 0).astype(bf16)
    for p, ref in enumerate(out_refs):
        ref[:, :d_part] = both[:, p * d_part : (p + 1) * d_part]
        if seg > d_part:
            ref[:, d_part:seg] = jnp.zeros((both.shape[0], seg - d_part), bf16)
        ref[:, seg:] = extras


def pack_kernel(tok_count, top_count, pipe_size, where_ref, *refs):
    blocks, slot_refs, place_ref = [ref[...] for ref in refs[:pipe_size]], refs[pipe_size:-1], refs[-1]
    both_rows, width = blocks[0].shape
    own_rows = both_rows // 2
    total = pipe_size * both_rows
    slot_count = slot_refs[0].shape[0] // 2
    me = where_ref[0]
    if pipe_size == 2:
        first = where_ref[1] == 0
        blocks = [jnp.where(first, blocks[0], blocks[1]), jnp.where(first, blocks[1], blocks[0])]
    rows = jnp.concatenate(blocks, 0)
    extras = rows[:, width - LANES :].astype(f32)
    at = (lax.broadcasted_iota(i32, (total, LANES), 1) ^ me).astype(f32)
    routed = jnp.zeros((total, LANES), f32)
    for k in range(top_count):
        routed = jnp.where(extras[:, k : k + 1] == at, 1.0, routed)
    at_row = lax.broadcasted_iota(i32, (total, LANES), 0) % tok_count
    position = jnp.zeros((total, LANES), f32)
    for d in range(1, tok_count):
        position = position + jnp.where(at_row >= d, pltpu.roll(routed, d, 0), 0.0)
    index = lax.broadcasted_iota(i32, (total, 1), 0)
    within = index % both_rows
    block = within % own_rows // tok_count
    device = index // both_rows
    base = within // own_rows * slot_count + (device * (own_rows // tok_count) + block) * CAP
    lane = lax.broadcasted_iota(i32, (total, EXPERTS * 2 * slot_count), 1).astype(f32)
    chosen = jnp.zeros(lane.shape, f32)
    small_lane = lax.broadcasted_iota(i32, (total, LANES), 1)
    used = own_rows // tok_count * CAP
    per_row = used // (ROWS - used)
    places = jnp.zeros((total, LANES), f32)
    for k in range(EXPERTS):
        here = routed[:, k : k + 1] > 0.0
        target = (k * 2 * slot_count + base).astype(f32) + position[:, k : k + 1]
        chosen = chosen + jnp.where((lane == target) & here, 1.0, 0.0)
        local = block * CAP + position[:, k : k + 1].astype(i32)
        spare = SQUARE * (1 + local % per_row) + k * ROWS + used + local // per_row
        at_slot = (small_lane == k * ROWS + local) | (small_lane == spare)
        places = places + jnp.where(at_slot & here, 1.0, 0.0)
    slots = lax.dot_general(chosen.astype(bf16), rows, ROWS_BY_ROWS, preferred_element_type=f32)
    for k in range(EXPERTS):
        slot_refs[k][...] = slots[2 * k * slot_count : 2 * (k + 1) * slot_count].astype(bf16)
    for p in range(pipe_size):
        start = p * both_rows
        place_ref[p, :, :LANES] = places[start : start + own_rows]
        place_ref[p, :, LANES:] = extras[start : start + own_rows]


def join_kernel(pipe_size, *refs):
    blocks, out_ref = [ref[...].astype(f32) for ref in refs[:PER_GROUP]], refs[-1]
    rows = blocks[0].shape[0] // 2 // pipe_size
    for a in range(2):
        starts = [(a * pipe_size + p) * rows for p in range(pipe_size)]
        out_ref[a] = jnp.concatenate([b[s : s + rows] for s in starts for b in blocks], 0).astype(bf16)


def hidden_gradients(top_count, me, info, own_g, own_u, own_b, got):
    extras = info[...].astype(f32)
    gate = jnp.zeros((extras.shape[0], 1), f32)
    for k in range(top_count):
        gate = gate + jnp.where(extras[:, k : k + 1] == me, extras[:, top_count + k : top_count + k + 1], 0.0)
    pre_gate = own_g[...] + got[0].astype(f32)
    pre_up = own_u[...] + got[1].astype(f32)
    back_proj = own_b[...] + got[2].astype(f32)
    sig = jax.nn.sigmoid(pre_gate)
    activated = pre_gate * sig
    hidden = activated * pre_up
    share = jnp.sum(back_proj * hidden, axis=1, keepdims=True)
    high = share.astype(bf16).astype(f32)
    lane = lax.broadcasted_iota(i32, (share.shape[0], LANES), 1)
    tail = jnp.where(lane == 0, high, jnp.where(lane == 1, share - high, 0.0))
    d_hidden = gate * back_proj
    d_gate = d_hidden * pre_up * sig * (1.0 + pre_gate * (1.0 - sig))
    return d_gate, d_hidden * activated, gate * hidden, tail


def store_halves(values, refs):
    for value, ref in zip(values, refs):
        half = value.shape[0] // 2
        ref[0] = value[:half].astype(bf16)
        ref[1] = value[half:].astype(bf16)


def act_kernel(top_count, where_ref, *refs):
    store_halves(hidden_gradients(top_count, where_ref[0].astype(f32), *refs[:5]), refs[6:])


def back_rows(d_part, pipe_size, where_ref, grads, w_gate, w_up, out_ref):
    left = [jnp.concatenate([g[i].astype(f32) for g in grads], 0) for i in (0, 1, 3)]
    back = jnp.dot(left[0].astype(bf16), w_gate[...], preferred_element_type=f32)
    back = back + jnp.dot(left[1].astype(bf16), w_up[...], preferred_element_type=f32)
    count = back.shape[0] // 4
    members = out_ref.shape[1] // pipe_size
    used = count // members // pipe_size
    for h in range(2):
        for member in range(members):
            for p in range(pipe_size):
                starts = [(2 * g + h) * count + (member * pipe_size + p) * used for g in range(GROUPS)]
                at = member * pipe_size + (p ^ where_ref[1] if pipe_size == 2 else p)
                for columns, values in ((slice(0, d_part), back), (slice(d_part, None), left[2])):
                    block = jnp.concatenate([values[start : start + used] for start in starts], 0)
                    out_ref[h, at, :, columns] = block.astype(bf16)


def last_act_kernel(d_part, top_count, pipe_size, where_ref, *refs):
    raw, outs = refs[:5], refs[-5:]
    others = [refs[5 + 4 * i : 9 + 4 * i] for i in range(PIECES - 1)]
    w_gate, w_up = refs[4 * PIECES + 1 : 4 * PIECES + 3]
    last = hidden_gradients(top_count, where_ref[0].astype(f32), *raw)
    store_halves(last, outs[:4])
    half = last[0].shape[0] // 2
    grads = [[ref[1] for ref in other] for other in others] + [[value[half:] for value in last]]
    back_rows(d_part, pipe_size, where_ref, grads, w_gate, w_up, outs[4])


def own_back_kernel(d_part, pipe_size, where_ref, *refs):
    grads = [[ref[0] for ref in refs[4 * i : 4 * i + 4]] for i in range(PIECES)]
    back_rows(d_part, pipe_size, where_ref, grads, *refs[4 * PIECES : 4 * PIECES + 2], refs[-1])


def fold_kernel(a_ref, b_ref, *out_refs):
    for i, ref in enumerate(out_refs):
        here = i // a_ref.shape[1], i % a_ref.shape[1], slice(None), slice(0, ref.shape[1])
        ref[...] = (a_ref[here].astype(f32) + b_ref[here].astype(f32)).astype(bf16)


def pack_slots(used, columns, tail):
    main = columns.shape[1] // 4 * 3
    per_row = used // (ROWS - used)
    spare = [
        jnp.concatenate([columns[r * per_row + j : r * per_row + j + 1, main:] for j in range(per_row)], 1)
        for r in range(ROWS - used)
    ]
    rows = jnp.concatenate([columns[:, :main]] + spare, 0)
    tail = jnp.concatenate([tail, jnp.zeros((ROWS - used, LANES), f32)], 0)
    return jnp.concatenate([rows, tail], 1)


def fold_pairs_kernel(used, d_part, a_ref, b_ref, c_ref, d_ref, *out_refs):
    here = a_ref[...].astype(f32) + d_ref[...].astype(f32)
    there = b_ref[...].astype(f32) + c_ref[...].astype(f32)
    for k, ref in enumerate(out_refs):
        at = slice(k * used, (k + 1) * used)
        columns = jnp.concatenate([here[at, :d_part], there[at, :d_part]], 1)
        ref[...] = pack_slots(used, columns, here[at, d_part:]).astype(bf16)


def owner_kernel(d_part, packed, where_ref, place_ref, *refs):
    piece_refs, tok_ref, grad_ref = refs[:EXPERTS], refs[EXPERTS], refs[EXPERTS + 1]
    piece_refs = [piece_refs[RETURN_ORDER.index(k)] for k in range(EXPERTS)]
    micro_count, tok_count, d_model = tok_ref.shape
    top_count = grad_ref.shape[1]
    mine = place_ref[where_ref[1]]
    places = mine[:, :LANES].astype(bf16)
    place = places[:, :SQUARE]
    ids = mine[:, LANES:]
    rows = jnp.concatenate([ref[...].astype(f32) for ref in piece_refs], 0).astype(bf16)
    wide = rows.shape[1] - LANES
    out = jnp.dot(place, rows[:, :wide], preferred_element_type=f32)
    if packed:
        rest, quarter = 0.0, d_model - wide
        for j in range(wide // quarter):
            spare = places[:, (1 + j) * SQUARE : (2 + j) * SQUARE]
            columns = rows[:, j * quarter : (j + 1) * quarter]
            rest = rest + jnp.dot(spare, columns, preferred_element_type=f32)
        out = jnp.concatenate([out, rest], 1)
        first = where_ref[1] == 0
        here, there = out[:, :d_part], out[:, d_part:]
        out = jnp.concatenate([jnp.where(first, here, there), jnp.where(first, there, here)], 1)
    for m in range(micro_count):
        tok_ref[m] = out[m * tok_count : (m + 1) * tok_count].astype(bf16)

    expert_of = ((lax.broadcasted_iota(i32, place.shape, 1) // ROWS) ^ where_ref[0]).astype(f32)
    diagonal = lax.broadcasted_iota(i32, (tok_count, tok_count), 0) == lax.broadcasted_iota(
        i32, (tok_count, tok_count), 1
    )
    for k in range(top_count):
        picked = jnp.where(expert_of == ids[:, k : k + 1], mine[:, :SQUARE], 0.0).astype(bf16)
        grad = jnp.dot(picked, rows[:, wide:], preferred_element_type=f32)
        grad = grad[:, 0:1] + grad[:, 1:2]
        for m in range(micro_count):
            part = jnp.broadcast_to(grad[m * tok_count : (m + 1) * tok_count], (tok_count, tok_count))
            grad_ref[m, k : k + 1, :] = jnp.sum(jnp.where(diagonal, part, 0.0), axis=0, keepdims=True)


def flip_kernel(*refs):
    refs[-1][...] = jnp.concatenate([ref[...] for ref in refs[:-1]], 0).T


def flip_weight_kernel(weight_ref, after, out_ref):
    del after
    out_ref[...] = weight_ref[...].T


def weight_kernel(scale, block, tok_ref, cot_ref, *refs):
    pieces, (out_refs, held, sems) = refs[: 3 * PIECES], (refs[-5:-2], refs[-2], refs[-1])
    rights = []
    for w in range(3):
        halves = [ref[h].astype(f32) for ref in pieces[w::3] for h in range(2)]
        rights.append(jnp.concatenate(halves, 0).astype(bf16))
    copies = []
    for i in range(tok_ref.shape[0] // block):
        here = slice(i * block, (i + 1) * block)
        for w, left in enumerate((tok_ref, tok_ref, cot_ref)):
            rows = jnp.dot(left[here], rights[w], preferred_element_type=f32)
            held[w, here] = (rows * scale).astype(bf16)
            copies.append(pltpu.make_async_copy(held.at[w, here], out_refs[w].at[here], sems.at[w, i]))
            copies[-1].start()
    for copy in copies:
        copy.wait()


def tie_kernel(*refs):
    del refs


def call(kernel, out_shape, operands, name, mib=8, flops=0, moved=0, **more):
    specs = {"s": pl.BlockSpec(memory_space=pltpu.SMEM), "v": pl.BlockSpec(memory_space=pltpu.VMEM)}
    specs["a"] = pl.BlockSpec(memory_space=pl.ANY)
    more.setdefault("in_specs", [specs[c] for c in operands])
    more.setdefault("out_specs", jax.tree.map(lambda _: specs["v"], out_shape))
    return pl.pallas_call(
        kernel,
        out_shape=out_shape,
        compiler_params=pltpu.CompilerParams(vmem_limit_bytes=mib << 20),
        cost_estimate=pl.CostEstimate(flops=flops, bytes_accessed=moved, transcendentals=0),
        name=name,
        **more,
    )


def tie(values, after, **cost):
    return call(
        tie_kernel,
        [shape(v.shape, v.dtype) for v in values],
        "a" * (len(values) + 1),
        "tie",
        out_specs=[pl.BlockSpec(memory_space=pl.ANY)] * len(values),
        input_output_aliases={i: i for i in range(len(values))},
        **cost,
    )(*values, after)


def on_device(tokens, cotangent, expert_ids, gate_values, w_gate, w_up, w_down_t):
    micro_count, tok_count, d_model = tokens.shape
    top_count = expert_ids.shape[2]
    pipe_size = lax.axis_size("pipe")
    expert_size = lax.axis_size("expert")
    group_size = expert_size // EXPERTS
    bits = [1 << i for i in reversed(range(group_size.bit_length() - 1))]
    d_part, f_part = w_gate.shape
    width = -(-d_part // LANES) * LANES + LANES
    own_rows = micro_count * tok_count
    slots_here = micro_count * CAP
    slot_count = pipe_size * slots_here
    pipe = lax.axis_index("pipe")
    where = jnp.stack([lax.axis_index("expert") // group_size, pipe]).astype(i32)

    inputs = (tokens, cotangent, jnp.swapaxes(expert_ids, 1, 2), jnp.swapaxes(gate_values, 1, 2))
    blocks = call(
        functools.partial(prep_kernel, d_part),
        [shape((2 * own_rows, width), bf16) for _ in range(pipe_size)],
        "aaaa",
        "prep",
        grid=(1,),
        in_specs=[pl.BlockSpec(x.shape, lambda i: (0, 0, 0)) for x in inputs],
    )(*[pltpu.with_memory_space_constraint(x, pltpu.HBM) for x in inputs])
    if pipe_size == 2:
        first = pipe == 0
        kept, sent = jnp.where(first, blocks[0], blocks[1]), jnp.where(first, blocks[1], blocks[0])
        blocks = [kept, swap(sent, "pipe", 1)]
    else:
        got = lax.all_to_all(jnp.stack(blocks), "pipe", split_axis=0, concat_axis=0, tiled=True)
        blocks = [got[p] for p in range(pipe_size)]
    *slots, place = call(
        functools.partial(pack_kernel, tok_count, top_count, pipe_size),
        tuple(shape((2 * slot_count, width), bf16) for _ in range(EXPERTS))
        + (shape((pipe_size, own_rows, 2 * LANES), f32),),
        "s" + "v" * pipe_size,
        "pack",
    )(where, *blocks)

    gathered = [slots[0]] + [swap(slots[k], "expert", k * group_size) for k in range(1, EXPERTS)]
    def join(g, *after, **cost):
        return call(
            functools.partial(join_kernel, pipe_size),
            shape((2, PER_GROUP * slot_count, width), bf16),
            "v" * PER_GROUP + "a" * len(after),
            "join",
            **cost,
        )(*gathered[g * PER_GROUP : (g + 1) * PER_GROUP], *after)

    def spread(rows):
        for bit in bits[1:]:
            rows = jnp.concatenate([rows, swap(rows, "expert", bit)], 1)
        return rows

    def project(rows):
        tok_rows, cot_rows = rows[0, :, :d_part], rows[1, :, :d_part]
        own = []
        for left, weight in ((tok_rows, w_gate), (tok_rows, w_up), (cot_rows, w_down_t)):
            own.append(jnp.dot(left, weight, preferred_element_type=f32))
        return own

    def exchange(rows, own):
        bit = pipe_size // 2
        while bit > 1:
            got = swap(jnp.stack([part.astype(bf16) for part in own]), "pipe", bit)
            own = [part + got[i].astype(f32) for i, part in enumerate(own)]
            bit //= 2
        got = swap(jnp.stack([part.astype(bf16) for part in own]), "pipe", 1)
        return [rows[0, :, width - LANES :], *own, got]

    first = join(0)
    there = swap(first, "expert", bits[0])
    first = spread(first)
    filler = tie([jnp.zeros((8, LANES), f32) + pipe.astype(f32)], place, **FILL_A)[0]
    first = tie([first], filler)[0]
    first_own = project(first)
    first_sent = jnp.stack([part.astype(bf16) for part in first_own])
    later = join(1, *first_own, first_sent, **JOIN_COST)
    later_there = swap(later, "expert", bits[0])
    here = spread(later)
    here_own = project(here)
    there = spread(tie([there], here_own[2])[0])
    there_own = project(there)
    last = spread(tie([later_there], there_own[2])[0])
    pieces, owns = [first, there, here, last], [first_own, there_own, here_own, project(last)]
    exchanged = [exchange(rows, own) for rows, own in zip(pieces, owns)]
    total = sum(piece[0].shape[0] for piece in exchanged)

    flipped = [
        call(flip_kernel, shape((d_part, total), bf16), "v" * len(pieces), "flip", mib=24)(
            *[rows[a, :, :d_part] for rows in pieces]
        )
        for a in range(2)
    ]

    flipped_weights = [
        call(flip_weight_kernel, shape((f_part, d_part), bf16), "va", "flip_weight", mib=24)(w, exchanged[-1][3])
        for w in (w_gate, w_up)
    ]

    out_width = d_part + LANES
    padded = EXPERTS * slots_here
    half_shape = shape((2, group_size // 4 * pipe_size, padded, out_width), bf16)
    moved = total * (f_part * 24 + d_part * 8) + 4 * d_part * f_part
    mib = min(52, 8 + 2 * moved // (1 << 20))

    def grad_shapes(piece):
        rows = piece[0].shape[0] // 2
        return [shape((2, rows, f_part), bf16)] * 3 + [shape((2, rows, LANES), bf16)]

    grads = [
        call(functools.partial(act_kernel, top_count), grad_shapes(piece), "svvvvva", "act", mib=mib)(
            where, *piece, exchanged[-1][3]
        )
        for piece in exchanged[:-1]
    ]
    *last_grad, high = call(
        functools.partial(last_act_kernel, d_part, top_count, pipe_size),
        grad_shapes(exchanged[-1]) + [half_shape],
        "s" + "v" * (4 * PIECES + 3) + "a" * len(flipped),
        "last_act",
        mib=mib,
    )(where, *exchanged[-1], *[x for grad in grads for x in grad], *flipped_weights, *flipped)
    grads.append(last_grad)
    low = call(
        functools.partial(own_back_kernel, d_part, pipe_size),
        half_shape,
        "s" + "v" * (4 * PIECES + 2) + "a",
        "own_back",
        mib=mib,
    )(where, *[x for grad in grads for x in grad], *flipped_weights, high)
    packed = pipe_size == 2 and group_size == 4
    if packed:
        parts = call(fold_kernel, [shape((padded, w), bf16) for w in (out_width, d_part) * 2], "vv", "fold")(
            low, swap(high, "expert", bits[1])
        )
        after = parts[0]
        got_both = swap_both(parts[3], bits[0])
        got_member = swap(parts[2], "expert", bits[0])
        got_pipe = swap(parts[1], "pipe", 1)
        contributions = call(
            functools.partial(fold_pairs_kernel, slots_here, d_part),
            [shape((ROWS, d_model // 4 * 3 + LANES), bf16) for _ in range(EXPERTS)],
            "vvvv",
            "fold_pairs",
        )(parts[0], got_both, got_pipe, got_member)
    else:
        for bit in reversed(bits[1:]):
            sums = (low.astype(f32) + swap(high, "expert", bit).astype(f32)).astype(bf16)
            low, high = jnp.split(sums, 2, 1) if bit != bits[1] else (sums[0], sums[1])
        sums = (low.astype(f32) + swap(high, "expert", bits[0]).astype(f32)).astype(bf16)
        after = sums
        if pipe_size == 2:
            got = swap(sums[1], "pipe", 1)
            sums = jnp.where(pipe == 0, jnp.stack([sums[0], got]), jnp.stack([got, sums[0]]))
        else:
            sums = lax.all_to_all(sums, "pipe", split_axis=0, concat_axis=0, tiled=True)
        wide = jnp.swapaxes(sums[:, :, :d_part], 0, 1).reshape(padded, d_model)
        wide = jnp.concatenate([wide, sums[0, :, d_part:]], 1)
        contributions = [
            jnp.pad(wide[k * slots_here : (k + 1) * slots_here], ((0, ROWS - slots_here), (0, 0)))
            for k in range(EXPERTS)
        ]
    contributions = [swap(x, "expert", k * group_size) if k else x for k, x in enumerate(contributions)]

    tokens_total = own_rows * pipe_size * expert_size
    scale = 1.0 / math.sqrt(tokens_total * top_count / EXPERTS)
    block = 256 if d_part % 256 == 0 else d_part
    dw_gate, dw_up, dw_down_t = call(
        functools.partial(weight_kernel, scale, block),
        [shape((d_part, f_part), bf16)] * 3,
        "vv" + "v" * (3 * PIECES) + "a",
        "weight_grads",
        mib=min(52, 12 + (d_part * (total * 4 + f_part * 8) >> 20)),
        out_specs=[pl.BlockSpec(memory_space=pl.ANY)] * 3,
        scratch_shapes=[
            pltpu.VMEM((3, d_part, f_part), bf16),
            pltpu.SemaphoreType.DMA((3, d_part // block)),
        ],
    )(*flipped, *[x for grad in grads for x in grad[:3]], after)

    d_tokens, gate_grads = call(
        functools.partial(owner_kernel, d_part, packed),
        (shape(tokens.shape, bf16), shape((micro_count, top_count, tok_count), f32)),
        "sv" + "v" * EXPERTS,
        "owner",
    )(where, place, *[contributions[k] for k in RETURN_ORDER])
    return (d_tokens, jnp.swapaxes(gate_grads, 1, 2), dw_gate, dw_up, dw_down_t)


def solution(mesh):
    rows = P(None, ("pipe", "expert"), None)
    weights = P("pipe", "expert")
    return jax.shard_map(
        on_device,
        mesh=mesh,
        in_specs=(rows, rows, rows, rows, weights, weights, weights),
        out_specs=(rows, rows, weights, weights, weights),
        check_vma=False,
    )
```

```python
import functools
import math

import jax
import jax.numpy as jnp
from jax import lax
from jax.experimental import pallas as pl
from jax.experimental.pallas import tpu as pltpu
from jax.sharding import PartitionSpec as P

EXPERTS = 4
CAP = 3
GROUPS = 2
PER_GROUP = EXPERTS // GROUPS
LANES = 128
ROWS = 8
PIECES = 4
SQUARE = EXPERTS * ROWS
RETURN_ORDER = (0, 3, 2, 1)
JOIN_COST = dict(flops=4000000000, moved=12000000)
FILL_A = dict(flops=8000000000, moved=24000000)
FILL_B = dict(flops=8_000_000_000, moved=24_000_000)
f32, bf16, i32 = jnp.float32, jnp.bfloat16, jnp.int32
ROWS_BY_ROWS = (((0,), (0,)), ((), ()))
shape = jax.ShapeDtypeStruct


def swap(x, axis, bit):
    return lax.ppermute(x, axis, [(i, i ^ bit) for i in range(lax.axis_size(axis))])


def swap_both(x, bit):
    count = lax.axis_size("expert")
    pairs = [(p * count + e, (p ^ 1) * count + (e ^ bit)) for p in range(2) for e in range(count)]
    return lax.ppermute(x, ("pipe", "expert"), pairs)


def scalar(ref, lane):
    return ref[...][0, lane]


def prep_kernel(d_part, tok_ref, cot_ref, ids_ref, gate_ref, *out_refs):
    micro_count, tok_count = tok_ref.shape[:2]
    top_count = ids_ref.shape[1]
    seg = out_refs[0].shape[-1] - LANES

    def flat(ref):
        return jnp.concatenate([ref[m].astype(f32) for m in range(micro_count)], 0)

    lane = lax.broadcasted_iota(i32, (tok_count, LANES), 1)
    diagonal = lax.broadcasted_iota(i32, (tok_count, tok_count), 0) == lax.broadcasted_iota(
        i32, (tok_count, tok_count), 1
    )
    blocks = []
    for m in range(micro_count):
        block = jnp.zeros((tok_count, LANES), f32)
        for at, ref in enumerate((ids_ref, gate_ref)):
            values = ref[m].astype(f32)
            for k in range(top_count):
                row = jnp.broadcast_to(values[k : k + 1], (tok_count, tok_count))
                column = jnp.sum(jnp.where(diagonal, row, 0.0), axis=1, keepdims=True)
                block = jnp.where(lane == at * top_count + k, column, block)
        blocks.append(block)
    extras = jnp.concatenate(blocks + blocks, 0).astype(bf16)
    both = jnp.concatenate([flat(tok_ref), flat(cot_ref)], 0).astype(bf16)
    for p, ref in enumerate(out_refs):
        ref[:, :d_part] = both[:, p * d_part : (p + 1) * d_part]
        if seg > d_part:
            ref[:, d_part:seg] = jnp.zeros((both.shape[0], seg - d_part), bf16)
        ref[:, seg:] = extras


def pack_kernel(tok_count, top_count, pipe_size, where_ref, *refs):
    blocks, slot_refs, place_ref = [ref[...] for ref in refs[:pipe_size]], refs[pipe_size:-1], refs[-1]
    both_rows, width = blocks[0].shape
    own_rows = both_rows // 2
    total = pipe_size * both_rows
    slot_count = slot_refs[0].shape[0] // 2
    me = scalar(where_ref, 0)
    if pipe_size == 2:
        first = scalar(where_ref, 1) == 0
        blocks = [jnp.where(first, blocks[0], blocks[1]), jnp.where(first, blocks[1], blocks[0])]
    rows = jnp.concatenate(blocks, 0)
    extras = rows[:, width - LANES :].astype(f32)
    at = (lax.broadcasted_iota(i32, (total, LANES), 1) ^ me).astype(f32)
    routed = jnp.zeros((total, LANES), f32)
    for k in range(top_count):
        routed = jnp.where(extras[:, k : k + 1] == at, 1.0, routed)
    at_row = lax.broadcasted_iota(i32, (total, LANES), 0) % tok_count
    position = jnp.zeros((total, LANES), f32)
    for d in range(1, tok_count):
        position = position + jnp.where(at_row >= d, pltpu.roll(routed, d, 0), 0.0)
    index = lax.broadcasted_iota(i32, (total, 1), 0)
    within = index % both_rows
    block = within % own_rows // tok_count
    device = index // both_rows
    base = within // own_rows * slot_count + (device * (own_rows // tok_count) + block) * CAP
    lane = lax.broadcasted_iota(i32, (total, EXPERTS * 2 * slot_count), 1).astype(f32)
    chosen = jnp.zeros(lane.shape, f32)
    small_lane = lax.broadcasted_iota(i32, (total, LANES), 1)
    used = own_rows // tok_count * CAP
    per_row = used // (ROWS - used)
    places = jnp.zeros((total, LANES), f32)
    for k in range(EXPERTS):
        here = routed[:, k : k + 1] > 0.0
        target = (k * 2 * slot_count + base).astype(f32) + position[:, k : k + 1]
        chosen = chosen + jnp.where((lane == target) & here, 1.0, 0.0)
        local = block * CAP + position[:, k : k + 1].astype(i32)
        spare = SQUARE * (1 + local % per_row) + k * ROWS + used + local // per_row
        at_slot = (small_lane == k * ROWS + local) | (small_lane == spare)
        places = places + jnp.where(at_slot & here, 1.0, 0.0)
    slots = lax.dot_general(chosen.astype(bf16), rows, ROWS_BY_ROWS, preferred_element_type=f32)
    for k in range(EXPERTS):
        slot_refs[k][...] = slots[2 * k * slot_count : 2 * (k + 1) * slot_count].astype(bf16)
    for p in range(pipe_size):
        start = p * both_rows
        place_ref[p, :, :LANES] = places[start : start + own_rows]
        place_ref[p, :, LANES:] = extras[start : start + own_rows]


def join_kernel(pipe_size, *refs):
    blocks, out_ref = [ref[...].astype(f32) for ref in refs[:PER_GROUP]], refs[-1]
    rows = blocks[0].shape[0] // 2 // pipe_size
    for a in range(2):
        starts = [(a * pipe_size + p) * rows for p in range(pipe_size)]
        out_ref[a] = jnp.concatenate([b[s : s + rows] for s in starts for b in blocks], 0).astype(bf16)


def hidden_gradients(top_count, me, info, own_g, own_u, own_b, got):
    extras = info[...].astype(f32)
    gate = jnp.zeros((extras.shape[0], 1), f32)
    for k in range(top_count):
        gate = gate + jnp.where(extras[:, k : k + 1] == me, extras[:, top_count + k : top_count + k + 1], 0.0)
    pre_gate = own_g[...] + got[0].astype(f32)
    pre_up = own_u[...] + got[1].astype(f32)
    back_proj = own_b[...] + got[2].astype(f32)
    sig = jax.nn.sigmoid(pre_gate)
    activated = pre_gate * sig
    hidden = activated * pre_up
    share = jnp.sum(back_proj * hidden, axis=1, keepdims=True)
    high = share.astype(bf16).astype(f32)
    lane = lax.broadcasted_iota(i32, (share.shape[0], LANES), 1)
    tail = jnp.where(lane == 0, high, jnp.where(lane == 1, share - high, 0.0))
    d_hidden = gate * back_proj
    d_gate = d_hidden * pre_up * sig * (1.0 + pre_gate * (1.0 - sig))
    return d_gate, d_hidden * activated, gate * hidden, tail


def store_halves(values, refs):
    for value, ref in zip(values, refs):
        half = value.shape[0] // 2
        ref[0] = value[:half].astype(bf16)
        ref[1] = value[half:].astype(bf16)


def act_kernel(top_count, where_ref, *refs):
    store_halves(hidden_gradients(top_count, scalar(where_ref, 0).astype(f32), *refs[:5]), refs[6:])


def back_rows(d_part, pipe_size, where_ref, grads, w_gate, w_up, out_ref):
    left = [jnp.concatenate([g[i].astype(f32) for g in grads], 0) for i in (0, 1, 3)]
    back = jnp.dot(left[0].astype(bf16), w_gate[...], preferred_element_type=f32)
    back = back + jnp.dot(left[1].astype(bf16), w_up[...], preferred_element_type=f32)
    count = back.shape[0] // 4
    members = out_ref.shape[1] // pipe_size
    used = count // members // pipe_size
    for h in range(2):
        for member in range(members):
            for p in range(pipe_size):
                starts = [(2 * g + h) * count + (member * pipe_size + p) * used for g in range(GROUPS)]
                at = member * pipe_size + (p ^ scalar(where_ref, 1) if pipe_size == 2 else p)
                for columns, values in ((slice(0, d_part), back), (slice(d_part, None), left[2])):
                    block = jnp.concatenate([values[start : start + used] for start in starts], 0)
                    out_ref[h, at, :, columns] = block.astype(bf16)


def last_act_kernel(d_part, top_count, pipe_size, where_ref, *refs):
    raw, outs = refs[:5], refs[-5:]
    others = [refs[5 + 4 * i : 9 + 4 * i] for i in range(PIECES - 1)]
    w_gate, w_up = refs[4 * PIECES + 1 : 4 * PIECES + 3]
    last = hidden_gradients(top_count, scalar(where_ref, 0).astype(f32), *raw)
    store_halves(last, outs[:4])
    half = last[0].shape[0] // 2
    grads = [[ref[1] for ref in other] for other in others] + [[value[half:] for value in last]]
    back_rows(d_part, pipe_size, where_ref, grads, w_gate, w_up, outs[4])


def own_back_kernel(d_part, pipe_size, where_ref, *refs):
    grads = [[ref[0] for ref in refs[4 * i : 4 * i + 4]] for i in range(PIECES)]
    back_rows(d_part, pipe_size, where_ref, grads, *refs[4 * PIECES : 4 * PIECES + 2], refs[-1])


def fold_kernel(a_ref, b_ref, *out_refs):
    for i, ref in enumerate(out_refs):
        here = i // a_ref.shape[1], i % a_ref.shape[1], slice(None), slice(0, ref.shape[1])
        ref[...] = (a_ref[here].astype(f32) + b_ref[here].astype(f32)).astype(bf16)


def pack_slots(used, columns, tail):
    main = columns.shape[1] // 4 * 3
    per_row = used // (ROWS - used)
    spare = [
        jnp.concatenate([columns[r * per_row + j : r * per_row + j + 1, main:] for j in range(per_row)], 1)
        for r in range(ROWS - used)
    ]
    rows = jnp.concatenate([columns[:, :main]] + spare, 0)
    tail = jnp.concatenate([tail, jnp.zeros((ROWS - used, LANES), f32)], 0)
    return jnp.concatenate([rows, tail], 1)


def fold_pairs_kernel(used, d_part, a_ref, b_ref, c_ref, d_ref, *out_refs):
    here = a_ref[...].astype(f32) + d_ref[...].astype(f32)
    there = b_ref[...].astype(f32) + c_ref[...].astype(f32)
    for k, ref in enumerate(out_refs):
        at = slice(k * used, (k + 1) * used)
        columns = jnp.concatenate([here[at, :d_part], there[at, :d_part]], 1)
        ref[...] = pack_slots(used, columns, here[at, d_part:]).astype(bf16)


def owner_kernel(d_part, packed, where_ref, place_ref, *refs):
    piece_refs, tok_ref, grad_ref = refs[:EXPERTS], refs[EXPERTS], refs[EXPERTS + 1]
    piece_refs = [piece_refs[RETURN_ORDER.index(k)] for k in range(EXPERTS)]
    micro_count, tok_count, d_model = tok_ref.shape
    top_count = grad_ref.shape[1]
    mine = place_ref[scalar(where_ref, 1)]
    places = mine[:, :LANES].astype(bf16)
    place = places[:, :SQUARE]
    ids = mine[:, LANES:]
    rows = jnp.concatenate([ref[...].astype(f32) for ref in piece_refs], 0).astype(bf16)
    wide = rows.shape[1] - LANES
    out = jnp.dot(place, rows[:, :wide], preferred_element_type=f32)
    if packed:
        rest, quarter = 0.0, d_model - wide
        for j in range(wide // quarter):
            spare = places[:, (1 + j) * SQUARE : (2 + j) * SQUARE]
            columns = rows[:, j * quarter : (j + 1) * quarter]
            rest = rest + jnp.dot(spare, columns, preferred_element_type=f32)
        out = jnp.concatenate([out, rest], 1)
        first = scalar(where_ref, 1) == 0
        here, there = out[:, :d_part], out[:, d_part:]
        out = jnp.concatenate([jnp.where(first, here, there), jnp.where(first, there, here)], 1)
    for m in range(micro_count):
        tok_ref[m] = out[m * tok_count : (m + 1) * tok_count].astype(bf16)

    expert_of = ((lax.broadcasted_iota(i32, place.shape, 1) // ROWS) ^ scalar(where_ref, 0)).astype(f32)
    diagonal = lax.broadcasted_iota(i32, (tok_count, tok_count), 0) == lax.broadcasted_iota(
        i32, (tok_count, tok_count), 1
    )
    for k in range(top_count):
        picked = jnp.where(expert_of == ids[:, k : k + 1], mine[:, :SQUARE], 0.0).astype(bf16)
        grad = jnp.dot(picked, rows[:, wide:], preferred_element_type=f32)
        grad = grad[:, 0:1] + grad[:, 1:2]
        for m in range(micro_count):
            part = jnp.broadcast_to(grad[m * tok_count : (m + 1) * tok_count], (tok_count, tok_count))
            grad_ref[m, k : k + 1, :] = jnp.sum(jnp.where(diagonal, part, 0.0), axis=0, keepdims=True)


def flip_kernel(*refs):
    refs[-1][...] = jnp.concatenate([ref[...] for ref in refs[:-1]], 0).T


def flip_weight_kernel(weight_ref, after, out_ref):
    del after
    out_ref[...] = weight_ref[...].T


def weight_kernel(scale, block, tok_ref, cot_ref, *refs):
    pieces, (out_refs, held, sems) = refs[: 3 * PIECES], (refs[-5:-2], refs[-2], refs[-1])
    rights = []
    for w in range(3):
        halves = [ref[h].astype(f32) for ref in pieces[w::3] for h in range(2)]
        rights.append(jnp.concatenate(halves, 0).astype(bf16))
    copies = []
    for i in range(tok_ref.shape[0] // block):
        here = slice(i * block, (i + 1) * block)
        for w, left in enumerate((tok_ref, tok_ref, cot_ref)):
            rows = jnp.dot(left[here], rights[w], preferred_element_type=f32)
            held[w, here] = (rows * scale).astype(bf16)
            copies.append(pltpu.make_async_copy(held.at[w, here], out_refs[w].at[here], sems.at[w, i]))
            copies[-1].start()
    for copy in copies:
        copy.wait()


def tie_kernel(*refs):
    del refs


def call(kernel, out_shape, operands, name, mib=8, flops=0, moved=0, **more):
    specs = {"v": pl.BlockSpec(memory_space=pltpu.VMEM)}
    specs["a"] = pl.BlockSpec(memory_space=pl.ANY)
    more.setdefault("in_specs", [specs[c] for c in operands])
    more.setdefault("out_specs", jax.tree.map(lambda _: specs["v"], out_shape))
    return pl.pallas_call(
        kernel,
        out_shape=out_shape,
        compiler_params=pltpu.CompilerParams(vmem_limit_bytes=mib << 20),
        cost_estimate=pl.CostEstimate(flops=flops, bytes_accessed=moved, transcendentals=0),
        name=name,
        **more,
    )


def tie(values, after, **cost):
    return call(
        tie_kernel,
        [shape(v.shape, v.dtype) for v in values],
        "a" * (len(values) + 1),
        "tie",
        out_specs=[pl.BlockSpec(memory_space=pl.ANY)] * len(values),
        input_output_aliases={i: i for i in range(len(values))},
        **cost,
    )(*values, after)


def on_device(tokens, cotangent, expert_ids, gate_values, w_gate, w_up, w_down_t):
    micro_count, tok_count, d_model = tokens.shape
    top_count = expert_ids.shape[2]
    pipe_size = lax.axis_size("pipe")
    expert_size = lax.axis_size("expert")
    group_size = expert_size // EXPERTS
    bits = [1 << i for i in reversed(range(group_size.bit_length() - 1))]
    d_part, f_part = w_gate.shape
    width = -(-d_part // LANES) * LANES + LANES
    own_rows = micro_count * tok_count
    slots_here = micro_count * CAP
    slot_count = pipe_size * slots_here
    pipe = lax.axis_index("pipe")
    lanes = lax.broadcasted_iota(i32, (ROWS, LANES), 1)
    where = jnp.where(lanes == 0, (lax.axis_index("expert") // group_size).astype(i32), pipe.astype(i32))

    inputs = (tokens, cotangent, jnp.swapaxes(expert_ids, 1, 2), jnp.swapaxes(gate_values, 1, 2))
    blocks = call(
        functools.partial(prep_kernel, d_part),
        [shape((2 * own_rows, width), bf16) for _ in range(pipe_size)],
        "aaaa",
        "prep",
        grid=(1,),
        in_specs=[pl.BlockSpec(x.shape, lambda i: (0, 0, 0)) for x in inputs],
    )(*[pltpu.with_memory_space_constraint(x, pltpu.HBM) for x in inputs])
    if pipe_size == 2:
        first = pipe == 0
        kept, sent = jnp.where(first, blocks[0], blocks[1]), jnp.where(first, blocks[1], blocks[0])
        blocks = [kept, swap(sent, "pipe", 1)]
    else:
        got = lax.all_to_all(jnp.stack(blocks), "pipe", split_axis=0, concat_axis=0, tiled=True)
        blocks = [got[p] for p in range(pipe_size)]
    *slots, place = call(
        functools.partial(pack_kernel, tok_count, top_count, pipe_size),
        tuple(shape((2 * slot_count, width), bf16) for _ in range(EXPERTS))
        + (shape((pipe_size, own_rows, 2 * LANES), f32),),
        "v" + "v" * pipe_size,
        "pack",
    )(where, *blocks)

    gathered = [slots[0]] + [swap(slots[k], "expert", k * group_size) for k in range(1, EXPERTS)]
    def join(g, *after, **cost):
        return call(
            functools.partial(join_kernel, pipe_size),
            shape((2, PER_GROUP * slot_count, width), bf16),
            "v" * PER_GROUP + "a" * len(after),
            "join",
            **cost,
        )(*gathered[g * PER_GROUP : (g + 1) * PER_GROUP], *after)

    def spread(rows):
        for bit in bits[1:]:
            rows = jnp.concatenate([rows, swap(rows, "expert", bit)], 1)
        return rows

    def project(rows):
        tok_rows, cot_rows = rows[0, :, :d_part], rows[1, :, :d_part]
        own = []
        for left, weight in ((tok_rows, w_gate), (tok_rows, w_up), (cot_rows, w_down_t)):
            own.append(jnp.dot(left, weight, preferred_element_type=f32))
        return own

    def exchange(rows, own):
        bit = pipe_size // 2
        while bit > 1:
            got = swap(jnp.stack([part.astype(bf16) for part in own]), "pipe", bit)
            own = [part + got[i].astype(f32) for i, part in enumerate(own)]
            bit //= 2
        got = swap(jnp.stack([part.astype(bf16) for part in own]), "pipe", 1)
        return [rows[0, :, width - LANES :], *own, got]

    first = join(0)
    there = swap(first, "expert", bits[0])
    first = spread(first)
    filler = tie([jnp.zeros((8, LANES), f32) + pipe.astype(f32)], place, **FILL_A)[0]
    first = tie([first], filler)[0]
    first_own = project(first)
    first_sent = jnp.stack([part.astype(bf16) for part in first_own])
    later = join(1, *first_own, first_sent, **JOIN_COST)
    later_there = swap(later, "expert", bits[0])
    here = spread(later)
    here_own = project(here)
    there = spread(tie([there], here_own[2])[0])
    there_own = project(there)
    last = spread(tie([later_there], there_own[2])[0])
    pieces, owns = [first, there, here, last], [first_own, there_own, here_own, project(last)]
    exchanged = [exchange(rows, own) for rows, own in zip(pieces, owns)]
    total = sum(piece[0].shape[0] for piece in exchanged)

    flipped = [
        call(flip_kernel, shape((d_part, total), bf16), "v" * len(pieces), "flip", mib=24)(
            *[rows[a, :, :d_part] for rows in pieces]
        )
        for a in range(2)
    ]

    flipped_weights = [
        call(flip_weight_kernel, shape((f_part, d_part), bf16), "va", "flip_weight", mib=24)(w, exchanged[-1][3])
        for w in (w_gate, w_up)
    ]

    out_width = d_part + LANES
    padded = EXPERTS * slots_here
    half_shape = shape((2, group_size // 4 * pipe_size, padded, out_width), bf16)
    moved = total * (f_part * 24 + d_part * 8) + 4 * d_part * f_part
    mib = min(52, 8 + 2 * moved // (1 << 20))

    def grad_shapes(piece):
        rows = piece[0].shape[0] // 2
        return [shape((2, rows, f_part), bf16)] * 3 + [shape((2, rows, LANES), bf16)]

    grads = [
        call(functools.partial(act_kernel, top_count), grad_shapes(piece), "vvvvvva", "act", mib=mib)(
            where, *piece, exchanged[-1][3]
        )
        for piece in exchanged[:-1]
    ]
    *last_grad, high = call(
        functools.partial(last_act_kernel, d_part, top_count, pipe_size),
        grad_shapes(exchanged[-1]) + [half_shape],
        "v" + "v" * (4 * PIECES + 3) + "a" * len(flipped),
        "last_act",
        mib=mib,
    )(where, *exchanged[-1], *[x for grad in grads for x in grad], *flipped_weights, *flipped)
    grads.append(last_grad)
    low = call(
        functools.partial(own_back_kernel, d_part, pipe_size),
        half_shape,
        "v" + "v" * (4 * PIECES + 2) + "a",
        "own_back",
        mib=mib,
    )(where, *[x for grad in grads for x in grad], *flipped_weights, high)
    packed = pipe_size == 2 and group_size == 4
    if packed:
        parts = call(fold_kernel, [shape((padded, w), bf16) for w in (out_width, d_part) * 2], "vv", "fold")(
            low, swap(high, "expert", bits[1])
        )
        after = parts[0]
        got_both = swap_both(parts[3], bits[0])
        got_member = swap(parts[2], "expert", bits[0])
        got_pipe = swap(parts[1], "pipe", 1)
        contributions = call(
            functools.partial(fold_pairs_kernel, slots_here, d_part),
            [shape((ROWS, d_model // 4 * 3 + LANES), bf16) for _ in range(EXPERTS)],
            "vvvv",
            "fold_pairs",
        )(parts[0], got_both, got_pipe, got_member)
    else:
        for bit in reversed(bits[1:]):
            sums = (low.astype(f32) + swap(high, "expert", bit).astype(f32)).astype(bf16)
            low, high = jnp.split(sums, 2, 1) if bit != bits[1] else (sums[0], sums[1])
        sums = (low.astype(f32) + swap(high, "expert", bits[0]).astype(f32)).astype(bf16)
        after = sums
        if pipe_size == 2:
            got = swap(sums[1], "pipe", 1)
            sums = jnp.where(pipe == 0, jnp.stack([sums[0], got]), jnp.stack([got, sums[0]]))
        else:
            sums = lax.all_to_all(sums, "pipe", split_axis=0, concat_axis=0, tiled=True)
        wide = jnp.swapaxes(sums[:, :, :d_part], 0, 1).reshape(padded, d_model)
        wide = jnp.concatenate([wide, sums[0, :, d_part:]], 1)
        contributions = [
            jnp.pad(wide[k * slots_here : (k + 1) * slots_here], ((0, ROWS - slots_here), (0, 0)))
            for k in range(EXPERTS)
        ]
    contributions = [swap(x, "expert", k * group_size) if k else x for k, x in enumerate(contributions)]

    tokens_total = own_rows * pipe_size * expert_size
    scale = 1.0 / math.sqrt(tokens_total * top_count / EXPERTS)
    block = 256 if d_part % 256 == 0 else d_part
    dw_gate, dw_up, dw_down_t = call(
        functools.partial(weight_kernel, scale, block),
        [shape((d_part, f_part), bf16)] * 3,
        "vv" + "v" * (3 * PIECES) + "a",
        "weight_grads",
        mib=min(52, 12 + (d_part * (total * 4 + f_part * 8) >> 20)),
        out_specs=[pl.BlockSpec(memory_space=pl.ANY)] * 3,
        scratch_shapes=[
            pltpu.VMEM((3, d_part, f_part), bf16),
            pltpu.SemaphoreType.DMA((3, d_part // block)),
        ],
    )(*flipped, *[x for grad in grads for x in grad[:3]], after)

    d_tokens, gate_grads = call(
        functools.partial(owner_kernel, d_part, packed),
        (shape(tokens.shape, bf16), shape((micro_count, top_count, tok_count), f32)),
        "vv" + "v" * EXPERTS,
        "owner",
    )(where, place, *[contributions[k] for k in RETURN_ORDER])
    return (d_tokens, jnp.swapaxes(gate_grads, 1, 2), dw_gate, dw_up, dw_down_t)


def solution(mesh):
    rows = P(None, ("pipe", "expert"), None)
    weights = P("pipe", "expert")
    return jax.shard_map(
        on_device,
        mesh=mesh,
        in_specs=(rows, rows, rows, rows, weights, weights, weights),
        out_specs=(rows, rows, weights, weights, weights),
        check_vma=False,
    )
```

```python
import functools
import math

import jax
import jax.numpy as jnp
from jax import lax
from jax.experimental import pallas as pl
from jax.experimental.pallas import tpu as pltpu
from jax.sharding import PartitionSpec as P

EXPERTS = 4
CAP = 3
GROUPS = 2
PER_GROUP = EXPERTS // GROUPS
LANES = 128
ROWS = 8
PIECES = 4
SQUARE = EXPERTS * ROWS
RETURN_ORDER = (0, 3, 1, 2)
JOIN_COST = dict(flops=4000000000, moved=12000000)
FILL_A = dict(flops=8000000000, moved=24000000)
FILL_B = dict(flops=8_000_000_000, moved=24_000_000)
f32, bf16, i32 = jnp.float32, jnp.bfloat16, jnp.int32
ROWS_BY_ROWS = (((0,), (0,)), ((), ()))
shape = jax.ShapeDtypeStruct


def swap(x, axis, bit):
    return lax.ppermute(x, axis, [(i, i ^ bit) for i in range(lax.axis_size(axis))])


def swap_both(x, bit):
    count = lax.axis_size("expert")
    pairs = [(p * count + e, (p ^ 1) * count + (e ^ bit)) for p in range(2) for e in range(count)]
    return lax.ppermute(x, ("pipe", "expert"), pairs)


def scalar(ref, lane):
    return ref[...][0, lane]


def prep_kernel(d_part, tok_ref, cot_ref, ids_ref, gate_ref, *out_refs):
    micro_count, tok_count = tok_ref.shape[:2]
    top_count = ids_ref.shape[1]
    seg = out_refs[0].shape[-1] - LANES

    def flat(ref):
        return jnp.concatenate([ref[m].astype(f32) for m in range(micro_count)], 0)

    lane = lax.broadcasted_iota(i32, (tok_count, LANES), 1)
    diagonal = lax.broadcasted_iota(i32, (tok_count, tok_count), 0) == lax.broadcasted_iota(
        i32, (tok_count, tok_count), 1
    )
    blocks = []
    for m in range(micro_count):
        block = jnp.zeros((tok_count, LANES), f32)
        for at, ref in enumerate((ids_ref, gate_ref)):
            values = ref[m].astype(f32)
            for k in range(top_count):
                row = jnp.broadcast_to(values[k : k + 1], (tok_count, tok_count))
                column = jnp.sum(jnp.where(diagonal, row, 0.0), axis=1, keepdims=True)
                block = jnp.where(lane == at * top_count + k, column, block)
        blocks.append(block)
    extras = jnp.concatenate(blocks + blocks, 0).astype(bf16)
    both = jnp.concatenate([flat(tok_ref), flat(cot_ref)], 0).astype(bf16)
    for p, ref in enumerate(out_refs):
        ref[:, :d_part] = both[:, p * d_part : (p + 1) * d_part]
        if seg > d_part:
            ref[:, d_part:seg] = jnp.zeros((both.shape[0], seg - d_part), bf16)
        ref[:, seg:] = extras


def pack_kernel(tok_count, top_count, pipe_size, where_ref, *refs):
    blocks, slot_refs, place_ref = [ref[...] for ref in refs[:pipe_size]], refs[pipe_size:-1], refs[-1]
    both_rows, width = blocks[0].shape
    own_rows = both_rows // 2
    total = pipe_size * both_rows
    slot_count = slot_refs[0].shape[0] // 2
    me = scalar(where_ref, 0)
    if pipe_size == 2:
        first = scalar(where_ref, 1) == 0
        blocks = [jnp.where(first, blocks[0], blocks[1]), jnp.where(first, blocks[1], blocks[0])]
    rows = jnp.concatenate(blocks, 0)
    extras = rows[:, width - LANES :].astype(f32)
    at = (lax.broadcasted_iota(i32, (total, LANES), 1) ^ me).astype(f32)
    routed = jnp.zeros((total, LANES), f32)
    for k in range(top_count):
        routed = jnp.where(extras[:, k : k + 1] == at, 1.0, routed)
    at_row = lax.broadcasted_iota(i32, (total, LANES), 0) % tok_count
    position = jnp.zeros((total, LANES), f32)
    for d in range(1, tok_count):
        position = position + jnp.where(at_row >= d, pltpu.roll(routed, d, 0), 0.0)
    index = lax.broadcasted_iota(i32, (total, 1), 0)
    within = index % both_rows
    block = within % own_rows // tok_count
    device = index // both_rows
    base = within // own_rows * slot_count + (device * (own_rows // tok_count) + block) * CAP
    lane = lax.broadcasted_iota(i32, (total, EXPERTS * 2 * slot_count), 1).astype(f32)
    chosen = jnp.zeros(lane.shape, f32)
    small_lane = lax.broadcasted_iota(i32, (total, LANES), 1)
    used = own_rows // tok_count * CAP
    per_row = used // (ROWS - used)
    places = jnp.zeros((total, LANES), f32)
    for k in range(EXPERTS):
        here = routed[:, k : k + 1] > 0.0
        target = (k * 2 * slot_count + base).astype(f32) + position[:, k : k + 1]
        chosen = chosen + jnp.where((lane == target) & here, 1.0, 0.0)
        local = block * CAP + position[:, k : k + 1].astype(i32)
        spare = SQUARE * (1 + local % per_row) + k * ROWS + used + local // per_row
        at_slot = (small_lane == k * ROWS + local) | (small_lane == spare)
        places = places + jnp.where(at_slot & here, 1.0, 0.0)
    slots = lax.dot_general(chosen.astype(bf16), rows, ROWS_BY_ROWS, preferred_element_type=f32)
    for k in range(EXPERTS):
        slot_refs[k][...] = slots[2 * k * slot_count : 2 * (k + 1) * slot_count].astype(bf16)
    for p in range(pipe_size):
        start = p * both_rows
        place_ref[p, :, :LANES] = places[start : start + own_rows]
        place_ref[p, :, LANES:] = extras[start : start + own_rows]


def join_kernel(pipe_size, *refs):
    blocks, out_ref = [ref[...].astype(f32) for ref in refs[:PER_GROUP]], refs[-1]
    rows = blocks[0].shape[0] // 2 // pipe_size
    for a in range(2):
        starts = [(a * pipe_size + p) * rows for p in range(pipe_size)]
        out_ref[a] = jnp.concatenate([b[s : s + rows] for s in starts for b in blocks], 0).astype(bf16)


def hidden_gradients(top_count, me, info, own_g, own_u, own_b, got):
    extras = info[...].astype(f32)
    gate = jnp.zeros((extras.shape[0], 1), f32)
    for k in range(top_count):
        gate = gate + jnp.where(extras[:, k : k + 1] == me, extras[:, top_count + k : top_count + k + 1], 0.0)
    pre_gate = own_g[...] + got[0].astype(f32)
    pre_up = own_u[...] + got[1].astype(f32)
    back_proj = own_b[...] + got[2].astype(f32)
    sig = jax.nn.sigmoid(pre_gate)
    activated = pre_gate * sig
    hidden = activated * pre_up
    share = jnp.sum(back_proj * hidden, axis=1, keepdims=True)
    high = share.astype(bf16).astype(f32)
    lane = lax.broadcasted_iota(i32, (share.shape[0], LANES), 1)
    tail = jnp.where(lane == 0, high, jnp.where(lane == 1, share - high, 0.0))
    d_hidden = gate * back_proj
    d_gate = d_hidden * pre_up * sig * (1.0 + pre_gate * (1.0 - sig))
    return d_gate, d_hidden * activated, gate * hidden, tail


def store_halves(values, refs):
    for value, ref in zip(values, refs):
        half = value.shape[0] // 2
        ref[0] = value[:half].astype(bf16)
        ref[1] = value[half:].astype(bf16)


def act_kernel(top_count, where_ref, *refs):
    store_halves(hidden_gradients(top_count, scalar(where_ref, 0).astype(f32), *refs[:5]), refs[6:])


def back_rows(d_part, pipe_size, where_ref, grads, w_gate, w_up, out_ref):
    left = [jnp.concatenate([g[i].astype(f32) for g in grads], 0) for i in (0, 1, 3)]
    back = jnp.dot(left[0].astype(bf16), w_gate[...], preferred_element_type=f32)
    back = back + jnp.dot(left[1].astype(bf16), w_up[...], preferred_element_type=f32)
    count = back.shape[0] // 4
    members = out_ref.shape[1] // pipe_size
    used = count // members // pipe_size
    for h in range(2):
        for member in range(members):
            for p in range(pipe_size):
                starts = [(2 * g + h) * count + (member * pipe_size + p) * used for g in range(GROUPS)]
                at = member * pipe_size + (p ^ scalar(where_ref, 1) if pipe_size == 2 else p)
                for columns, values in ((slice(0, d_part), back), (slice(d_part, None), left[2])):
                    block = jnp.concatenate([values[start : start + used] for start in starts], 0)
                    out_ref[h, at, :, columns] = block.astype(bf16)


def last_act_kernel(d_part, top_count, pipe_size, where_ref, *refs):
    raw, outs = refs[:5], refs[-5:]
    others = [refs[5 + 4 * i : 9 + 4 * i] for i in range(PIECES - 1)]
    w_gate, w_up = refs[4 * PIECES + 1 : 4 * PIECES + 3]
    last = hidden_gradients(top_count, scalar(where_ref, 0).astype(f32), *raw)
    store_halves(last, outs[:4])
    half = last[0].shape[0] // 2
    grads = [[ref[1] for ref in other] for other in others] + [[value[half:] for value in last]]
    back_rows(d_part, pipe_size, where_ref, grads, w_gate, w_up, outs[4])


def own_back_kernel(d_part, pipe_size, where_ref, *refs):
    grads = [[ref[0] for ref in refs[4 * i : 4 * i + 4]] for i in range(PIECES)]
    back_rows(d_part, pipe_size, where_ref, grads, *refs[4 * PIECES : 4 * PIECES + 2], refs[-1])


def fold_kernel(a_ref, b_ref, *out_refs):
    for i, ref in enumerate(out_refs):
        here = i // a_ref.shape[1], i % a_ref.shape[1], slice(None), slice(0, ref.shape[1])
        ref[...] = (a_ref[here].astype(f32) + b_ref[here].astype(f32)).astype(bf16)


def pack_slots(used, columns, tail):
    main = columns.shape[1] // 4 * 3
    per_row = used // (ROWS - used)
    spare = [
        jnp.concatenate([columns[r * per_row + j : r * per_row + j + 1, main:] for j in range(per_row)], 1)
        for r in range(ROWS - used)
    ]
    rows = jnp.concatenate([columns[:, :main]] + spare, 0)
    tail = jnp.concatenate([tail, jnp.zeros((ROWS - used, LANES), f32)], 0)
    return jnp.concatenate([rows, tail], 1)


def fold_pairs_kernel(used, d_part, a_ref, b_ref, c_ref, d_ref, *out_refs):
    here = a_ref[...].astype(f32) + d_ref[...].astype(f32)
    there = b_ref[...].astype(f32) + c_ref[...].astype(f32)
    for k, ref in enumerate(out_refs):
        at = slice(k * used, (k + 1) * used)
        columns = jnp.concatenate([here[at, :d_part], there[at, :d_part]], 1)
        ref[...] = pack_slots(used, columns, here[at, d_part:]).astype(bf16)


def owner_kernel(d_part, packed, where_ref, place_ref, *refs):
    piece_refs, tok_ref, grad_ref = refs[:EXPERTS], refs[EXPERTS], refs[EXPERTS + 1]
    piece_refs = [piece_refs[RETURN_ORDER.index(k)] for k in range(EXPERTS)]
    micro_count, tok_count, d_model = tok_ref.shape
    top_count = grad_ref.shape[1]
    mine = place_ref[scalar(where_ref, 1)]
    places = mine[:, :LANES].astype(bf16)
    place = places[:, :SQUARE]
    ids = mine[:, LANES:]
    rows = jnp.concatenate([ref[...].astype(f32) for ref in piece_refs], 0).astype(bf16)
    wide = rows.shape[1] - LANES
    out = jnp.dot(place, rows[:, :wide], preferred_element_type=f32)
    if packed:
        rest, quarter = 0.0, d_model - wide
        for j in range(wide // quarter):
            spare = places[:, (1 + j) * SQUARE : (2 + j) * SQUARE]
            columns = rows[:, j * quarter : (j + 1) * quarter]
            rest = rest + jnp.dot(spare, columns, preferred_element_type=f32)
        out = jnp.concatenate([out, rest], 1)
        first = scalar(where_ref, 1) == 0
        here, there = out[:, :d_part], out[:, d_part:]
        out = jnp.concatenate([jnp.where(first, here, there), jnp.where(first, there, here)], 1)
    for m in range(micro_count):
        tok_ref[m] = out[m * tok_count : (m + 1) * tok_count].astype(bf16)

    expert_of = ((lax.broadcasted_iota(i32, place.shape, 1) // ROWS) ^ scalar(where_ref, 0)).astype(f32)
    diagonal = lax.broadcasted_iota(i32, (tok_count, tok_count), 0) == lax.broadcasted_iota(
        i32, (tok_count, tok_count), 1
    )
    for k in range(top_count):
        picked = jnp.where(expert_of == ids[:, k : k + 1], mine[:, :SQUARE], 0.0).astype(bf16)
        grad = jnp.dot(picked, rows[:, wide:], preferred_element_type=f32)
        grad = grad[:, 0:1] + grad[:, 1:2]
        for m in range(micro_count):
            part = jnp.broadcast_to(grad[m * tok_count : (m + 1) * tok_count], (tok_count, tok_count))
            grad_ref[m, k : k + 1, :] = jnp.sum(jnp.where(diagonal, part, 0.0), axis=0, keepdims=True)


def flip_kernel(*refs):
    refs[-1][...] = jnp.concatenate([ref[...] for ref in refs[:-1]], 0).T


def flip_weight_kernel(weight_ref, after, out_ref):
    del after
    out_ref[...] = weight_ref[...].T


def weight_kernel(scale, block, tok_ref, cot_ref, *refs):
    pieces, (out_refs, held, sems) = refs[: 3 * PIECES], (refs[-5:-2], refs[-2], refs[-1])
    rights = []
    for w in range(3):
        halves = [ref[h].astype(f32) for ref in pieces[w::3] for h in range(2)]
        rights.append(jnp.concatenate(halves, 0).astype(bf16))
    copies = []
    for i in range(tok_ref.shape[0] // block):
        here = slice(i * block, (i + 1) * block)
        for w, left in enumerate((tok_ref, tok_ref, cot_ref)):
            rows = jnp.dot(left[here], rights[w], preferred_element_type=f32)
            held[w, here] = (rows * scale).astype(bf16)
            copies.append(pltpu.make_async_copy(held.at[w, here], out_refs[w].at[here], sems.at[w, i]))
            copies[-1].start()
    for copy in copies:
        copy.wait()


def tie_kernel(*refs):
    del refs


def call(kernel, out_shape, operands, name, mib=8, flops=0, moved=0, **more):
    specs = {"v": pl.BlockSpec(memory_space=pltpu.VMEM)}
    specs["a"] = pl.BlockSpec(memory_space=pl.ANY)
    more.setdefault("in_specs", [specs[c] for c in operands])
    more.setdefault("out_specs", jax.tree.map(lambda _: specs["v"], out_shape))
    return pl.pallas_call(
        kernel,
        out_shape=out_shape,
        compiler_params=pltpu.CompilerParams(vmem_limit_bytes=mib << 20),
        cost_estimate=pl.CostEstimate(flops=flops, bytes_accessed=moved, transcendentals=0),
        name=name,
        **more,
    )


def tie(values, after, **cost):
    return call(
        tie_kernel,
        [shape(v.shape, v.dtype) for v in values],
        "a" * (len(values) + 1),
        "tie",
        out_specs=[pl.BlockSpec(memory_space=pl.ANY)] * len(values),
        input_output_aliases={i: i for i in range(len(values))},
        **cost,
    )(*values, after)


def on_device(tokens, cotangent, expert_ids, gate_values, w_gate, w_up, w_down_t):
    micro_count, tok_count, d_model = tokens.shape
    top_count = expert_ids.shape[2]
    pipe_size = lax.axis_size("pipe")
    expert_size = lax.axis_size("expert")
    group_size = expert_size // EXPERTS
    bits = [1 << i for i in reversed(range(group_size.bit_length() - 1))]
    d_part, f_part = w_gate.shape
    width = -(-d_part // LANES) * LANES + LANES
    own_rows = micro_count * tok_count
    slots_here = micro_count * CAP
    slot_count = pipe_size * slots_here
    pipe = lax.axis_index("pipe")
    lanes = lax.broadcasted_iota(i32, (ROWS, LANES), 1)
    where = jnp.where(lanes == 0, (lax.axis_index("expert") // group_size).astype(i32), pipe.astype(i32))

    inputs = (tokens, cotangent, jnp.swapaxes(expert_ids, 1, 2), jnp.swapaxes(gate_values, 1, 2))
    blocks = call(
        functools.partial(prep_kernel, d_part),
        [shape((2 * own_rows, width), bf16) for _ in range(pipe_size)],
        "aaaa",
        "prep",
        grid=(1,),
        in_specs=[pl.BlockSpec(x.shape, lambda i: (0, 0, 0)) for x in inputs],
    )(*[pltpu.with_memory_space_constraint(x, pltpu.HBM) for x in inputs])
    if pipe_size == 2:
        first = pipe == 0
        kept, sent = jnp.where(first, blocks[0], blocks[1]), jnp.where(first, blocks[1], blocks[0])
        blocks = [kept, swap(sent, "pipe", 1)]
    else:
        got = lax.all_to_all(jnp.stack(blocks), "pipe", split_axis=0, concat_axis=0, tiled=True)
        blocks = [got[p] for p in range(pipe_size)]
    *slots, place = call(
        functools.partial(pack_kernel, tok_count, top_count, pipe_size),
        tuple(shape((2 * slot_count, width), bf16) for _ in range(EXPERTS))
        + (shape((pipe_size, own_rows, 2 * LANES), f32),),
        "v" + "v" * pipe_size,
        "pack",
    )(where, *blocks)

    gathered = [slots[0]] + [swap(slots[k], "expert", k * group_size) for k in range(1, EXPERTS)]
    def join(g, *after, **cost):
        return call(
            functools.partial(join_kernel, pipe_size),
            shape((2, PER_GROUP * slot_count, width), bf16),
            "v" * PER_GROUP + "a" * len(after),
            "join",
            **cost,
        )(*gathered[g * PER_GROUP : (g + 1) * PER_GROUP], *after)

    def spread(rows):
        for bit in bits[1:]:
            rows = jnp.concatenate([rows, swap(rows, "expert", bit)], 1)
        return rows

    def project(rows):
        tok_rows, cot_rows = rows[0, :, :d_part], rows[1, :, :d_part]
        own = []
        for left, weight in ((tok_rows, w_gate), (tok_rows, w_up), (cot_rows, w_down_t)):
            own.append(jnp.dot(left, weight, preferred_element_type=f32))
        return own

    def exchange(rows, own):
        bit = pipe_size // 2
        while bit > 1:
            got = swap(jnp.stack([part.astype(bf16) for part in own]), "pipe", bit)
            own = [part + got[i].astype(f32) for i, part in enumerate(own)]
            bit //= 2
        got = swap(jnp.stack([part.astype(bf16) for part in own]), "pipe", 1)
        return [rows[0, :, width - LANES :], *own, got]

    first = join(0)
    there = swap(first, "expert", bits[0])
    first = spread(first)
    filler = tie([jnp.zeros((8, LANES), f32) + pipe.astype(f32)], place, **FILL_A)[0]
    first = tie([first], filler)[0]
    first_own = project(first)
    first_sent = jnp.stack([part.astype(bf16) for part in first_own])
    later = join(1, *first_own, first_sent, **JOIN_COST)
    later_there = swap(later, "expert", bits[0])
    here = spread(later)
    here_own = project(here)
    there = spread(tie([there], here_own[2])[0])
    there_own = project(there)
    last = spread(tie([later_there], there_own[2])[0])
    pieces, owns = [first, there, here, last], [first_own, there_own, here_own, project(last)]
    exchanged = [exchange(rows, own) for rows, own in zip(pieces, owns)]
    total = sum(piece[0].shape[0] for piece in exchanged)

    flipped = [
        call(flip_kernel, shape((d_part, total), bf16), "v" * len(pieces), "flip", mib=24)(
            *[rows[a, :, :d_part] for rows in pieces]
        )
        for a in range(2)
    ]

    flipped_weights = [
        call(flip_weight_kernel, shape((f_part, d_part), bf16), "va", "flip_weight", mib=24)(w, exchanged[-1][3])
        for w in (w_gate, w_up)
    ]

    out_width = d_part + LANES
    padded = EXPERTS * slots_here
    half_shape = shape((2, group_size // 4 * pipe_size, padded, out_width), bf16)
    moved = total * (f_part * 24 + d_part * 8) + 4 * d_part * f_part
    mib = min(52, 8 + 2 * moved // (1 << 20))

    def grad_shapes(piece):
        rows = piece[0].shape[0] // 2
        return [shape((2, rows, f_part), bf16)] * 3 + [shape((2, rows, LANES), bf16)]

    grads = [
        call(functools.partial(act_kernel, top_count), grad_shapes(piece), "vvvvvva", "act", mib=mib)(
            where, *piece, exchanged[-1][3]
        )
        for piece in exchanged[:-1]
    ]
    *last_grad, high = call(
        functools.partial(last_act_kernel, d_part, top_count, pipe_size),
        grad_shapes(exchanged[-1]) + [half_shape],
        "v" + "v" * (4 * PIECES + 3) + "a" * len(flipped),
        "last_act",
        mib=mib,
    )(where, *exchanged[-1], *[x for grad in grads for x in grad], *flipped_weights, *flipped)
    grads.append(last_grad)
    low = call(
        functools.partial(own_back_kernel, d_part, pipe_size),
        half_shape,
        "v" + "v" * (4 * PIECES + 2) + "a",
        "own_back",
        mib=mib,
    )(where, *[x for grad in grads for x in grad], *flipped_weights, high)
    packed = pipe_size == 2 and group_size == 4
    if packed:
        parts = call(fold_kernel, [shape((padded, w), bf16) for w in (out_width, d_part) * 2], "vv", "fold")(
            low, swap(high, "expert", bits[1])
        )
        after = parts[0]
        got_both = swap_both(parts[3], bits[0])
        got_member = swap(parts[2], "expert", bits[0])
        got_pipe = swap(parts[1], "pipe", 1)
        contributions = call(
            functools.partial(fold_pairs_kernel, slots_here, d_part),
            [shape((ROWS, d_model // 4 * 3 + LANES), bf16) for _ in range(EXPERTS)],
            "vvvv",
            "fold_pairs",
        )(parts[0], got_both, got_pipe, got_member)
    else:
        for bit in reversed(bits[1:]):
            sums = (low.astype(f32) + swap(high, "expert", bit).astype(f32)).astype(bf16)
            low, high = jnp.split(sums, 2, 1) if bit != bits[1] else (sums[0], sums[1])
        sums = (low.astype(f32) + swap(high, "expert", bits[0]).astype(f32)).astype(bf16)
        after = sums
        if pipe_size == 2:
            got = swap(sums[1], "pipe", 1)
            sums = jnp.where(pipe == 0, jnp.stack([sums[0], got]), jnp.stack([got, sums[0]]))
        else:
            sums = lax.all_to_all(sums, "pipe", split_axis=0, concat_axis=0, tiled=True)
        wide = jnp.swapaxes(sums[:, :, :d_part], 0, 1).reshape(padded, d_model)
        wide = jnp.concatenate([wide, sums[0, :, d_part:]], 1)
        contributions = [
            jnp.pad(wide[k * slots_here : (k + 1) * slots_here], ((0, ROWS - slots_here), (0, 0)))
            for k in range(EXPERTS)
        ]
    contributions = [swap(x, "expert", k * group_size) if k else x for k, x in enumerate(contributions)]

    tokens_total = own_rows * pipe_size * expert_size
    scale = 1.0 / math.sqrt(tokens_total * top_count / EXPERTS)
    block = 256 if d_part % 256 == 0 else d_part
    dw_gate, dw_up, dw_down_t = call(
        functools.partial(weight_kernel, scale, block),
        [shape((d_part, f_part), bf16)] * 3,
        "vv" + "v" * (3 * PIECES) + "a",
        "weight_grads",
        mib=min(52, 12 + (d_part * (total * 4 + f_part * 8) >> 20)),
        out_specs=[pl.BlockSpec(memory_space=pl.ANY)] * 3,
        scratch_shapes=[
            pltpu.VMEM((3, d_part, f_part), bf16),
            pltpu.SemaphoreType.DMA((3, d_part // block)),
        ],
    )(*flipped, *[x for grad in grads for x in grad[:3]], after)

    d_tokens, gate_grads = call(
        functools.partial(owner_kernel, d_part, packed),
        (shape(tokens.shape, bf16), shape((micro_count, top_count, tok_count), f32)),
        "vv" + "v" * EXPERTS,
        "owner",
    )(where, place, *[contributions[k] for k in RETURN_ORDER])
    return (d_tokens, jnp.swapaxes(gate_grads, 1, 2), dw_gate, dw_up, dw_down_t)


def solution(mesh):
    rows = P(None, ("pipe", "expert"), None)
    weights = P("pipe", "expert")
    return jax.shard_map(
        on_device,
        mesh=mesh,
        in_specs=(rows, rows, rows, rows, weights, weights, weights),
        out_specs=(rows, rows, weights, weights, weights),
        check_vma=False,
    )
```
